128 devices in a mesh: tm: 16 (over x, z), col: 8 (over y, core).
Axes of the slice: x: 4, y: 4, z: 4, core: 2. Of those that a mesh axis runs over, the one named last changes fastest.
Arguments:
- diagonal: float32 [16, 1024, 1024], P('tm', 'col'), may hold values from -1 to 8, as said below
- coupling: float32 [16, 1024, 1024], P('tm', 'col'), may hold values from -1 to 0.5
- arrowhead: float32 [16, 1024, 64], P('tm', 'col'), may hold values from -1 to 1
- tip_matrix: float32 [64, 64], replicated, may hold values from -1 to 6, as said below
Outputs:
- factors: float32 [16, 1024, 1024], P('tm', 'col')
- link_blocks: float32 [16, 2, 1024, 1024], P('tm', None, 'col')
- arrow_rows: float32 [16, 1024, 64], P('tm', 'col')
- tip_block: float32 [64, 64], replicated
The draws below stay inside these ranges and needn't reach their ends.
Inputs may be any that keep to these rules, and one draw needn't show every extreme that they name: Each diagonal[t] and tip_matrix is symmetric, and Q is positive definite. `tip_matrix`: symmetric.
All inputs are finite; a program needn't handle non-finite values.
Results may differ from the reference program's by a relative error of at most 0.0001.
Values sent between devices are 32-bit elements; how exact they have to be, the bound alone decides.
A program may use at most 192 MiB of HBM per device.

```python
import jax
import jax.numpy as jnp
from jax import lax

NODES = 1024
TIP = 64
BLOCKS = 16


def rough_noise(key, shape):
    return jax.random.normal(key, shape, jnp.float32)


def draw_diagonal(key, part):
    key = jax.random.fold_in(key, 11)
    first_key, second_key, third_key = jax.random.split(key, 3)
    noise = jnp.clip(rough_noise(first_key, (BLOCKS, NODES, NODES)), -5.0, 5.0)
    symmetric = (noise + jnp.swapaxes(noise, 1, 2)) * (0.15 / NODES ** 0.5)
    scales = jnp.exp(jax.random.uniform(third_key, (BLOCKS, NODES), jnp.float32, -0.35, 0.35))
    length = NODES / 256.0
    places = jnp.arange(NODES, dtype=jnp.float32)
    kernel = jnp.exp(-jnp.abs(places[:, None] - places[None, :]) / length)
    smooth = scales[:, :, None] * scales[:, None, :] * kernel[None]
    middle = jax.random.uniform(second_key, (BLOCKS, NODES), jnp.float32, 4.0, 5.0)
    identity = jnp.eye(NODES, dtype=jnp.float32)
    return symmetric * (1.0 - identity) + smooth + middle[:, :, None] * identity


def draw_coupling(key, part):
    key = jax.random.fold_in(key, 12)
    first_key, second_key = jax.random.split(key)
    noise = jnp.clip(rough_noise(first_key, (BLOCKS, NODES, NODES)), -5.0, 5.0) * (0.35 / NODES ** 0.5)
    strength = jax.random.uniform(second_key, (BLOCKS, NODES), jnp.float32, 0.85, 0.95)
    identity = jnp.eye(NODES, dtype=jnp.float32)
    return noise * (1.0 - identity) - strength[:, :, None] * identity


def draw_arrowhead(key, part):
    key = jax.random.fold_in(key, 13)
    rising = 1.0 + 2.0 * jnp.arange(BLOCKS, dtype=jnp.float32) / (BLOCKS - 1)
    scales = jnp.sqrt(3.0 * rising / (NODES * BLOCKS))
    noise = rough_noise(key, (BLOCKS, NODES, TIP))
    return jnp.clip(noise, -6.0, 6.0) * scales[:, None, None]


def draw_tip_matrix(key, part):
    key = jax.random.fold_in(key, 14)
    first_key, second_key = jax.random.split(key)
    noise = rough_noise(first_key, (TIP, TIP))
    symmetric = (noise + noise.T) * (0.1 / TIP ** 0.5)
    middle = jax.random.uniform(second_key, (TIP,), jnp.float32, 4.0, 5.5)
    identity = jnp.eye(TIP, dtype=jnp.float32)
    return symmetric * (1.0 - identity) + middle[:, None] * identity


def setup_inputs(seed: int = 0) -> dict:
    splits = jax.random.split(jax.random.key(seed), 5)
    diagonal = draw_diagonal(jax.random.fold_in(splits[4], 71), 0)
    coupling = draw_coupling(jax.random.fold_in(splits[4], 71), 0)
    arrowhead = draw_arrowhead(jax.random.fold_in(splits[4], 71), 0)
    tip_matrix = draw_tip_matrix(jax.random.fold_in(splits[4], 71), 0)
    return {"diagonal": diagonal, "coupling": coupling, "arrowhead": arrowhead, "tip_matrix": tip_matrix}


highest = lax.Precision.HIGHEST

def product(left_op, right_op):
    return jnp.dot(left_op.astype(jnp.float32), right_op.astype(jnp.float32), precision=highest, preferred_element_type=jnp.float32)

def eliminate(matrix, link_pair, arrow_whole):
    factor = jnp.linalg.cholesky(matrix)
    solved = jax.scipy.linalg.solve_triangular(factor, link_pair.T, lower=True).T
    tipped = jax.scipy.linalg.solve_triangular(factor, arrow_whole, lower=True).T
    return (factor, solved, tipped)

def reference(diagonal, coupling, arrowhead, tip_matrix):
    zeros_block = jnp.zeros((NODES, NODES), jnp.float32)
    blocks = [diagonal[target] for target in range(BLOCKS)]
    arrow_list = [arrowhead[target] for target in range(BLOCKS)]
    left_links = [zeros_block for target in range(BLOCKS)]
    right_links = [zeros_block for target in range(BLOCKS)]
    records = {}
    reduced = tip_matrix
    for distance in (1, 2):
        current = {}
        for target in range(distance, BLOCKS, 2 * distance):
            if distance == 1:
                prior_link = coupling[target - 1]
                next_link = coupling[target] if target + 1 < BLOCKS else zeros_block
            else:
                prior_link = right_links[target - distance]
                next_link = left_links[target + distance] if target + distance < BLOCKS else zeros_block
            factor, solved, tipped = eliminate(blocks[target], jnp.concatenate([prior_link, next_link], 0), arrow_list[target])
            left_rows = solved[:NODES]
            right_rows = solved[NODES:]
            records[target] = (factor, jnp.stack([left_rows, right_rows]), tipped.T)
            current[target] = (left_rows, right_rows, tipped)
            reduced = reduced - product(tipped, tipped.T)
        for target in range(0, BLOCKS, 2 * distance):
            left_rows, right_rows, tipped = current[target + distance]
            updated = blocks[target] - product(left_rows, left_rows.T)
            new_arrow = arrow_list[target] - product(left_rows, tipped.T)
            right_links[target] = -product(left_rows, right_rows.T)
            if target >= distance:
                prior_left, prior_right, prior_tip = current[target - distance]
                updated = updated - product(prior_right, prior_right.T)
                new_arrow = new_arrow - product(prior_right, prior_tip.T)
                left_links[target] = -product(prior_right, prior_left.T)
            else:
                left_links[target] = zeros_block
            blocks[target] = updated
            arrow_list[target] = new_arrow
    factor_list = []
    pair_list = []
    rows_list = []
    for target in range(BLOCKS):
        if target % 4 == 0:
            factor_list.append(blocks[target])
            pair_list.append(jnp.stack([left_links[target], right_links[target]]))
            rows_list.append(arrow_list[target])
        else:
            factor, paired, arrow_part = records[target]
            factor_list.append(factor)
            pair_list.append(paired)
            rows_list.append(arrow_part)
    return (jnp.stack(factor_list), jnp.stack(pair_list), jnp.stack(rows_list), reduced)
```

```python
import jax
import jax.numpy as jnp
from jax import lax
from jax.experimental import pallas as pl
from jax.experimental.pallas import tpu as pltpu
from jax.sharding import PartitionSpec as P

LANES = 128
PANEL = 16
highest = lax.Precision.HIGHEST


def split_two(value):
    high = value.astype(jnp.bfloat16)
    low = (value - high.astype(jnp.float32)).astype(jnp.bfloat16)
    return high, low


def split_three(value):
    high = value.astype(jnp.bfloat16)
    rest = value - high.astype(jnp.float32)
    middle = rest.astype(jnp.bfloat16)
    low = (rest - middle.astype(jnp.float32)).astype(jnp.bfloat16)
    return high, middle, low


def spread_row(vec, row):
    return jnp.broadcast_to(vec[row : row + 1, :], (8, LANES))


def spread_lane(vec, lane):
    return jnp.take_along_axis(vec, jnp.full(vec.shape, lane, jnp.int32), axis=1)


def factor_tile(work):
    sub = lax.broadcasted_iota(jnp.int32, (8, LANES), 0)
    for panel in range(LANES // PANEL):
        first = panel * PANEL
        left = [work[first : first + 8, :LANES], work[first + 8 : first + 16, :LANES]]
        right = [work[first : first + 8, LANES:], work[first + 8 : first + 16, LANES:]]
        cols = [
            [spread_lane(left[h], first + c) if h >= c // 8 else None for h in range(2)]
            for c in range(PANEL)
        ]
        pivots = [None, None]
        for r in range(PANEL):
            h, q = r // 8, r % 8
            pivot = spread_row(cols[r][h], q)
            pivots[h] = pivot if q == 0 else jnp.where(sub == q, pivot, pivots[h])
            if r == PANEL - 1:
                break
            inverse = 1.0 / pivot
            coef, masked = [None, None], [None, None]
            for g in range(h, 2):
                coef[g] = cols[r][g] * inverse
                masked[g] = jnp.where(sub > q, coef[g], 0.0) if g == h else coef[g]
            for c in range(r + 1, PANEL):
                entry = spread_row(cols[r][c // 8], c % 8)
                for g in range(c // 8, 2):
                    cols[c][g] = cols[c][g] - coef[g] * entry
            left_row, right_row = spread_row(left[h], q), spread_row(right[h], q)
            for g in range(h, 2):
                if g == h and q == 7:
                    continue
                left[g] = left[g] - masked[g] * left_row
                right[g] = right[g] - masked[g] * right_row
        rows = []
        for h in range(2):
            scale = lax.rsqrt(pivots[h])
            rows.append(jnp.concatenate([left[h] * scale, right[h] * scale], 1))
        rows = jnp.concatenate(rows, 0)
        work[first : first + PANEL, :] = rows
        if first + PANEL < LANES:
            a, b, c = split_three(rows)
            lhs = jnp.concatenate([a, a, b, a, b, c], 0)[:, :LANES]
            rhs = jnp.concatenate([a, b, a, c, b, a], 0)
            update = lax.dot_general(
                lhs, rhs, (((0,), (0,)), ((), ())), preferred_element_type=jnp.float32
            )
            n = first + PANEL
            work[n:, :] = work[n:, :] - update[n:, :]


def dot_nt(left, right):
    return lax.dot_general(
        left, right, (((1,), (1,)), ((), ())), preferred_element_type=jnp.float32
    )


def wide_left(value):
    high, low = split_two(value)
    return jnp.concatenate([high, high, low], 1)


def wide_right(value):
    high, low = split_two(value)
    return jnp.concatenate([high, low, high], 1)


def factor_step(k, tiles, work, lhs, rhs):
    count, total, _ = tiles.shape
    nodes = count * LANES
    row_id = lax.broadcasted_iota(jnp.int32, (LANES, LANES), 0)
    col_id = lax.broadcasted_iota(jnp.int32, (LANES, LANES), 1)
    here = pl.ds(pl.multiple_of(k * LANES, LANES), LANES)
    work[:, :LANES] = tiles[k, here, :]
    work[:, LANES:] = jnp.where(row_id == col_id, 1.0, 0.0)
    factor_tile(work)
    inverse = wide_right(work[:, LANES:])
    solved = dot_nt(wide_left(tiles[k]), inverse)
    rows = lax.broadcasted_iota(jnp.int32, (total, LANES), 0)
    solved = jnp.where(rows >= (k + 1) * LANES, solved, 0.0)
    tiles[k] = solved
    tiles[k, here, :] = jnp.where(row_id <= col_id, work[:, :LANES], 0.0).T
    high, low = split_two(solved)
    lhs[...] = jnp.concatenate([high, high, low], 1)
    rhs[...] = jnp.concatenate([high[:nodes], low[:nodes], high[:nodes]], 1)
    for pair in range(count // 2):
        top = 2 * LANES * pair

        @pl.when(2 * pair + 1 > k)
        def _():
            update = dot_nt(lhs[top:, :], rhs[top : top + 2 * LANES, :])
            tiles[2 * pair, top:, :] = tiles[2 * pair, top:, :] - update[:, :LANES]
            tiles[2 * pair + 1, top:, :] = tiles[2 * pair + 1, top:, :] - update[:, LANES:]


def factor_kernel(matrix, links, arrow_t, tiles, work, lhs, rhs):
    count = tiles.shape[0]
    nodes = count * LANES
    for k in range(count):
        lanes = slice(k * LANES, (k + 1) * LANES)
        tiles[k, :nodes, :] = matrix[:, lanes]
        tiles[k, nodes : nodes + 256, :] = links[:, lanes]
        tiles[k, nodes + 256 :, :] = arrow_t[:, lanes]

    def step(k, carry):
        factor_step(k, tiles, work, lhs, rhs)
        return carry

    lax.fori_loop(0, count, step, 0)


def factorize(matrix, links, arrow_t):
    nodes = matrix.shape[0]
    total = nodes + links.shape[0] + arrow_t.shape[0]
    return pl.pallas_call(
        factor_kernel,
        out_shape=jax.ShapeDtypeStruct((nodes // LANES, total, LANES), jnp.float32),
        in_specs=[pl.BlockSpec(memory_space=pltpu.VMEM)] * 3,
        out_specs=pl.BlockSpec(memory_space=pltpu.VMEM),
        scratch_shapes=[
            pltpu.VMEM((LANES, 2 * LANES), jnp.float32),
            pltpu.VMEM((total, 3 * LANES), jnp.bfloat16),
            pltpu.VMEM((nodes, 3 * LANES), jnp.bfloat16),
        ],
        compiler_params=pltpu.CompilerParams(vmem_limit_bytes=48 * 1024 * 1024),
        name="factor_block",
    )(matrix, links, arrow_t)


def from_behind(array, axis, by):
    peers = lax.axis_size(axis)
    pairs = [(i, i + by) for i in range(peers) if 0 <= i + by < peers]
    return lax.ppermute(array, axis, pairs)


def outer_rows(left_op, right_op):
    return lax.dot_general(
        left_op,
        right_op,
        (((1,), (1,)), ((), ())),
        precision=highest,
        preferred_element_type=jnp.float32,
    )


def fetch_link(values, offset):
    return from_behind(values, "tm", offset)


def send_update(values, offset):
    return from_behind((values[0], values[1], values[2]), "tm", offset)


def local_products(solved):
    return outer_rows(solved, lax.all_gather(solved, "col", axis=0, tiled=True))


def split_columns(combined, col_count, row_count):
    shaped = combined.reshape(combined.shape[0], col_count, 2, row_count)
    left_part = shaped[:, :, 0, :].reshape(combined.shape[0], col_count * row_count)
    right_part = shaped[:, :, 1, :].reshape(combined.shape[0], col_count * row_count)
    return (left_part, right_part)


def body(diagonal, coupling, arrowhead, tip_matrix):
    col_count = lax.axis_size("col")
    tm_count = lax.axis_size("tm")
    col_index = lax.axis_index("col")
    tm_index = lax.axis_index("tm")
    row_count = diagonal.shape[1]
    node_count = diagonal.shape[2]
    block_rows = diagonal[0]
    arrow_part = arrowhead[0]
    left_fill = jnp.zeros_like(block_rows)
    right_fill = jnp.zeros_like(block_rows)
    factor_keep = block_rows
    pair_keep = jnp.zeros((2, row_count, node_count), jnp.float32)
    arrow_keep = arrow_part
    reduced = tip_matrix
    for distance in (1, 2):
        whole_block, whole_arrow = (
            lax.all_gather(block_rows, "col", axis=0, tiled=True),
            lax.all_gather(arrow_part, "col", axis=0, tiled=True),
        )
        if distance == 1:
            prior_link = fetch_link(coupling[0], 1)
            next_link = jnp.where(tm_index < tm_count - 1, coupling[0], 0.0)
        else:
            prior_link = fetch_link(right_fill, 2)
            next_link = fetch_link(left_fill, -2)
        active = tm_index % (2 * distance) == distance
        tip_rows = jnp.pad(whole_arrow.T, ((0, LANES - whole_arrow.shape[1]), (0, 0)))
        tiles = factorize(whole_block, jnp.concatenate([prior_link, next_link], 0), tip_rows)
        flat = jnp.where(active, jnp.transpose(tiles, (1, 0, 2)).reshape(-1, node_count), 0.0)
        factor = flat[:node_count]
        solved = flat[node_count : node_count + 2 * row_count]
        tipped = flat[node_count + 2 * row_count :][: whole_arrow.shape[1]]
        own_columns = lax.dynamic_slice_in_dim(tipped, col_index * row_count, row_count, 1)
        partial_value = outer_rows(own_columns, own_columns)
        reduced = reduced - lax.psum(partial_value, ("tm", "col"))
        factor_keep = jnp.where(
            active,
            lax.dynamic_slice_in_dim(factor, col_index * row_count, row_count, 0),
            factor_keep,
        )
        pair_keep = jnp.where(active, solved.reshape(2, row_count, node_count), pair_keep)
        arrow_keep = jnp.where(active, own_columns.T, arrow_keep)
        combined = local_products(solved)
        near_part, far_part = split_columns(combined, col_count, row_count)
        tip_part = outer_rows(solved, tipped)
        right_near, right_far, right_tip = send_update(
            (near_part[:row_count], far_part[:row_count], tip_part[:row_count]), -distance
        )
        left_far, left_near, left_tip = send_update(
            (near_part[row_count:], far_part[row_count:], tip_part[row_count:]), distance
        )
        receiving = tm_index % (2 * distance) == 0
        block_rows = jnp.where(receiving, block_rows - right_near - left_near, block_rows)
        arrow_part = jnp.where(receiving, arrow_part - right_tip - left_tip, arrow_part)
        right_fill = jnp.where(receiving, -right_far, right_fill)
        left_fill = jnp.where(receiving, -left_far, left_fill)
    remaining = tm_index % 4 == 0
    factors = jnp.where(remaining, block_rows, factor_keep)
    link_blocks = jnp.where(remaining, jnp.stack([left_fill, right_fill]), pair_keep)
    arrow_rows = jnp.where(remaining, arrow_part, arrow_keep)
    return (factors[None], link_blocks[None], arrow_rows[None], reduced)


def solution(mesh):
    in_specs = (P("tm", "col", None), P("tm", "col", None), P("tm", "col", None), P())
    out_specs = (P("tm", "col", None), P("tm", None, "col", None), P("tm", "col", None), P())
    return jax.shard_map(body, mesh=mesh, in_specs=in_specs, out_specs=out_specs, check_vma=False)
```

```python
import jax
import jax.numpy as jnp
from jax import lax
from jax.experimental import pallas as pl
from jax.experimental.pallas import tpu as pltpu
from jax.sharding import PartitionSpec as P

LANES = 128
PANEL = 16


def split_two(value):
    high = value.astype(jnp.bfloat16)
    low = (value - high.astype(jnp.float32)).astype(jnp.bfloat16)
    return high, low


def split_three(value):
    high = value.astype(jnp.bfloat16)
    rest = value - high.astype(jnp.float32)
    middle = rest.astype(jnp.bfloat16)
    low = (rest - middle.astype(jnp.float32)).astype(jnp.bfloat16)
    return high, middle, low


def spread_row(vec, row):
    return jnp.broadcast_to(vec[row : row + 1, :], (8, LANES))


def spread_lane(vec, lane):
    return jnp.take_along_axis(vec, jnp.full(vec.shape, lane, jnp.int32), axis=1)


def factor_tile(work):
    sub = lax.broadcasted_iota(jnp.int32, (8, LANES), 0)
    for panel in range(LANES // PANEL):
        first = panel * PANEL
        left = [work[first : first + 8, :LANES], work[first + 8 : first + 16, :LANES]]
        right = [work[first : first + 8, LANES:], work[first + 8 : first + 16, LANES:]]
        cols = [
            [spread_lane(left[h], first + c) if h >= c // 8 else None for h in range(2)]
            for c in range(PANEL)
        ]
        pivots = [None, None]
        for r in range(PANEL):
            h, q = r // 8, r % 8
            pivot = spread_row(cols[r][h], q)
            pivots[h] = pivot if q == 0 else jnp.where(sub == q, pivot, pivots[h])
            if r == PANEL - 1:
                break
            inverse = 1.0 / pivot
            coef, masked = [None, None], [None, None]
            for g in range(h, 2):
                coef[g] = cols[r][g] * inverse
                masked[g] = jnp.where(sub > q, coef[g], 0.0) if g == h else coef[g]
            for c in range(r + 1, PANEL):
                entry = spread_row(cols[r][c // 8], c % 8)
                for g in range(c // 8, 2):
                    cols[c][g] = cols[c][g] - coef[g] * entry
            left_row, right_row = spread_row(left[h], q), spread_row(right[h], q)
            for g in range(h, 2):
                if g == h and q == 7:
                    continue
                left[g] = left[g] - masked[g] * left_row
                right[g] = right[g] - masked[g] * right_row
        rows = []
        for h in range(2):
            scale = lax.rsqrt(pivots[h])
            rows.append(jnp.concatenate([left[h] * scale, right[h] * scale], 1))
        rows = jnp.concatenate(rows, 0)
        work[first : first + PANEL, :] = rows
        if first + PANEL < LANES:
            a, b, c = split_three(rows)
            lhs = jnp.concatenate([a, a, b, a, b, c], 0)[:, :LANES]
            rhs = jnp.concatenate([a, b, a, c, b, a], 0)
            update = lax.dot_general(
                lhs, rhs, (((0,), (0,)), ((), ())), preferred_element_type=jnp.float32
            )
            n = first + PANEL
            work[n:, :] = work[n:, :] - update[n:, :]


def dot_nt(left, right):
    return lax.dot_general(
        left, right, (((1,), (1,)), ((), ())), preferred_element_type=jnp.float32
    )


def wide_left(value):
    high, low = split_two(value)
    return jnp.concatenate([high, high, low], 1)


def wide_right(value):
    high, low = split_two(value)
    return jnp.concatenate([high, low, high], 1)


def factor_step(k, tiles, work, lhs, rhs, nodes, send_links):
    count, total, _ = tiles.shape
    row_id = lax.broadcasted_iota(jnp.int32, (LANES, LANES), 0)
    col_id = lax.broadcasted_iota(jnp.int32, (LANES, LANES), 1)
    here = pl.ds(pl.multiple_of(k * LANES, LANES), LANES)
    work[:, :LANES] = tiles[k, here, :]
    work[:, LANES:] = jnp.where(row_id == col_id, 1.0, 0.0)
    factor_tile(work)
    inverse = wide_right(work[:, LANES:])
    solved = dot_nt(wide_left(tiles[k]), inverse)
    rows = lax.broadcasted_iota(jnp.int32, (total, LANES), 0)
    solved = jnp.where(rows >= (k + 1) * LANES, solved, 0.0)
    tiles[k] = solved
    tiles[k, here, :] = jnp.where(row_id <= col_id, work[:, :LANES], 0.0).T
    send_links()
    high, low = split_two(solved)
    lhs[...] = jnp.concatenate([high, high, low], 1)
    rhs[...] = jnp.concatenate([high[:nodes], low[:nodes], high[:nodes]], 1)
    for pair in range(count // 2):
        top = 2 * LANES * pair

        @pl.when(2 * pair + 1 > k)
        def _():
            update = dot_nt(lhs[top:, :], rhs[top : top + 2 * LANES, :])

            @pl.when(2 * pair > k)
            def _():
                tiles[2 * pair, top:, :] = tiles[2 * pair, top:, :] - update[:, :LANES]

            tiles[2 * pair + 1, top:, :] = tiles[2 * pair + 1, top:, :] - update[:, LANES:]


MESH = pl.DeviceIdType.MESH


def kernel(
    chips, tip_rows, blocks,
    diag, coup, arrow, tip,
    factor_out, link_out, arrow_out, tip_out,
    tiles, dbuf, fbuf, nbuf, ybuf, gbuf, abuf, tbuf, tsrc, zbuf, zsrc, tipbuf,
    work, lhs, rhs, row_high, row_low, col_high, col_low,
    dsend, drecv, asend, arecv, ysend, yrecv, csend, frecv, gsend, nrecv,
    tsend, trecv, zsend, zrecv, bsend, brecv,
):
    t = lax.axis_index("tm")
    c = lax.axis_index("col")
    y, q = lax.div(c, 2), lax.rem(c, 2)
    sibling = c + 1 - 2 * q
    cols = 2 * chips
    count = cols
    nodes = count * LANES
    link_top, tip_top = nodes, nodes + 2 * LANES
    phase = lax.rem(t, 4)
    odd = lax.rem(t, 2)
    second = 1 - odd
    step_size = 2 - odd
    is_second = phase == 2
    last = blocks - 1

    def remote(src, dst, send, recv, tm, col):
        return pltpu.make_async_remote_copy(
            src_ref=src, dst_ref=dst, send_sem=send, recv_sem=recv,
            device_id={"tm": tm, "col": col}, device_id_type=MESH,
        )

    def arrived(dst, recv):
        remote(dst, dst, recv, recv, t, sibling).wait_recv()

    barrier = pltpu.get_barrier_semaphore()

    def greet(tm, col):
        pl.semaphore_signal(
            barrier, inc=1, device_id={"tm": tm, "col": col}, device_id_type=MESH
        )

    for other in range(1, cols):
        greet(t, lax.rem(c + other, cols))
    for other in range(1, blocks):
        greet(lax.rem(t + other, blocks), c)
    for other in (1, 2, blocks - 2, blocks - 1):
        greet(lax.rem(t + other, blocks), sibling)
    for k in range(count):
        tiles[k] = jnp.zeros(tiles.shape[1:], jnp.float32)
    pl.semaphore_wait(barrier, cols - 1 + blocks - 1 + 4)

    def coupling_copy(k):
        return remote(
            coup.at[0, :, pl.ds(k * LANES, LANES)], fbuf.at[0, k],
            csend.at[k], frecv.at[0, k], t + 1, c,
        )

    @pl.when(odd == 0)
    def _():
        for k in range(count):
            coupling_copy(k).start()

    own_rows = pl.ds(pl.multiple_of(c * LANES, LANES), LANES)

    def peer_of(other):
        return lax.rem(c + other, cols)

    def diag_copy(k, other):
        place = dbuf.at[k, own_rows]
        return remote(place, place, dsend.at[other, k], drecv.at[c, k], t, peer_of(other))

    def arrow_copy(other):
        return remote(
            abuf.at[c], abuf.at[c], asend.at[other], arecv.at[c], t, peer_of(other)
        )

    def link_copy(k, other):
        src = tiles.at[k, pl.ds(link_top, 2 * LANES)]
        if other < chips:
            target = 2 * lax.rem(y + other, chips) + q
            return remote(src, ybuf.at[y, k], ysend.at[other, k], yrecv.at[y, k], t, target)
        return remote(
            src, ybuf.at[chips, k], ysend.at[0, k], yrecv.at[chips, k], t, sibling
        )

    def near_wait(k, level):
        for side in range(2):
            arrived(nbuf.at[level, side, k], nrecv.at[level, side, k])

    def update_copy(left, right, m, p):
        tile = 2 * m + q
        src = gbuf.at[left, right, p, m]
        send = gsend.at[left, right, p, m]
        col = 2 * y + p
        if left == right:
            tm = t + step_size if left else t - step_size
            return remote(
                src, nbuf.at[second, left, tile], send, nrecv.at[second, left, tile], tm, col
            )
        if left == 0:
            tm, slot = t + 1 - 3 * second, second
        else:
            tm, slot = t - 1 + 3 * second, 1 - second
        return remote(src, fbuf.at[slot, tile], send, frecv.at[slot, tile], tm, col)

    def update_wanted(left, right):
        if left == right:
            return t + step_size <= last if left else t >= 0
        if left == 0:
            return (phase == 1) | is_second
        return (phase == 3) | (is_second & (t + 2 <= last))

    def tip_copy(side):
        tm = t + step_size if side else t - step_size
        return remote(
            tsrc.at[side], tbuf.at[second, side], tsend.at[side], trecv.at[second, side], tm, c
        )

    def square_copy():
        slot = lax.div(phase, 2)
        return remote(zsrc, zbuf.at[slot], zsend, zrecv.at[slot], t + 2 - phase, c)

    group = lax.div(t, 4)

    def total_copy(other):
        place = tipbuf.at[group]
        return remote(
            place, place, bsend.at[other], brecv.at[group], lax.rem(t + other, blocks), c
        )

    @pl.when(phase != 0)
    def _():
        @pl.when(odd == 1)
        def _():
            keep = jnp.where(t < last, 1.0, 0.0)
            for k in range(count):
                fbuf[1, k] = coup[0, :, k * LANES : (k + 1) * LANES] * keep

        abuf[c] = arrow[0].T

        @pl.when(is_second)
        def _():
            for side in range(2):
                arrived(tbuf.at[0, side], trecv.at[0, side])
            abuf[c] = abuf[c] + (tbuf[0, 0] + tbuf[0, 1])

        def send_tile(k):
            lanes = pl.ds(pl.multiple_of(k * LANES, LANES), LANES)
            dbuf[k, own_rows, :] = diag[0, :, lanes]

            @pl.when(is_second)
            def _():
                near_wait(k, 0)
                dbuf[k, own_rows, :] = dbuf[k, own_rows, :] + (nbuf[0, 0, k] + nbuf[0, 1, k])

            for other in range(1, cols):
                diag_copy(k, other).start()

        send_tile(0)
        for other in range(1, cols):
            arrow_copy(other).start()

        @pl.when(c >= 1)
        def _():
            send_tile(1)

        def collect(k):
            for slot in range(chips):
                @pl.when(slot != y)
                def _():
                    arrived(ybuf.at[slot, k], yrecv.at[slot, k])
            arrived(ybuf.at[chips, k], yrecv.at[chips, k])
            lanes = pl.ds(pl.multiple_of(k * LANES, LANES), LANES)
            for slot in range(chips):
                high, low = split_two(ybuf[slot, k])
                for side in range(2):
                    to = slice((side * chips + slot) * LANES, (side * chips + slot + 1) * LANES)
                    part = slice(side * LANES, (side + 1) * LANES)
                    col_high[to, lanes] = high[part]
                    col_low[to, lanes] = low[part]
            for place, value in ((q, ybuf[y, k]), (1 - q, ybuf[chips, k])):
                high, low = split_two(value)
                for side in range(2):
                    to = pl.ds(pl.multiple_of((2 * side + place) * LANES, LANES), LANES)
                    part = slice(side * LANES, (side + 1) * LANES)
                    row_high[to, lanes] = high[part]
                    row_low[to, lanes] = low[part]

        def step(k, carry):
            @pl.when(k + 2 <= c)
            def _():
                send_tile(k + 2)

            for other in range(cols):
                @pl.when((other >= k) & (other != c))
                def _():
                    arrived(
                        dbuf.at[k, pl.ds(other * LANES, LANES)], drecv.at[other, k]
                    )

            @pl.when(k != c)
            def _():
                arrived(abuf.at[k], arecv.at[k])

            arrived(fbuf.at[0, k], frecv.at[0, k])

            @pl.when(is_second)
            def _():
                arrived(fbuf.at[1, k], frecv.at[1, k])

            tiles[k, :nodes, :] = tiles[k, :nodes, :] + dbuf[k]
            for side in range(2):
                part = slice(link_top + side * LANES, link_top + (side + 1) * LANES)
                tiles[k, part, :] = tiles[k, part, :] + fbuf[side, k]
            tiles[k, tip_top:, :] = tiles[k, tip_top:, :] + abuf[k]

            def send_links():
                for other in range(1, chips + 1):
                    link_copy(k, other).start()
                ybuf[y, k] = tiles[k, link_top:tip_top, :]

            factor_step(k, tiles, work, lhs, rhs, nodes, send_links)

            @pl.when(k >= 1)
            def _():
                collect(k - 1)

            return carry

        lax.fori_loop(0, count, step, 0)

        terms = jnp.zeros((tip_rows, 2 * LANES + tip_rows), jnp.float32)
        for k in range(count):
            terms = terms - dot_nt(
                wide_left(tiles[k, tip_top:, :]), wide_right(tiles[k, link_top:, :])
            )
        tsrc[0] = terms[:, :LANES]
        tsrc[1] = terms[:, LANES : 2 * LANES]
        square = jnp.concatenate(
            [terms[:, 2 * LANES :], jnp.zeros((tip_rows, LANES - tip_rows), jnp.float32)], 1
        )
        tip_copy(0).start()

        @pl.when(t + step_size <= last)
        def _():
            tip_copy(1).start()

        @pl.when(odd == 1)
        def _():
            zsrc[...] = square
            square_copy().start()

        @pl.when(is_second)
        def _():
            for slot in range(2):
                arrived(zbuf.at[slot], zrecv.at[slot])
            tipbuf[group] = square + (zbuf[0] + zbuf[1])
            for other in range(1, blocks):
                total_copy(other).start()

        collect(count - 1)

        def contribution(left, right, half):
            width = min(2, chips - 2 * half)
            rows = slice(left * 2 * LANES, (left + 1) * 2 * LANES)
            first = (right * chips + 2 * half) * LANES
            columns = slice(first, first + width * LANES)
            value = dot_nt(row_high[rows, :], col_high[columns, :])
            value = value + dot_nt(row_high[rows, :], col_low[columns, :])
            value = value + dot_nt(row_low[rows, :], col_high[columns, :])
            for m in range(width):
                for p in range(2):
                    gbuf[left, right, p, 2 * half + m] = -value[
                        p * LANES : (p + 1) * LANES, m * LANES : (m + 1) * LANES
                    ]
            for m in range(width):
                for p in range(2):
                    update_copy(left, right, 2 * half + m, p).start()

        halves = (chips + 1) // 2
        order = [(side, side, half) for half in range(halves) for side in (1, 0)]
        order += [(side, 1 - side, half) for half in range(halves) for side in (0, 1)]
        for left, right, half in order:
            @pl.when(update_wanted(left, right))
            def _():
                contribution(left, right, half)

        for k in range(count):
            lanes = slice(k * LANES, (k + 1) * LANES)
            factor_out[0, :, lanes] = tiles[k, own_rows, :]
            for side in range(2):
                part = slice(link_top + side * LANES, link_top + (side + 1) * LANES)
                link_out[0, side, :, lanes] = tiles[k, part, :]
        arrow_out[0] = tiles[c, tip_top:, :].T

        def drain(k, carry):
            @pl.when(k <= c)
            def _():
                for other in range(1, cols):
                    diag_copy(k, other).wait_send()

            @pl.when((k > c) & is_second)
            def _():
                near_wait(k, 0)

            for other in range(1, chips + 1):
                link_copy(k, other).wait_send()
            return carry

        lax.fori_loop(0, count, drain, 0)
        for other in range(1, cols):
            arrow_copy(other).wait_send()
        tip_copy(0).wait_send()

        @pl.when(t + step_size <= last)
        def _():
            tip_copy(1).wait_send()

        @pl.when(odd == 1)
        def _():
            square_copy().wait_send()

        @pl.when(is_second)
        def _():
            for other in range(1, blocks):
                total_copy(other).wait_send()

        for left in range(2):
            for right in range(2):
                @pl.when(update_wanted(left, right))
                def _():
                    for m in range(chips):
                        for p in range(2):
                            update_copy(left, right, m, p).wait_send()

    @pl.when(phase == 0)
    def _():
        for level in range(2):
            @pl.when(t == 0)
            def _():
                nbuf[level, 1] = jnp.zeros(nbuf.shape[2:], jnp.float32)
                tbuf[level, 1] = jnp.zeros(tbuf.shape[2:], jnp.float32)

        @pl.when(t == 0)
        def _():
            fbuf[0] = jnp.zeros(fbuf.shape[1:], jnp.float32)

        for level in range(2):
            arrived(tbuf.at[level, 0], trecv.at[level, 0])

            @pl.when(t > 0)
            def _():
                arrived(tbuf.at[level, 1], trecv.at[level, 1])

        arrow_out[0] = arrow[0] + (
            (tbuf[0, 0] + tbuf[0, 1]) + (tbuf[1, 0] + tbuf[1, 1])
        ).T
        for level in range(2):
            for k in range(count):
                lanes = slice(k * LANES, (k + 1) * LANES)
                arrived(nbuf.at[level, 0, k], nrecv.at[level, 0, k])

                @pl.when(t > 0)
                def _():
                    arrived(nbuf.at[level, 1, k], nrecv.at[level, 1, k])

                base = diag[0, :, lanes] if level == 0 else factor_out[0, :, lanes]
                factor_out[0, :, lanes] = base + (nbuf[level, 0, k] + nbuf[level, 1, k])
        for k in range(count):
            lanes = slice(k * LANES, (k + 1) * LANES)
            arrived(fbuf.at[1, k], frecv.at[1, k])
            link_out[0, 1, :, lanes] = fbuf[1, k]

            @pl.when(t > 0)
            def _():
                arrived(fbuf.at[0, k], frecv.at[0, k])

            link_out[0, 0, :, lanes] = fbuf[0, k]

    @pl.when(odd == 0)
    def _():
        for k in range(count):
            coupling_copy(k).wait_send()

    total = tip[...]
    for index in range(blocks // 4):
        @pl.when(t != 4 * index + 2)
        def _():
            arrived(tipbuf.at[index], brecv.at[index])

        total = total + tipbuf[index][:, :tip_rows]
    tip_out[...] = total


def body(diagonal, coupling, arrowhead, tip_matrix):
    cols = lax.axis_size("col")
    blocks = lax.axis_size("tm")
    chips = cols // 2
    nodes = diagonal.shape[2]
    tip_rows = tip_matrix.shape[0]
    total = nodes + 2 * LANES + tip_rows
    count = nodes // LANES
    f32, bf16, dma = jnp.float32, jnp.bfloat16, pltpu.SemaphoreType.DMA
    scratch = [
        pltpu.VMEM((count, total, LANES), f32),
        pltpu.VMEM((count, nodes, LANES), f32),
        pltpu.VMEM((2, count, LANES, LANES), f32),
        pltpu.VMEM((2, 2, count, LANES, LANES), f32),
        pltpu.VMEM((chips + 1, count, 2 * LANES, LANES), f32),
        pltpu.VMEM((2, 2, 2, chips, LANES, LANES), f32),
        pltpu.VMEM((cols, tip_rows, LANES), f32),
        pltpu.VMEM((2, 2, tip_rows, LANES), f32),
        pltpu.VMEM((2, tip_rows, LANES), f32),
        pltpu.VMEM((2, tip_rows, LANES), f32),
        pltpu.VMEM((tip_rows, LANES), f32),
        pltpu.VMEM((blocks // 4, tip_rows, LANES), f32),
        pltpu.VMEM((LANES, 2 * LANES), f32),
        pltpu.VMEM((total, 3 * LANES), bf16),
        pltpu.VMEM((nodes, 3 * LANES), bf16),
        pltpu.VMEM((4 * LANES, nodes), bf16),
        pltpu.VMEM((4 * LANES, nodes), bf16),
        pltpu.VMEM((nodes, nodes), bf16),
        pltpu.VMEM((nodes, nodes), bf16),
        dma((cols, count)),
        dma((cols, count)),
        dma((cols,)),
        dma((cols,)),
        dma((chips, count)),
        dma((chips + 1, count)),
        dma((count,)),
        dma((2, count)),
        dma((2, 2, 2, chips)),
        dma((2, 2, count)),
        dma((2,)),
        dma((2, 2)),
        dma,
        dma((2,)),
        dma((blocks,)),
        dma((blocks // 4,)),
    ]

    def call(*refs):
        kernel(chips, tip_rows, blocks, *refs)

    return pl.pallas_call(
        call,
        out_shape=(
            jax.ShapeDtypeStruct(diagonal.shape, f32),
            jax.ShapeDtypeStruct((1, 2) + diagonal.shape[1:], f32),
            jax.ShapeDtypeStruct(arrowhead.shape, f32),
            jax.ShapeDtypeStruct(tip_matrix.shape, f32),
        ),
        in_specs=[pl.BlockSpec(memory_space=pltpu.VMEM)] * 4,
        out_specs=(pl.BlockSpec(memory_space=pltpu.VMEM),) * 4,
        scratch_shapes=scratch,
        compiler_params=pltpu.CompilerParams(
            collective_id=0, has_side_effects=True, vmem_limit_bytes=56 * 1024 * 1024
        ),
        name="cyclic_reduction",
    )(diagonal, coupling, arrowhead, tip_matrix)


def solution(mesh):
    in_specs = (P("tm", "col", None), P("tm", "col", None), P("tm", "col", None), P())
    out_specs = (P("tm", "col", None), P("tm", None, "col", None), P("tm", "col", None), P())
    return jax.shard_map(body, mesh=mesh, in_specs=in_specs, out_specs=out_specs, check_vma=False)
```

```python
import jax
import jax.numpy as jnp
from jax import lax
from jax.experimental import pallas as pl
from jax.experimental.pallas import tpu as pltpu
from jax.sharding import PartitionSpec as P

LANES = 128
PANEL = 16


def split_two(value):
    high = value.astype(jnp.bfloat16)
    low = (value - high.astype(jnp.float32)).astype(jnp.bfloat16)
    return high, low


def split_three(value):
    high = value.astype(jnp.bfloat16)
    rest = value - high.astype(jnp.float32)
    middle = rest.astype(jnp.bfloat16)
    low = (rest - middle.astype(jnp.float32)).astype(jnp.bfloat16)
    return high, middle, low


def spread_row(vec, row):
    return jnp.broadcast_to(vec[row : row + 1, :], (8, LANES))


def spread_lane(vec, lane):
    return jnp.take_along_axis(vec, jnp.full(vec.shape, lane, jnp.int32), axis=1)


def factor_tile(work):
    sub = lax.broadcasted_iota(jnp.int32, (8, LANES), 0)
    for panel in range(LANES // PANEL):
        first = panel * PANEL
        left = [work[first : first + 8, :LANES], work[first + 8 : first + 16, :LANES]]
        right = [work[first : first + 8, LANES:], work[first + 8 : first + 16, LANES:]]
        cols = [
            [spread_lane(left[h], first + c) if h >= c // 8 else None for h in range(2)]
            for c in range(PANEL)
        ]
        pivots = [None, None]
        for r in range(PANEL):
            h, q = r // 8, r % 8
            pivot = spread_row(cols[r][h], q)
            pivots[h] = pivot if q == 0 else jnp.where(sub == q, pivot, pivots[h])
            if r == PANEL - 1:
                break
            inverse = 1.0 / pivot
            coef, masked = [None, None], [None, None]
            for g in range(h, 2):
                coef[g] = cols[r][g] * inverse
                masked[g] = jnp.where(sub > q, coef[g], 0.0) if g == h else coef[g]
            for c in range(r + 1, PANEL):
                entry = spread_row(cols[r][c // 8], c % 8)
                for g in range(c // 8, 2):
                    cols[c][g] = cols[c][g] - coef[g] * entry
            left_row, right_row = spread_row(left[h], q), spread_row(right[h], q)
            for g in range(h, 2):
                if g == h and q == 7:
                    continue
                left[g] = left[g] - masked[g] * left_row
                right[g] = right[g] - masked[g] * right_row
        rows = []
        for h in range(2):
            scale = lax.rsqrt(pivots[h])
            rows.append(jnp.concatenate([left[h] * scale, right[h] * scale], 1))
        rows = jnp.concatenate(rows, 0)
        work[first : first + PANEL, :] = rows
        if first + PANEL < LANES:
            a, b, c = split_three(rows)
            lhs = jnp.concatenate([a, a, b, a, b, c], 0)[:, :LANES]
            rhs = jnp.concatenate([a, b, a, c, b, a], 0)
            update = lax.dot_general(
                lhs, rhs, (((0,), (0,)), ((), ())), preferred_element_type=jnp.float32
            )
            n = first + PANEL
            work[n:, :] = work[n:, :] - update[n:, :]


def dot_nt(left, right):
    return lax.dot_general(
        left, right, (((1,), (1,)), ((), ())), preferred_element_type=jnp.float32
    )


def wide_left(value):
    high, low = split_two(value)
    return jnp.concatenate([high, high, low], 1)


def wide_right(value):
    high, low = split_two(value)
    return jnp.concatenate([high, low, high], 1)


def factor_step(k, tiles, work, lhs, rhs, nodes, send_links):
    count, total, _ = tiles.shape
    row_id = lax.broadcasted_iota(jnp.int32, (LANES, LANES), 0)
    col_id = lax.broadcasted_iota(jnp.int32, (LANES, LANES), 1)
    here = pl.ds(pl.multiple_of(k * LANES, LANES), LANES)
    work[:, :LANES] = tiles[k, here, :]
    work[:, LANES:] = jnp.where(row_id == col_id, 1.0, 0.0)
    factor_tile(work)
    inverse = wide_right(work[:, LANES:])
    solved = dot_nt(wide_left(tiles[k]), inverse)
    rows = lax.broadcasted_iota(jnp.int32, (total, LANES), 0)
    solved = jnp.where(rows >= (k + 1) * LANES, solved, 0.0)
    tiles[k] = solved
    tiles[k, here, :] = jnp.where(row_id <= col_id, work[:, :LANES], 0.0).T
    send_links()
    high, low = split_two(solved)
    lhs[...] = jnp.concatenate([high, high, low], 1)
    rhs[...] = jnp.concatenate([high[:nodes], low[:nodes], high[:nodes]], 1)
    for pair in range(count // 2):
        top = 2 * LANES * pair

        @pl.when(2 * pair + 1 > k)
        def _():
            update = dot_nt(lhs[top:, :], rhs[top : top + 2 * LANES, :])

            @pl.when(2 * pair > k)
            def _():
                tiles[2 * pair, top:, :] = tiles[2 * pair, top:, :] - update[:, :LANES]

            tiles[2 * pair + 1, top:, :] = tiles[2 * pair + 1, top:, :] - update[:, LANES:]


MESH = pl.DeviceIdType.MESH


def dot_three(left_high, left_low, right_high, right_low):
    value = dot_nt(left_high, right_high)
    value = value + dot_nt(left_high, right_low)
    return value + dot_nt(left_low, right_high)


def kernel(
    chips, tip_rows, blocks,
    diag, coup, arrow, tip,
    factor_out, link_out, arrow_out, tip_out,
    tiles, dbuf, fbuf, nbuf, peer, pair, stream, gsrc, acc, kept_peer, kept_pair, kept_own,
    kept_acc, swap_src, swap_dst, abuf, tbuf, tsrc, zbuf, zsrc, tipbuf,
    work, lhs, rhs, row_high, row_low, col_high, col_low,
    kept_row_high, kept_row_low, kept_col_high, kept_col_low,
    dsend, drecv, asend, arecv, psend, precv, orecv, csend, frecv, gsend, nrecv,
    tsend, trecv, zsend, zrecv, bsend, brecv, ssend, srecv,
):
    t = lax.axis_index("tm")
    c = lax.axis_index("col")
    y, q = lax.div(c, 2), lax.rem(c, 2)
    sibling = c + 1 - 2 * q
    cols = 2 * chips
    count = cols
    nodes = count * LANES
    link_top, tip_top = nodes, nodes + 2 * LANES
    phase = lax.rem(t, 4)
    odd = lax.rem(t, 2)
    second = 1 - odd
    step_size = 2 - odd
    is_second = phase == 2
    last = blocks - 1
    early = nodes - LANES
    toward_next, toward_kept = t + 2 - phase, t - 2 + phase
    turn = lax.div(phase, 2)
    gather_at = pl.multiple_of(LANES * (1 - turn), LANES)
    stream_at = pl.multiple_of(LANES * turn, LANES)
    kept_exists = toward_kept <= last
    helps = (odd == 1) & kept_exists
    own_rows = pl.ds(pl.multiple_of(c * LANES, LANES), LANES)

    def remote(src, dst, send, recv, tm, col):
        return pltpu.make_async_remote_copy(
            src_ref=src, dst_ref=dst, send_sem=send, recv_sem=recv,
            device_id={"tm": tm, "col": col}, device_id_type=MESH,
        )

    def arrived(dst, recv):
        remote(dst, dst, recv, recv, t, sibling).wait_recv()

    barrier = pltpu.get_barrier_semaphore()

    def greet(tm, col):
        pl.semaphore_signal(
            barrier, inc=1, device_id={"tm": tm, "col": col}, device_id_type=MESH
        )

    for other in range(1, cols):
        greet(t, lax.rem(c + other, cols))
    for other in range(1, blocks):
        greet(lax.rem(t + other, blocks), c)
    for other in (1, blocks - 1):
        greet(lax.rem(t + other, blocks), sibling)
    for k in range(count):
        tiles[k] = jnp.zeros(tiles.shape[1:], jnp.float32)
    pl.semaphore_wait(barrier, cols - 1 + blocks - 1 + 2)

    def coupling_copy(k):
        return remote(
            coup.at[0, :, pl.ds(k * LANES, LANES)], fbuf.at[0, k],
            csend.at[k], frecv.at[0, k], t + 1, c,
        )

    @pl.when(odd == 0)
    def _():
        for k in range(count):
            coupling_copy(k).start()

    def peer_of(other):
        return lax.rem(c + other, cols)

    def same_core(other):
        return 2 * lax.rem(y + other, chips) + q

    def diag_copy(k, other):
        place = dbuf.at[k, own_rows]
        return remote(place, place, dsend.at[other, k], drecv.at[c, k], t, peer_of(other))

    def arrow_copy(other):
        return remote(
            abuf.at[c], abuf.at[c], asend.at[other], arecv.at[c], t, peer_of(other)
        )

    def own_links(level, k):
        return tiles.at[k, pl.ds(link_top, 2 * LANES)] if level == 0 else stream.at[k]

    def own_side(level, k, at):
        if level == 0:
            return tiles.at[k, pl.ds(pl.multiple_of(link_top + at, LANES), LANES)]
        return stream.at[k, pl.ds(at, LANES)]

    def side_copy(level, k, other):
        if other < chips:
            return remote(
                own_side(level, k, gather_at), peer.at[level, y, k],
                psend.at[level, 0, other, k], precv.at[level, 0, y, k], t, same_core(other),
            )
        return remote(
            own_links(level, k), pair.at[level, k],
            psend.at[level, 0, 0, k], precv.at[level, 0, chips, k], t, sibling,
        )

    def kept_copy(k):
        return remote(
            own_side(0, k, stream_at), kept_own.at[0, turn, k],
            psend.at[0, 1, 0, k], orecv.at[0, turn, k], toward_kept, c,
        )

    def helper_copy(k, side):
        return remote(
            tiles.at[k, pl.ds(link_top, 2 * LANES)], stream.at[k],
            psend.at[0, 0, side, k], orecv.at[1, 0, k], t - 1 + 2 * side, c,
        )

    def far_kept_copy(k, side):
        return remote(
            tiles.at[k, pl.ds(link_top + side * LANES, LANES)], kept_own.at[1, side, k],
            psend.at[0, 1, side, k], orecv.at[1, side, k], t - 2 + 4 * side, c,
        )

    def each_second(k, action):
        for side in range(2):
            @pl.when(t + 2 * side <= last)
            def _():
                action(helper_copy(k, side))
                action(far_kept_copy(k, side))

    def forward_copy(level, side, k, other):
        src = kept_own.at[level, side, k]
        if other < chips:
            return remote(
                src, kept_peer.at[level, side, y, k],
                psend.at[level, side, other, k], precv.at[level, side, y, k],
                t, same_core(other),
            )
        return remote(
            src, kept_pair.at[level, side, k],
            psend.at[level, side, 0, k], precv.at[level, side, chips, k], t, sibling,
        )

    def near_wait(k):
        for side in range(2):
            arrived(nbuf.at[side, k], nrecv.at[side, k])

    def product_copy(kind, m, p):
        tile = 2 * m + q
        src, send, col = gsrc.at[kind, p, m], gsend.at[kind, p, m], 2 * y + p
        if kind == 0:
            dst, recv, tm = nbuf.at[1 - turn, tile], nrecv.at[1 - turn, tile], toward_next
        elif kind == 1:
            dst, recv, tm = fbuf.at[turn, tile], frecv.at[turn, tile], toward_next
        else:
            dst, recv, tm = fbuf.at[1 - turn, tile], frecv.at[1 - turn, tile], toward_kept
        return remote(src, dst, send, recv, tm, col)

    def tip_copy(side):
        tm = t + step_size if side else t - step_size
        return remote(
            tsrc.at[side], tbuf.at[second, side], tsend.at[side], trecv.at[second, side], tm, c
        )

    def square_copy():
        return remote(zsrc, zbuf.at[turn], zsend, zrecv.at[turn], toward_next, c)

    group = lax.div(t, 4)

    def total_copy(other):
        place = tipbuf.at[group]
        return remote(
            place, place, bsend.at[other], brecv.at[group], lax.rem(t + other, blocks), c
        )

    def lanes_of(k):
        return pl.ds(pl.multiple_of(k * LANES, LANES), LANES)

    def exchange(level, k):
        for other in range(1, chips + 1):
            side_copy(level, k, other).start()
        peer[level, y, k] = own_side(level, k, gather_at)[...]

    def collect(level, k):
        for slot in range(chips):
            @pl.when(slot != y)
            def _():
                arrived(peer.at[level, slot, k], precv.at[level, 0, slot, k])
        arrived(pair.at[level, k], precv.at[level, 0, chips, k])
        lanes = lanes_of(k)
        for slot in range(chips):
            high, low = split_two(peer[level, slot, k])
            to = slice(slot * LANES, (slot + 1) * LANES)
            col_high[to, lanes] = high
            col_low[to, lanes] = low
        for place, at in ((0, stream_at), (1, gather_at)):
            for index, value in (
                (q, own_side(level, k, at)[...]),
                (1 - q, pair[level, k, pl.ds(at, LANES), :]),
            ):
                high, low = split_two(value)
                to = pl.ds(pl.multiple_of((2 * place + index) * LANES, LANES), LANES)
                row_high[to, lanes] = high
                row_low[to, lanes] = low

    def products(level):
        kinds = (0, 1) if level == 0 else (2,)
        rows_of = {0: slice(2 * LANES, 4 * LANES), 1: slice(0, 2 * LANES), 2: slice(0, 2 * LANES)}
        for kind in kinds:
            rows = rows_of[kind]
            acc[min(kind, 1)] = dot_three(
                row_high[rows, :early], row_low[rows, :early],
                col_high[:, :early], col_low[:, :early],
            )
        collect(level, count - 1)
        for kind in kinds:
            rows = rows_of[kind]
            value = acc[min(kind, 1)] + dot_three(
                row_high[rows, early:], row_low[rows, early:],
                col_high[:, early:], col_low[:, early:],
            )
            for m in range(chips):
                for p in range(2):
                    gsrc[kind, p, m] = -value[
                        p * LANES : (p + 1) * LANES, m * LANES : (m + 1) * LANES
                    ]
            for m in range(chips):
                for p in range(2):
                    product_copy(kind, m, p).start()

    @pl.when(phase != 0)
    def _():
        @pl.when(odd == 1)
        def _():
            keep = jnp.where(t < last, 1.0, 0.0)
            for k in range(count):
                fbuf[1, k] = coup[0, :, k * LANES : (k + 1) * LANES] * keep

        abuf[c] = arrow[0].T

        @pl.when(is_second)
        def _():
            for side in range(2):
                arrived(tbuf.at[0, side], trecv.at[0, side])
            abuf[c] = abuf[c] + (tbuf[0, 0] + tbuf[0, 1])

        def send_tile(k):
            dbuf[k, own_rows, :] = diag[0, :, lanes_of(k)]

            @pl.when(is_second)
            def _():
                near_wait(k)
                dbuf[k, own_rows, :] = dbuf[k, own_rows, :] + (nbuf[0, k] + nbuf[1, k])

            for other in range(1, cols):
                diag_copy(k, other).start()

        send_tile(0)
        for other in range(1, cols):
            arrow_copy(other).start()

        @pl.when(c >= 1)
        def _():
            send_tile(1)

        def step(k, carry):
            @pl.when(k + 2 <= c)
            def _():
                send_tile(k + 2)

            for other in range(cols):
                @pl.when((other >= k) & (other != c))
                def _():
                    arrived(
                        dbuf.at[k, pl.ds(other * LANES, LANES)], drecv.at[other, k]
                    )

            @pl.when(k != c)
            def _():
                arrived(abuf.at[k], arecv.at[k])

            arrived(fbuf.at[0, k], frecv.at[0, k])

            @pl.when(is_second)
            def _():
                arrived(fbuf.at[1, k], frecv.at[1, k])

            tiles[k, :nodes, :] = tiles[k, :nodes, :] + dbuf[k]
            for side in range(2):
                part = slice(link_top + side * LANES, link_top + (side + 1) * LANES)
                tiles[k, part, :] = tiles[k, part, :] + fbuf[side, k]
            tiles[k, tip_top:, :] = tiles[k, tip_top:, :] + abuf[k]

            def send_links():
                @pl.when(odd == 1)
                def _():
                    exchange(0, k)

                    @pl.when(kept_exists)
                    def _():
                        kept_copy(k).start()

                @pl.when(is_second)
                def _():
                    each_second(k, lambda copy: copy.start())

            factor_step(k, tiles, work, lhs, rhs, nodes, send_links)

            @pl.when((k >= 1) & (odd == 1))
            def _():
                collect(0, k - 1)

            return carry

        lax.fori_loop(0, count, step, 0)

        terms = jnp.zeros((tip_rows, 2 * LANES + tip_rows), jnp.float32)
        for k in range(count):
            terms = terms - dot_nt(
                wide_left(tiles[k, tip_top:, :]), wide_right(tiles[k, link_top:, :])
            )
        tsrc[0] = terms[:, :LANES]
        tsrc[1] = terms[:, LANES : 2 * LANES]
        square = jnp.concatenate(
            [terms[:, 2 * LANES :], jnp.zeros((tip_rows, LANES - tip_rows), jnp.float32)], 1
        )
        tip_copy(0).start()

        @pl.when(t + step_size <= last)
        def _():
            tip_copy(1).start()

        @pl.when(odd == 1)
        def _():
            zsrc[...] = square
            square_copy().start()
            products(0)

        @pl.when(is_second)
        def _():
            for slot in range(2):
                arrived(zbuf.at[slot], zrecv.at[slot])
            tipbuf[group] = square + (zbuf[0] + zbuf[1])
            for other in range(1, blocks):
                total_copy(other).start()

        for k in range(count):
            lanes = slice(k * LANES, (k + 1) * LANES)
            factor_out[0, :, lanes] = tiles[k, own_rows, :]
            for side in range(2):
                part = slice(link_top + side * LANES, link_top + (side + 1) * LANES)
                link_out[0, side, :, lanes] = tiles[k, part, :]
        arrow_out[0] = tiles[c, tip_top:, :].T

        @pl.when(helps)
        def _():
            def help_step(k, carry):
                arrived(stream.at[k], orecv.at[1, 0, k])
                exchange(1, k)

                @pl.when(k >= 1)
                def _():
                    collect(1, k - 1)

                return carry

            lax.fori_loop(0, count, help_step, 0)
            products(1)

        def drain(k, carry):
            @pl.when(k <= c)
            def _():
                for other in range(1, cols):
                    diag_copy(k, other).wait_send()

            @pl.when((k > c) & is_second)
            def _():
                near_wait(k)

            @pl.when(is_second)
            def _():
                each_second(k, lambda copy: copy.wait_send())

            @pl.when(odd == 1)
            def _():
                for other in range(1, chips + 1):
                    side_copy(0, k, other).wait_send()

            @pl.when(helps)
            def _():
                kept_copy(k).wait_send()
                for other in range(1, chips + 1):
                    side_copy(1, k, other).wait_send()

            return carry

        lax.fori_loop(0, count, drain, 0)
        for other in range(1, cols):
            arrow_copy(other).wait_send()
        tip_copy(0).wait_send()

        @pl.when(t + step_size <= last)
        def _():
            tip_copy(1).wait_send()

        @pl.when(odd == 1)
        def _():
            square_copy().wait_send()
            for kind in range(2):
                for m in range(chips):
                    for p in range(2):
                        product_copy(kind, m, p).wait_send()

        @pl.when(helps)
        def _():
            for m in range(chips):
                for p in range(2):
                    product_copy(2, m, p).wait_send()

        @pl.when(is_second)
        def _():
            for other in range(1, blocks):
                total_copy(other).wait_send()

    @pl.when(phase == 0)
    def _():
        @pl.when(t == 0)
        def _():
            for level in range(2):
                tbuf[level, 1] = jnp.zeros(tbuf.shape[2:], jnp.float32)
            fbuf[0] = jnp.zeros(fbuf.shape[1:], jnp.float32)
            for ref in (kept_row_high, kept_row_low, kept_col_high, kept_col_low):
                ref[1] = jnp.zeros(ref.shape[1:], jnp.bfloat16)

        def each_side(action):
            action(0)

            @pl.when(t > 0)
            def _():
                action(1)

        def kept_collect(level, side, k):
            for slot in range(chips):
                @pl.when(slot != y)
                def _():
                    arrived(kept_peer.at[level, side, slot, k], precv.at[level, side, slot, k])
            arrived(kept_pair.at[level, side, k], precv.at[level, side, chips, k])
            lanes = lanes_of(k)
            for slot in range(chips):
                high, low = split_two(kept_peer[level, side, slot, k])
                to = slice(slot * LANES, (slot + 1) * LANES)
                kept_col_high[side, to, lanes] = high
                kept_col_low[side, to, lanes] = low
            for index, value in (
                (q, kept_own[level, side, k]), (1 - q, kept_pair[level, side, k])
            ):
                high, low = split_two(value)
                to = pl.ds(pl.multiple_of(index * LANES, LANES), LANES)
                kept_row_high[side, to, lanes] = high
                kept_row_low[side, to, lanes] = low

        def kept_products(lanes):
            value = None
            for side in range(2):
                term = dot_three(
                    kept_row_high[side, :, lanes], kept_row_low[side, :, lanes],
                    kept_col_high[side, :, lanes], kept_col_low[side, :, lanes],
                )
                value = term if value is None else value + term
            return value

        for level in range(2):
            def kept_step(k, carry):
                def take(side):
                    arrived(kept_own.at[level, side, k], orecv.at[level, side, k])
                    for other in range(1, chips + 1):
                        forward_copy(level, side, k, other).start()
                    kept_peer[level, side, y, k] = kept_own[level, side, k]

                each_side(take)

                @pl.when(k >= 1)
                def _():
                    each_side(lambda side: kept_collect(level, side, k - 1))

                return carry

            lax.fori_loop(0, count, kept_step, 0)
            partial_sum = kept_products(slice(0, early))
            if level == 0:
                kept_acc[...] = partial_sum
            else:
                kept_acc[...] = kept_acc[...] + partial_sum
            each_side(lambda side: kept_collect(level, side, count - 1))
            kept_acc[...] = kept_acc[...] + kept_products(slice(early, nodes))

        def swap_copy():
            return remote(swap_src, swap_dst, ssend, srecv, t, sibling)

        other_rows = pl.ds(pl.multiple_of((1 - q) * LANES, LANES), LANES)
        for m in range(chips):
            swap_src[m] = kept_acc[other_rows, m * LANES : (m + 1) * LANES]
        swap_copy().start()
        my_rows = pl.ds(pl.multiple_of(q * LANES, LANES), LANES)
        for m in range(chips):
            lanes = lanes_of(2 * m + q)
            factor_out[0, :, lanes] = (
                diag[0, :, lanes] - kept_acc[my_rows, m * LANES : (m + 1) * LANES]
            )

        for level in range(2):
            each_side(lambda side: arrived(tbuf.at[level, side], trecv.at[level, side]))
        arrow_out[0] = arrow[0] + (
            (tbuf[0, 0] + tbuf[0, 1]) + (tbuf[1, 0] + tbuf[1, 1])
        ).T
        arrived(swap_dst, srecv)
        for m in range(chips):
            lanes = lanes_of(2 * m + 1 - q)
            factor_out[0, :, lanes] = diag[0, :, lanes] - swap_dst[m]
        for k in range(count):
            lanes = slice(k * LANES, (k + 1) * LANES)
            arrived(fbuf.at[1, k], frecv.at[1, k])
            link_out[0, 1, :, lanes] = fbuf[1, k]

            @pl.when(t > 0)
            def _():
                arrived(fbuf.at[0, k], frecv.at[0, k])

            link_out[0, 0, :, lanes] = fbuf[0, k]

        swap_copy().wait_send()

        def kept_drain(k, carry):
            def wait_all(side):
                for level in range(2):
                    for other in range(1, chips + 1):
                        forward_copy(level, side, k, other).wait_send()

            each_side(wait_all)
            return carry

        lax.fori_loop(0, count, kept_drain, 0)

    @pl.when(odd == 0)
    def _():
        for k in range(count):
            coupling_copy(k).wait_send()

    total = tip[...]
    for index in range(blocks // 4):
        @pl.when(t != 4 * index + 2)
        def _():
            arrived(tipbuf.at[index], brecv.at[index])

        total = total + tipbuf[index][:, :tip_rows]
    tip_out[...] = total


def body(diagonal, coupling, arrowhead, tip_matrix):
    cols = lax.axis_size("col")
    blocks = lax.axis_size("tm")
    chips = cols // 2
    nodes = diagonal.shape[2]
    tip_rows = tip_matrix.shape[0]
    total = nodes + 2 * LANES + tip_rows
    count = nodes // LANES
    half = chips * LANES
    f32, bf16, dma = jnp.float32, jnp.bfloat16, pltpu.SemaphoreType.DMA
    tile = (LANES, LANES)
    scratch = [
        pltpu.VMEM((count, total, LANES), f32),
        pltpu.VMEM((count, nodes, LANES), f32),
        pltpu.VMEM((2, count) + tile, f32),
        pltpu.VMEM((2, count) + tile, f32),
        pltpu.VMEM((2, chips, count) + tile, f32),
        pltpu.VMEM((2, count, 2 * LANES, LANES), f32),
        pltpu.VMEM((count, 2 * LANES, LANES), f32),
        pltpu.VMEM((3, 2, chips) + tile, f32),
        pltpu.VMEM((2, 2 * LANES, half), f32),
        pltpu.VMEM((2, 2, chips, count) + tile, f32),
        pltpu.VMEM((2, 2, count) + tile, f32),
        pltpu.VMEM((2, 2, count) + tile, f32),
        pltpu.VMEM((2 * LANES, half), f32),
        pltpu.VMEM((chips,) + tile, f32),
        pltpu.VMEM((chips,) + tile, f32),
        pltpu.VMEM((cols, tip_rows, LANES), f32),
        pltpu.VMEM((2, 2, tip_rows, LANES), f32),
        pltpu.VMEM((2, tip_rows, LANES), f32),
        pltpu.VMEM((2, tip_rows, LANES), f32),
        pltpu.VMEM((tip_rows, LANES), f32),
        pltpu.VMEM((blocks // 4, tip_rows, LANES), f32),
        pltpu.VMEM((LANES, 2 * LANES), f32),
        pltpu.VMEM((total, 3 * LANES), bf16),
        pltpu.VMEM((nodes, 3 * LANES), bf16),
        pltpu.VMEM((4 * LANES, nodes), bf16),
        pltpu.VMEM((4 * LANES, nodes), bf16),
        pltpu.VMEM((half, nodes), bf16),
        pltpu.VMEM((half, nodes), bf16),
        pltpu.VMEM((2, 2 * LANES, nodes), bf16),
        pltpu.VMEM((2, 2 * LANES, nodes), bf16),
        pltpu.VMEM((2, half, nodes), bf16),
        pltpu.VMEM((2, half, nodes), bf16),
        dma((cols, count)),
        dma((cols, count)),
        dma((cols,)),
        dma((cols,)),
        dma((2, 2, max(chips, 2), count)),
        dma((2, 2, chips + 1, count)),
        dma((2, 2, count)),
        dma((count,)),
        dma((2, count)),
        dma((3, 2, chips)),
        dma((2, count)),
        dma((2,)),
        dma((2, 2)),
        dma,
        dma((2,)),
        dma((blocks,)),
        dma((blocks // 4,)),
        dma,
        dma,
    ]

    def call(*refs):
        kernel(chips, tip_rows, blocks, *refs)

    return pl.pallas_call(
        call,
        out_shape=(
            jax.ShapeDtypeStruct(diagonal.shape, f32),
            jax.ShapeDtypeStruct((1, 2) + diagonal.shape[1:], f32),
            jax.ShapeDtypeStruct(arrowhead.shape, f32),
            jax.ShapeDtypeStruct(tip_matrix.shape, f32),
        ),
        in_specs=[pl.BlockSpec(memory_space=pltpu.VMEM)] * 4,
        out_specs=(pl.BlockSpec(memory_space=pltpu.VMEM),) * 4,
        scratch_shapes=scratch,
        compiler_params=pltpu.CompilerParams(
            collective_id=0, has_side_effects=True, vmem_limit_bytes=60 * 1024 * 1024
        ),
        name="cyclic_reduction",
    )(diagonal, coupling, arrowhead, tip_matrix)


def solution(mesh):
    in_specs = (P("tm", "col", None), P("tm", "col", None), P("tm", "col", None), P())
    out_specs = (P("tm", "col", None), P("tm", None, "col", None), P("tm", "col", None), P())
    return jax.shard_map(body, mesh=mesh, in_specs=in_specs, out_specs=out_specs, check_vma=False)
```

```python
import jax
import jax.numpy as jnp
from jax import lax
from jax.experimental import pallas as pl
from jax.experimental.pallas import tpu as pltpu
from jax.sharding import PartitionSpec as P

LANES = 128
PANEL = 16


def split_two(value):
    high = value.astype(jnp.bfloat16)
    low = (value - high.astype(jnp.float32)).astype(jnp.bfloat16)
    return high, low


def split_three(value):
    high = value.astype(jnp.bfloat16)
    rest = value - high.astype(jnp.float32)
    middle = rest.astype(jnp.bfloat16)
    low = (rest - middle.astype(jnp.float32)).astype(jnp.bfloat16)
    return high, middle, low


def spread_row(vec, row):
    return jnp.broadcast_to(vec[row : row + 1, :], (8, LANES))


def spread_lane(vec, lane):
    return jnp.take_along_axis(vec, jnp.full(vec.shape, lane, jnp.int32), axis=1)


def factor_tile(work):
    sub = lax.broadcasted_iota(jnp.int32, (8, LANES), 0)
    for panel in range(LANES // PANEL):
        first = panel * PANEL
        left = [work[first : first + 8, :LANES], work[first + 8 : first + 16, :LANES]]
        right = [work[first : first + 8, LANES:], work[first + 8 : first + 16, LANES:]]
        cols = [
            [spread_lane(left[h], first + c) if h >= c // 8 else None for h in range(2)]
            for c in range(PANEL)
        ]
        pivots = [None, None]
        for r in range(PANEL):
            h, q = r // 8, r % 8
            pivot = spread_row(cols[r][h], q)
            pivots[h] = pivot if q == 0 else jnp.where(sub == q, pivot, pivots[h])
            if r == PANEL - 1:
                break
            inverse = 1.0 / pivot
            coef, masked = [None, None], [None, None]
            for g in range(h, 2):
                coef[g] = cols[r][g] * inverse
                masked[g] = jnp.where(sub > q, coef[g], 0.0) if g == h else coef[g]
            for c in range(r + 1, PANEL):
                entry = spread_row(cols[r][c // 8], c % 8)
                for g in range(c // 8, 2):
                    cols[c][g] = cols[c][g] - coef[g] * entry
            left_row, right_row = spread_row(left[h], q), spread_row(right[h], q)
            for g in range(h, 2):
                if g == h and q == 7:
                    continue
                left[g] = left[g] - masked[g] * left_row
                right[g] = right[g] - masked[g] * right_row
        rows = []
        for h in range(2):
            scale = lax.rsqrt(pivots[h])
            rows.append(jnp.concatenate([left[h] * scale, right[h] * scale], 1))
        rows = jnp.concatenate(rows, 0)
        work[first : first + PANEL, :] = rows
        if first + PANEL < LANES:
            a, b, c = split_three(rows)
            lhs = jnp.concatenate([a, a, b, a, b, c], 0)[:, :LANES]
            rhs = jnp.concatenate([a, b, a, c, b, a], 0)
            update = lax.dot_general(
                lhs, rhs, (((0,), (0,)), ((), ())), preferred_element_type=jnp.float32
            )
            n = first + PANEL
            work[n:, :] = work[n:, :] - update[n:, :]


def dot_nt(left, right):
    return lax.dot_general(
        left, right, (((1,), (1,)), ((), ())), preferred_element_type=jnp.float32
    )


def wide_left(value):
    high, low = split_two(value)
    return jnp.concatenate([high, high, low], 1)


def wide_right(value):
    high, low = split_two(value)
    return jnp.concatenate([high, low, high], 1)


def factor_step(k, tiles, work, lhs, rhs, nodes, send_links):
    count, total, _ = tiles.shape
    row_id = lax.broadcasted_iota(jnp.int32, (LANES, LANES), 0)
    col_id = lax.broadcasted_iota(jnp.int32, (LANES, LANES), 1)
    here = pl.ds(pl.multiple_of(k * LANES, LANES), LANES)
    work[:, :LANES] = tiles[k, here, :]
    work[:, LANES:] = jnp.where(row_id == col_id, 1.0, 0.0)
    factor_tile(work)
    inverse = wide_right(work[:, LANES:])
    solved = dot_nt(wide_left(tiles[k]), inverse)
    rows = lax.broadcasted_iota(jnp.int32, (total, LANES), 0)
    solved = jnp.where(rows >= (k + 1) * LANES, solved, 0.0)
    tiles[k] = solved
    tiles[k, here, :] = jnp.where(row_id <= col_id, work[:, :LANES], 0.0).T
    send_links()
    high, low = split_two(solved)
    lhs[...] = jnp.concatenate([high, high, low], 1)
    rhs[...] = jnp.concatenate([high[:nodes], low[:nodes], high[:nodes]], 1)
    for pair in range(count // 2):
        top = 2 * LANES * pair

        @pl.when(2 * pair + 1 > k)
        def _():
            update = dot_nt(lhs[top:, :], rhs[top : top + 2 * LANES, :])

            @pl.when(2 * pair > k)
            def _():
                tiles[2 * pair, top:, :] = tiles[2 * pair, top:, :] - update[:, :LANES]

            tiles[2 * pair + 1, top:, :] = tiles[2 * pair + 1, top:, :] - update[:, LANES:]


MESH = pl.DeviceIdType.MESH


def dot_three(left_high, left_low, right_high, right_low):
    value = dot_nt(left_high, right_high)
    value = value + dot_nt(left_high, right_low)
    return value + dot_nt(left_low, right_high)


def kernel(
    chips, tip_rows, blocks,
    diag, coup, arrow, tip,
    factor_out, link_out, arrow_out, tip_out,
    tiles, dbuf, fbuf, nbuf, peer, pair, stream, gsrc, acc, kept_peer, kept_pair, kept_own,
    kept_acc, swap_src, swap_dst, abuf, tbuf, tsrc, zbuf, zsrc, tipbuf,
    work, lhs, rhs, row_high, row_low, col_high, col_low,
    kept_row_high, kept_row_low, kept_col_high, kept_col_low,
    dsend, drecv, asend, arecv, psend, precv, orecv, csend, frecv, gsend, nrecv,
    tsend, trecv, zsend, zrecv, bsend, brecv, ssend, srecv,
):
    t = lax.axis_index("tm")
    c = lax.axis_index("col")
    y, q = lax.div(c, 2), lax.rem(c, 2)
    sibling = c + 1 - 2 * q
    cols = 2 * chips
    count = cols
    nodes = count * LANES
    link_top, tip_top = nodes, nodes + 2 * LANES
    phase = lax.rem(t, 4)
    odd = lax.rem(t, 2)
    second = 1 - odd
    step_size = 2 - odd
    is_second = phase == 2
    last = blocks - 1
    early = nodes - LANES
    toward_next, toward_kept = t + 2 - phase, t - 2 + phase
    turn = lax.div(phase, 2)
    gather_at = pl.multiple_of(LANES * (1 - turn), LANES)
    stream_at = pl.multiple_of(LANES * turn, LANES)
    kept_exists = toward_kept <= last
    helps = (odd == 1) & kept_exists
    own_rows = pl.ds(pl.multiple_of(c * LANES, LANES), LANES)

    def remote(src, dst, send, recv, tm, col):
        return pltpu.make_async_remote_copy(
            src_ref=src, dst_ref=dst, send_sem=send, recv_sem=recv,
            device_id={"tm": tm, "col": col}, device_id_type=MESH,
        )

    def arrived(dst, recv):
        remote(dst, dst, recv, recv, t, sibling).wait_recv()

    barrier = pltpu.get_barrier_semaphore()

    def greet(tm, col):
        pl.semaphore_signal(
            barrier, inc=1, device_id={"tm": tm, "col": col}, device_id_type=MESH
        )

    for other in range(1, cols):
        greet(t, lax.rem(c + other, cols))
    for other in range(1, blocks):
        greet(lax.rem(t + other, blocks), c)
    for other in (1, blocks - 1):
        greet(lax.rem(t + other, blocks), sibling)
    for k in range(count):
        tiles[k] = jnp.zeros(tiles.shape[1:], jnp.float32)
    pl.semaphore_wait(barrier, cols - 1 + blocks - 1 + 2)

    def coupling_copy(k):
        return remote(
            coup.at[0, :, pl.ds(k * LANES, LANES)], fbuf.at[0, k],
            csend.at[k], frecv.at[0, k], t + 1, c,
        )

    @pl.when(odd == 0)
    def _():
        for k in range(count):
            coupling_copy(k).start()

    def peer_of(other):
        return lax.rem(c + other, cols)

    def same_core(other):
        return 2 * lax.rem(y + other, chips) + q

    hops = [1, chips - 1] if chips > 2 else list(range(1, chips))
    rings = chips == 4

    def relay_ends(k):
        turn_at = 1 - 2 * lax.rem(y + k, 2)
        return lax.rem(y + turn_at + chips, chips), lax.rem(y - turn_at + chips, chips)

    def tile_copy(src_col, k, slot, target):
        place = dbuf.at[k, pl.ds(pl.multiple_of(src_col * LANES, LANES), LANES)]
        return remote(place, place, dsend.at[slot, k], drecv.at[src_col, k], t, target)

    def tile_arrived(src_col, k):
        place = dbuf.at[k, pl.ds(pl.multiple_of(src_col * LANES, LANES), LANES)]
        arrived(place, drecv.at[src_col, k])

    def own_tile_copies(k):
        return [tile_copy(c, k, 0, sibling)] + [
            tile_copy(c, k, 1 + i, same_core(hop)) for i, hop in enumerate(hops)
        ]

    def near_forwards(k, action):
        for i, hop in enumerate(hops):
            src = same_core(hop)

            @pl.when(src >= k)
            def _():
                action(src, tile_copy(src, k, 3 + i, sibling))

    def ring_forward(k, action):
        if rings:
            source, target = relay_ends(k)
            src = 2 * source + q

            @pl.when(src >= k)
            def _():
                action(tile_copy(src, k, 6, 2 * target + q))

    def opposite_forward(k, action):
        if rings:
            src = same_core(2)

            @pl.when(src >= k)
            def _():
                action(src, tile_copy(src, k, 5, sibling))

    def pass_on(src, k, copy):
        tile_arrived(src, k)
        copy.start()

    def relay_near(k):
        near_forwards(k, lambda src, copy: pass_on(src, k, copy))
        ring_forward(k, lambda copy: copy.start())

    def relay_opposite(k):
        opposite_forward(k, lambda src, copy: pass_on(src, k, copy))

    def arrow_copy(other):
        return remote(
            abuf.at[c], abuf.at[c], asend.at[other], arecv.at[c], t, peer_of(other)
        )

    def own_links(level, k):
        return tiles.at[k, pl.ds(link_top, 2 * LANES)] if level == 0 else stream.at[k]

    def own_side(level, k, at):
        if level == 0:
            return tiles.at[k, pl.ds(pl.multiple_of(link_top + at, LANES), LANES)]
        return stream.at[k, pl.ds(at, LANES)]

    def spread(src, place, level, side, k, action):
        for i, hop in enumerate(hops):
            action(remote(
                src, place.at[y, k], psend.at[level, side, 1 + i, k],
                precv.at[level, side, y, k], t, same_core(hop),
            ))
        if rings:
            @pl.when(k == count - 1)
            def _():
                action(remote(
                    src, place.at[y, k], psend.at[level, side, 3, k],
                    precv.at[level, side, y, k], t, same_core(2),
                ))

    def relay(place, level, side, k, action):
        if rings:
            @pl.when(k < count - 1)
            def _():
                source, target = relay_ends(k)
                tile = place.at[source, k]
                action(remote(
                    tile, tile, psend.at[level, side, 3, k],
                    precv.at[level, side, source, k], t, 2 * target + q,
                ))

    def relay_when_here(place, level, side, k):
        for hop in hops:
            slot = lax.rem(y + hop, chips)
            arrived(place.at[slot, k], precv.at[level, side, slot, k])
        relay(place, level, side, k, lambda copy: copy.start())

    def opposite_arrived(place, level, side, k):
        if rings:
            slot = lax.rem(y + 2, chips)
            arrived(place.at[slot, k], precv.at[level, side, slot, k])

    def pair_copy(level, k):
        return remote(
            own_links(level, k), pair.at[level, k],
            psend.at[level, 0, 0, k], precv.at[level, 0, chips, k], t, sibling,
        )

    def kept_copy(level, k):
        return remote(
            own_side(level, k, stream_at), kept_own.at[level, turn, k],
            psend.at[level, 1, 0, k], orecv.at[level, turn, k], toward_kept, c,
        )

    def helper_copy(k, side):
        return remote(
            tiles.at[k, pl.ds(link_top, 2 * LANES)], stream.at[k],
            psend.at[0, 0, side, k], orecv.at[1, 0, k], t - 1 + 2 * side, c,
        )

    def each_second(k, action):
        for side in range(2):
            @pl.when(t + 2 * side <= last)
            def _():
                action(helper_copy(k, side))

    def kept_pair_copy(level, side, k):
        return remote(
            kept_own.at[level, side, k], kept_pair.at[level, side, k],
            psend.at[level, side, 0, k], precv.at[level, side, chips, k], t, sibling,
        )

    def near_wait(k):
        for side in range(2):
            arrived(nbuf.at[side, k], nrecv.at[side, k])

    def product_copy(kind, m, p):
        tile = 2 * m + q
        src, send, col = gsrc.at[kind, p, m], gsend.at[kind, p, m], 2 * y + p
        if kind == 0:
            dst, recv, tm = nbuf.at[1 - turn, tile], nrecv.at[1 - turn, tile], toward_next
        elif kind == 1:
            dst, recv, tm = fbuf.at[turn, tile], frecv.at[turn, tile], toward_next
        else:
            dst, recv, tm = fbuf.at[1 - turn, tile], frecv.at[1 - turn, tile], toward_kept
        return remote(src, dst, send, recv, tm, col)

    def tip_copy(side):
        tm = t + step_size if side else t - step_size
        return remote(
            tsrc.at[side], tbuf.at[second, side], tsend.at[side], trecv.at[second, side], tm, c
        )

    def square_copy():
        return remote(zsrc, zbuf.at[turn], zsend, zrecv.at[turn], toward_next, c)

    group = lax.div(t, 4)

    def total_copy(other):
        place = tipbuf.at[group]
        return remote(
            place, place, bsend.at[other], brecv.at[group], lax.rem(t + other, blocks), c
        )

    def lanes_of(k):
        return pl.ds(pl.multiple_of(k * LANES, LANES), LANES)

    def exchange(level, k):
        spread(
            own_side(level, k, gather_at), peer.at[level], level, 0, k, lambda copy: copy.start()
        )
        pair_copy(level, k).start()

        @pl.when(kept_exists)
        def _():
            kept_copy(level, k).start()

        peer[level, y, k] = own_side(level, k, gather_at)[...]

    def pass_links(level, k):
        relay_when_here(peer.at[level], level, 0, k)

    def exchange_done(level, k):
        spread(
            own_side(level, k, gather_at), peer.at[level], level, 0, k,
            lambda copy: copy.wait_send(),
        )
        relay(peer.at[level], level, 0, k, lambda copy: copy.wait_send())
        pair_copy(level, k).wait_send()

        @pl.when(kept_exists)
        def _():
            kept_copy(level, k).wait_send()

    def collect(level, k):
        opposite_arrived(peer.at[level], level, 0, k)
        arrived(pair.at[level, k], precv.at[level, 0, chips, k])
        lanes = lanes_of(k)
        for slot in range(chips):
            high, low = split_two(peer[level, slot, k])
            to = slice(slot * LANES, (slot + 1) * LANES)
            col_high[to, lanes] = high
            col_low[to, lanes] = low
        for place, at in ((0, stream_at), (1, gather_at)):
            for index, value in (
                (q, own_side(level, k, at)[...]),
                (1 - q, pair[level, k, pl.ds(at, LANES), :]),
            ):
                high, low = split_two(value)
                to = pl.ds(pl.multiple_of((2 * place + index) * LANES, LANES), LANES)
                row_high[to, lanes] = high
                row_low[to, lanes] = low

    def products(level):
        kinds = (0, 1) if level == 0 else (2,)
        collect(level, count - 2)
        rows_of = {0: slice(2 * LANES, 4 * LANES), 1: slice(0, 2 * LANES), 2: slice(0, 2 * LANES)}
        for kind in kinds:
            rows = rows_of[kind]
            acc[min(kind, 1)] = dot_three(
                row_high[rows, :early], row_low[rows, :early],
                col_high[:, :early], col_low[:, :early],
            )
        pass_links(level, count - 1)
        collect(level, count - 1)
        for kind in kinds:
            rows = rows_of[kind]
            value = acc[min(kind, 1)] + dot_three(
                row_high[rows, early:], row_low[rows, early:],
                col_high[:, early:], col_low[:, early:],
            )
            for m in range(chips):
                for p in range(2):
                    gsrc[kind, p, m] = -value[
                        p * LANES : (p + 1) * LANES, m * LANES : (m + 1) * LANES
                    ]
            for m in range(chips):
                for p in range(2):
                    product_copy(kind, m, p).start()

    @pl.when(phase != 0)
    def _():
        @pl.when(odd == 1)
        def _():
            keep = jnp.where(t < last, 1.0, 0.0)
            for k in range(count):
                fbuf[1, k] = coup[0, :, k * LANES : (k + 1) * LANES] * keep

        abuf[c] = arrow[0].T

        @pl.when(is_second)
        def _():
            for side in range(2):
                arrived(tbuf.at[0, side], trecv.at[0, side])
            abuf[c] = abuf[c] + (tbuf[0, 0] + tbuf[0, 1])

        def send_tile(k):
            dbuf[k, own_rows, :] = diag[0, :, lanes_of(k)]

            @pl.when(is_second)
            def _():
                near_wait(k)
                dbuf[k, own_rows, :] = dbuf[k, own_rows, :] + (nbuf[0, k] + nbuf[1, k])

            for copy in own_tile_copies(k):
                copy.start()

        send_tile(0)
        for other in range(1, cols):
            arrow_copy(other).start()

        @pl.when(c >= 1)
        def _():
            send_tile(1)

        relay_near(0)

        @pl.when(c >= 2)
        def _():
            send_tile(2)

        relay_opposite(0)
        relay_near(1)

        def step(k, carry):
            @pl.when(k + 3 <= c)
            def _():
                send_tile(k + 3)

            @pl.when(k + 1 < count)
            def _():
                relay_opposite(k + 1)

            @pl.when(k + 2 < count)
            def _():
                relay_near(k + 2)

            for chip in range(chips):
                src = 2 * chip + 1 - q

                @pl.when(src >= k)
                def _():
                    tile_arrived(src, k)

            @pl.when(k != c)
            def _():
                arrived(abuf.at[k], arecv.at[k])

            arrived(fbuf.at[0, k], frecv.at[0, k])

            @pl.when(is_second)
            def _():
                arrived(fbuf.at[1, k], frecv.at[1, k])

            tiles[k, :nodes, :] = tiles[k, :nodes, :] + dbuf[k]
            for side in range(2):
                part = slice(link_top + side * LANES, link_top + (side + 1) * LANES)
                tiles[k, part, :] = tiles[k, part, :] + fbuf[side, k]
            tiles[k, tip_top:, :] = tiles[k, tip_top:, :] + abuf[k]

            def send_links():
                @pl.when(odd == 1)
                def _():
                    exchange(0, k)

                @pl.when(is_second)
                def _():
                    each_second(k, lambda copy: copy.start())

            factor_step(k, tiles, work, lhs, rhs, nodes, send_links)

            @pl.when((k >= 1) & (odd == 1))
            def _():
                pass_links(0, k - 1)

            @pl.when((k >= 2) & (odd == 1))
            def _():
                collect(0, k - 2)

            return carry

        lax.fori_loop(0, count, step, 0)

        terms = jnp.zeros((tip_rows, 2 * LANES + tip_rows), jnp.float32)
        for k in range(count):
            terms = terms - dot_nt(
                wide_left(tiles[k, tip_top:, :]), wide_right(tiles[k, link_top:, :])
            )
        tsrc[0] = terms[:, :LANES]
        tsrc[1] = terms[:, LANES : 2 * LANES]
        square = jnp.concatenate(
            [terms[: tip_rows // 2, 2 * LANES :], terms[tip_rows // 2 :, 2 * LANES :]], 1
        )
        tip_copy(0).start()

        @pl.when(t + step_size <= last)
        def _():
            tip_copy(1).start()

        @pl.when(odd == 1)
        def _():
            zsrc[...] = square
            square_copy().start()
            products(0)

        @pl.when(is_second)
        def _():
            for slot in range(2):
                arrived(zbuf.at[slot], zrecv.at[slot])
            tipbuf[group] = square + (zbuf[0] + zbuf[1])
            for other in range(1, blocks):
                total_copy(other).start()

        for k in range(count):
            lanes = slice(k * LANES, (k + 1) * LANES)
            factor_out[0, :, lanes] = tiles[k, own_rows, :]
            for side in range(2):
                part = slice(link_top + side * LANES, link_top + (side + 1) * LANES)
                link_out[0, side, :, lanes] = tiles[k, part, :]
        arrow_out[0] = tiles[c, tip_top:, :].T

        @pl.when(helps)
        def _():
            def help_step(k, carry):
                arrived(stream.at[k], orecv.at[1, 0, k])
                exchange(1, k)

                @pl.when(k >= 1)
                def _():
                    pass_links(1, k - 1)

                @pl.when(k >= 2)
                def _():
                    collect(1, k - 2)

                return carry

            lax.fori_loop(0, count, help_step, 0)
            products(1)

        def drain(k, carry):
            @pl.when(k <= c)
            def _():
                for copy in own_tile_copies(k):
                    copy.wait_send()

            near_forwards(k, lambda src, copy: copy.wait_send())
            ring_forward(k, lambda copy: copy.wait_send())
            opposite_forward(k, lambda src, copy: copy.wait_send())

            @pl.when((k > c) & is_second)
            def _():
                near_wait(k)

            @pl.when(is_second)
            def _():
                each_second(k, lambda copy: copy.wait_send())

            @pl.when(odd == 1)
            def _():
                exchange_done(0, k)

            @pl.when(helps)
            def _():
                exchange_done(1, k)

            return carry

        lax.fori_loop(0, count, drain, 0)
        for other in range(1, cols):
            arrow_copy(other).wait_send()
        tip_copy(0).wait_send()

        @pl.when(t + step_size <= last)
        def _():
            tip_copy(1).wait_send()

        @pl.when(odd == 1)
        def _():
            square_copy().wait_send()
            for kind in range(2):
                for m in range(chips):
                    for p in range(2):
                        product_copy(kind, m, p).wait_send()

        @pl.when(helps)
        def _():
            for m in range(chips):
                for p in range(2):
                    product_copy(2, m, p).wait_send()

        @pl.when(is_second)
        def _():
            for other in range(1, blocks):
                total_copy(other).wait_send()

    @pl.when(phase == 0)
    def _():
        @pl.when(t == 0)
        def _():
            for level in range(2):
                tbuf[level, 1] = jnp.zeros(tbuf.shape[2:], jnp.float32)
            fbuf[0] = jnp.zeros(fbuf.shape[1:], jnp.float32)
            for ref in (kept_row_high, kept_row_low, kept_col_high, kept_col_low):
                ref[1] = jnp.zeros(ref.shape[1:], jnp.bfloat16)

        def each_side(action):
            action(0)

            @pl.when(t > 0)
            def _():
                action(1)

        def kept_pass(level, side, k):
            relay_when_here(kept_peer.at[level, side], level, side, k)

        def kept_collect(level, side, k):
            opposite_arrived(kept_peer.at[level, side], level, side, k)
            arrived(kept_pair.at[level, side, k], precv.at[level, side, chips, k])
            lanes = lanes_of(k)
            for slot in range(chips):
                high, low = split_two(kept_peer[level, side, slot, k])
                to = slice(slot * LANES, (slot + 1) * LANES)
                kept_col_high[side, to, lanes] = high
                kept_col_low[side, to, lanes] = low
            for index, value in (
                (q, kept_own[level, side, k]), (1 - q, kept_pair[level, side, k])
            ):
                high, low = split_two(value)
                to = pl.ds(pl.multiple_of(index * LANES, LANES), LANES)
                kept_row_high[side, to, lanes] = high
                kept_row_low[side, to, lanes] = low

        def kept_products(lanes):
            value = None
            for side in range(2):
                term = dot_three(
                    kept_row_high[side, :, lanes], kept_row_low[side, :, lanes],
                    kept_col_high[side, :, lanes], kept_col_low[side, :, lanes],
                )
                value = term if value is None else value + term
            return value

        for level in range(2):
            def kept_step(k, carry):
                def take(side):
                    arrived(kept_own.at[level, side, k], orecv.at[level, side, k])
                    spread(
                        kept_own.at[level, side, k], kept_peer.at[level, side], level, side, k,
                        lambda copy: copy.start(),
                    )
                    kept_pair_copy(level, side, k).start()
                    kept_peer[level, side, y, k] = kept_own[level, side, k]

                each_side(take)

                @pl.when(k >= 1)
                def _():
                    each_side(lambda side: kept_pass(level, side, k - 1))

                @pl.when(k >= 2)
                def _():
                    each_side(lambda side: kept_collect(level, side, k - 2))

                return carry

            lax.fori_loop(0, count, kept_step, 0)
            each_side(lambda side: kept_collect(level, side, count - 2))
            partial_sum = kept_products(slice(0, early))
            if level == 0:
                kept_acc[...] = partial_sum
            else:
                kept_acc[...] = kept_acc[...] + partial_sum
            each_side(lambda side: kept_pass(level, side, count - 1))
            each_side(lambda side: kept_collect(level, side, count - 1))
            kept_acc[...] = kept_acc[...] + kept_products(slice(early, nodes))

        def swap_copy():
            return remote(swap_src, swap_dst, ssend, srecv, t, sibling)

        other_rows = pl.ds(pl.multiple_of((1 - q) * LANES, LANES), LANES)
        for m in range(chips):
            swap_src[m] = kept_acc[other_rows, m * LANES : (m + 1) * LANES]
        swap_copy().start()
        my_rows = pl.ds(pl.multiple_of(q * LANES, LANES), LANES)
        for m in range(chips):
            lanes = lanes_of(2 * m + q)
            factor_out[0, :, lanes] = (
                diag[0, :, lanes] - kept_acc[my_rows, m * LANES : (m + 1) * LANES]
            )

        for level in range(2):
            each_side(lambda side: arrived(tbuf.at[level, side], trecv.at[level, side]))
        arrow_out[0] = arrow[0] + (
            (tbuf[0, 0] + tbuf[0, 1]) + (tbuf[1, 0] + tbuf[1, 1])
        ).T
        arrived(swap_dst, srecv)
        for m in range(chips):
            lanes = lanes_of(2 * m + 1 - q)
            factor_out[0, :, lanes] = diag[0, :, lanes] - swap_dst[m]
        for k in range(count):
            lanes = slice(k * LANES, (k + 1) * LANES)
            arrived(fbuf.at[1, k], frecv.at[1, k])
            link_out[0, 1, :, lanes] = fbuf[1, k]

            @pl.when(t > 0)
            def _():
                arrived(fbuf.at[0, k], frecv.at[0, k])

            link_out[0, 0, :, lanes] = fbuf[0, k]

        swap_copy().wait_send()

        def kept_drain(k, carry):
            def wait_all(side):
                for level in range(2):
                    spread(
                        kept_own.at[level, side, k], kept_peer.at[level, side], level, side, k,
                        lambda copy: copy.wait_send(),
                    )
                    relay(
                        kept_peer.at[level, side], level, side, k,
                        lambda copy: copy.wait_send(),
                    )
                    kept_pair_copy(level, side, k).wait_send()

            each_side(wait_all)
            return carry

        lax.fori_loop(0, count, kept_drain, 0)

    @pl.when(odd == 0)
    def _():
        for k in range(count):
            coupling_copy(k).wait_send()

    total = tip[...]
    for index in range(blocks // 4):
        @pl.when(t != 4 * index + 2)
        def _():
            arrived(tipbuf.at[index], brecv.at[index])

        part = tipbuf[index]
        total = total + jnp.concatenate([part[:, :tip_rows], part[:, tip_rows:]], 0)
    tip_out[...] = total


def body(diagonal, coupling, arrowhead, tip_matrix):
    cols = lax.axis_size("col")
    blocks = lax.axis_size("tm")
    chips = cols // 2
    nodes = diagonal.shape[2]
    tip_rows = tip_matrix.shape[0]
    total = nodes + 2 * LANES + tip_rows
    count = nodes // LANES
    half = chips * LANES
    f32, bf16, dma = jnp.float32, jnp.bfloat16, pltpu.SemaphoreType.DMA
    tile = (LANES, LANES)
    scratch = [
        pltpu.VMEM((count, total, LANES), f32),
        pltpu.VMEM((count, nodes, LANES), f32),
        pltpu.VMEM((2, count) + tile, f32),
        pltpu.VMEM((2, count) + tile, f32),
        pltpu.VMEM((2, chips, count) + tile, f32),
        pltpu.VMEM((2, count, 2 * LANES, LANES), f32),
        pltpu.VMEM((count, 2 * LANES, LANES), f32),
        pltpu.VMEM((3, 2, chips) + tile, f32),
        pltpu.VMEM((2, 2 * LANES, half), f32),
        pltpu.VMEM((2, 2, chips, count) + tile, f32),
        pltpu.VMEM((2, 2, count) + tile, f32),
        pltpu.VMEM((2, 2, count) + tile, f32),
        pltpu.VMEM((2 * LANES, half), f32),
        pltpu.VMEM((chips,) + tile, f32),
        pltpu.VMEM((chips,) + tile, f32),
        pltpu.VMEM((cols, tip_rows, LANES), f32),
        pltpu.VMEM((2, 2, tip_rows, LANES), f32),
        pltpu.VMEM((2, tip_rows, LANES), f32),
        pltpu.VMEM((2, tip_rows // 2, LANES), f32),
        pltpu.VMEM((tip_rows // 2, LANES), f32),
        pltpu.VMEM((blocks // 4, tip_rows // 2, LANES), f32),
        pltpu.VMEM((LANES, 2 * LANES), f32),
        pltpu.VMEM((total, 3 * LANES), bf16),
        pltpu.VMEM((nodes, 3 * LANES), bf16),
        pltpu.VMEM((4 * LANES, nodes), bf16),
        pltpu.VMEM((4 * LANES, nodes), bf16),
        pltpu.VMEM((half, nodes), bf16),
        pltpu.VMEM((half, nodes), bf16),
        pltpu.VMEM((2, 2 * LANES, nodes), bf16),
        pltpu.VMEM((2, 2 * LANES, nodes), bf16),
        pltpu.VMEM((2, half, nodes), bf16),
        pltpu.VMEM((2, half, nodes), bf16),
        dma((7, count)),
        dma((cols, count)),
        dma((cols,)),
        dma((cols,)),
        dma((2, 2, 4, count)),
        dma((2, 2, chips + 1, count)),
        dma((2, 2, count)),
        dma((count,)),
        dma((2, count)),
        dma((3, 2, chips)),
        dma((2, count)),
        dma((2,)),
        dma((2, 2)),
        dma,
        dma((2,)),
        dma((blocks,)),
        dma((blocks // 4,)),
        dma,
        dma,
    ]

    def call(*refs):
        kernel(chips, tip_rows, blocks, *refs)

    return pl.pallas_call(
        call,
        out_shape=(
            jax.ShapeDtypeStruct(diagonal.shape, f32),
            jax.ShapeDtypeStruct((1, 2) + diagonal.shape[1:], f32),
            jax.ShapeDtypeStruct(arrowhead.shape, f32),
            jax.ShapeDtypeStruct(tip_matrix.shape, f32),
        ),
        in_specs=[pl.BlockSpec(memory_space=pltpu.VMEM)] * 4,
        out_specs=(pl.BlockSpec(memory_space=pltpu.VMEM),) * 4,
        scratch_shapes=scratch,
        compiler_params=pltpu.CompilerParams(
            collective_id=0, has_side_effects=True, vmem_limit_bytes=60 * 1024 * 1024
        ),
        name="cyclic_reduction",
    )(diagonal, coupling, arrowhead, tip_matrix)


def solution(mesh):
    in_specs = (P("tm", "col", None), P("tm", "col", None), P("tm", "col", None), P())
    out_specs = (P("tm", "col", None), P("tm", None, "col", None), P("tm", "col", None), P())
    return jax.shard_map(body, mesh=mesh, in_specs=in_specs, out_specs=out_specs, check_vma=False)
```

```python
import jax
import jax.numpy as jnp
from jax import lax
from jax.experimental import pallas as pl
from jax.experimental.pallas import tpu as pltpu
from jax.sharding import PartitionSpec as P

LANES = 128
PANEL = 16


def split_two(value):
    high = value.astype(jnp.bfloat16)
    low = (value - high.astype(jnp.float32)).astype(jnp.bfloat16)
    return high, low


def split_three(value):
    high = value.astype(jnp.bfloat16)
    rest = value - high.astype(jnp.float32)
    middle = rest.astype(jnp.bfloat16)
    low = (rest - middle.astype(jnp.float32)).astype(jnp.bfloat16)
    return high, middle, low


def spread_row(vec, row):
    return jnp.broadcast_to(vec[row : row + 1, :], (8, LANES))


def spread_lane(vec, lane):
    return jnp.take_along_axis(vec, jnp.full(vec.shape, lane, jnp.int32), axis=1)


def factor_tile(work, fill=lambda panel: None):
    sub = lax.broadcasted_iota(jnp.int32, (8, LANES), 0)
    for panel in range(LANES // PANEL):
        first = panel * PANEL
        left = [work[first : first + 8, :LANES], work[first + 8 : first + 16, :LANES]]
        right = [work[first : first + 8, LANES:], work[first + 8 : first + 16, LANES:]]
        cols = [
            [spread_lane(left[h], first + c) if h >= c // 8 else None for h in range(2)]
            for c in range(PANEL)
        ]
        pivots = [None, None]
        for r in range(PANEL):
            h, q = r // 8, r % 8
            pivot = spread_row(cols[r][h], q)
            pivots[h] = pivot if q == 0 else jnp.where(sub == q, pivot, pivots[h])
            if r == PANEL - 1:
                break
            inverse = 1.0 / pivot
            coef, masked = [None, None], [None, None]
            for g in range(h, 2):
                coef[g] = cols[r][g] * inverse
                masked[g] = jnp.where(sub > q, coef[g], 0.0) if g == h else coef[g]
            for c in range(r + 1, PANEL):
                entry = spread_row(cols[r][c // 8], c % 8)
                for g in range(c // 8, 2):
                    cols[c][g] = cols[c][g] - coef[g] * entry
            left_row, right_row = spread_row(left[h], q), spread_row(right[h], q)
            for g in range(h, 2):
                if g == h and q == 7:
                    continue
                left[g] = left[g] - masked[g] * left_row
                right[g] = right[g] - masked[g] * right_row
        fill(panel)
        rows = []
        for h in range(2):
            scale = lax.rsqrt(pivots[h])
            rows.append(jnp.concatenate([left[h] * scale, right[h] * scale], 1))
        rows = jnp.concatenate(rows, 0)
        work[first : first + PANEL, :] = rows
        if first + PANEL < LANES:
            a, b, c = split_three(rows)
            lhs = jnp.concatenate([a, a, b, a, b, c], 0)[:, :LANES]
            rhs = jnp.concatenate([a, b, a, c, b, a], 0)
            update = lax.dot_general(
                lhs, rhs, (((0,), (0,)), ((), ())), preferred_element_type=jnp.float32
            )
            n = first + PANEL
            work[n:, :] = work[n:, :] - update[n:, :]


def dot_nt(left, right):
    return lax.dot_general(
        left, right, (((1,), (1,)), ((), ())), preferred_element_type=jnp.float32
    )


def wide_left(value):
    high, low = split_two(value)
    return jnp.concatenate([high, high, low], 1)


def wide_right(value):
    high, low = split_two(value)
    return jnp.concatenate([high, low, high], 1)


def prepare_step(k, start, work):
    row_id = lax.broadcasted_iota(jnp.int32, (LANES, LANES), 0)
    col_id = lax.broadcasted_iota(jnp.int32, (LANES, LANES), 1)
    work[:, :LANES] = start
    work[:, LANES:] = jnp.where(row_id == col_id, 1.0, 0.0)


def factor_and_update(acc, work, lhs, rhs):
    count, total, _ = acc.shape

    def fill(panel):
        pair, part = panel // 2, panel % 2
        if pair >= count // 2:
            return
        top = 2 * LANES * pair
        middle = top + (total - top) // 32 * 16
        rows = slice(top, middle) if part == 0 else slice(middle, total)
        update = dot_nt(lhs[rows, :], rhs[top : top + 2 * LANES, :])
        acc[2 * pair, rows, :] = acc[2 * pair, rows, :] - update[:, :LANES]
        acc[2 * pair + 1, rows, :] = acc[2 * pair + 1, rows, :] - update[:, LANES:]

    factor_tile(work, fill)


def solve_panel(k, column, done, work, lhs, rhs, nodes):
    total = column.shape[0]
    row_id = lax.broadcasted_iota(jnp.int32, (LANES, LANES), 0)
    col_id = lax.broadcasted_iota(jnp.int32, (LANES, LANES), 1)
    here = pl.ds(pl.multiple_of(k * LANES, LANES), LANES)
    solved = dot_nt(wide_left(column), wide_right(work[:, LANES:]))
    rows = lax.broadcasted_iota(jnp.int32, (total, LANES), 0)
    solved = jnp.where(rows >= (k + 1) * LANES, solved, 0.0)
    done[k] = solved
    done[k, here, :] = jnp.where(row_id <= col_id, work[:, :LANES], 0.0).T
    high, low = split_two(solved)
    lhs[...] = jnp.concatenate([high, high, low], 1)
    rhs[...] = jnp.concatenate([high[:nodes], low[:nodes], high[:nodes]], 1)


MESH = pl.DeviceIdType.MESH


def dot_three(left_high, left_low, right_high, right_low):
    value = dot_nt(left_high, right_high)
    value = value + dot_nt(left_high, right_low)
    return value + dot_nt(left_low, right_high)


def kernel(
    chips, tip_rows, blocks,
    diag, coup, arrow, tip,
    factor_out, link_out, arrow_out, tip_out,
    done, accum, dbuf, fbuf, nbuf, peer, pair, stream, gsrc, acc, kept_peer, kept_pair, kept_own,
    kept_acc, swap_src, swap_dst, abuf, tbuf, tsrc, zbuf, zsrc, tipbuf,
    work, lhs, rhs, row_high, row_low, col_high, col_low,
    kept_row_high, kept_row_low, kept_col_high, kept_col_low,
    dsend, drecv, asend, arecv, psend, precv, orecv, csend, frecv, gsend, nrecv,
    tsend, trecv, zsend, zrecv, bsend, brecv, ssend, srecv,
):
    t = lax.axis_index("tm")
    c = lax.axis_index("col")
    y, q = lax.div(c, 2), lax.rem(c, 2)
    sibling = c + 1 - 2 * q
    cols = 2 * chips
    count = cols
    nodes = count * LANES
    link_top, tip_top = nodes, nodes + 2 * LANES
    phase = lax.rem(t, 4)
    odd = lax.rem(t, 2)
    second = 1 - odd
    step_size = 2 - odd
    is_second = phase == 2
    last = blocks - 1
    early = nodes - LANES
    toward_next, toward_kept = t + 2 - phase, t - 2 + phase
    turn = lax.div(phase, 2)
    gather_at = pl.multiple_of(LANES * (1 - turn), LANES)
    stream_at = pl.multiple_of(LANES * turn, LANES)
    kept_exists = toward_kept <= last
    helps = (odd == 1) & kept_exists
    own_rows = pl.ds(pl.multiple_of(c * LANES, LANES), LANES)

    def remote(src, dst, send, recv, tm, col):
        return pltpu.make_async_remote_copy(
            src_ref=src, dst_ref=dst, send_sem=send, recv_sem=recv,
            device_id={"tm": tm, "col": col}, device_id_type=MESH,
        )

    def arrived(dst, recv):
        remote(dst, dst, recv, recv, t, sibling).wait_recv()

    barrier = pltpu.get_barrier_semaphore()

    def greet(tm, col):
        pl.semaphore_signal(
            barrier, inc=1, device_id={"tm": tm, "col": col}, device_id_type=MESH
        )

    for other in range(1, cols):
        greet(t, lax.rem(c + other, cols))
    for other in range(1, blocks):
        greet(lax.rem(t + other, blocks), c)
    for other in (1, blocks - 1):
        greet(lax.rem(t + other, blocks), sibling)
    for k in range(count):
        accum[k] = jnp.zeros(accum.shape[1:], jnp.float32)
    lhs[...] = jnp.zeros(lhs.shape, jnp.bfloat16)
    rhs[...] = jnp.zeros(rhs.shape, jnp.bfloat16)
    pl.semaphore_wait(barrier, cols - 1 + blocks - 1 + 2)

    def coupling_copy(k):
        return remote(
            coup.at[0, :, pl.ds(k * LANES, LANES)], fbuf.at[0, k],
            csend.at[k], frecv.at[0, k], t + 1, c,
        )

    @pl.when(odd == 0)
    def _():
        for k in range(count):
            coupling_copy(k).start()

    def peer_of(other):
        return lax.rem(c + other, cols)

    def same_core(other):
        return 2 * lax.rem(y + other, chips) + q

    hops = [1, chips - 1] if chips > 2 else list(range(1, chips))
    rings = chips == 4

    def relay_ends(k):
        turn_at = 1 - 2 * lax.rem(y + k, 2)
        return lax.rem(y + turn_at + chips, chips), lax.rem(y - turn_at + chips, chips)

    def tile_copy(src_col, k, slot, target):
        place = dbuf.at[k, pl.ds(pl.multiple_of(src_col * LANES, LANES), LANES)]
        return remote(place, place, dsend.at[slot, k], drecv.at[src_col, k], t, target)

    def tile_arrived(src_col, k):
        place = dbuf.at[k, pl.ds(pl.multiple_of(src_col * LANES, LANES), LANES)]
        arrived(place, drecv.at[src_col, k])

    def own_tile_copies(k, action):
        @pl.when(c == k)
        def _():
            for other in range(1, cols):
                action(tile_copy(c, k, other - 1, peer_of(other)))

        @pl.when(c > k)
        def _():
            action(tile_copy(c, k, 0, sibling))
            for i, hop in enumerate(hops):
                action(tile_copy(c, k, 1 + i, same_core(hop)))

    def near_forwards(k, action):
        for i, hop in enumerate(hops):
            src = same_core(hop)

            @pl.when(src > k)
            def _():
                action(src, tile_copy(src, k, 7 + i, sibling))

    def ring_forward(k, action):
        if rings:
            source, target = relay_ends(k)
            src = 2 * source + q

            @pl.when(src > k)
            def _():
                action(tile_copy(src, k, 10, 2 * target + q))

    def opposite_forward(k, action):
        if rings:
            src = same_core(2)

            @pl.when(src > k)
            def _():
                action(src, tile_copy(src, k, 9, sibling))

    def pass_on(src, k, copy):
        tile_arrived(src, k)
        copy.start()

    def relay_near(k):
        near_forwards(k, lambda src, copy: pass_on(src, k, copy))
        ring_forward(k, lambda copy: copy.start())

    def relay_opposite(k):
        opposite_forward(k, lambda src, copy: pass_on(src, k, copy))

    def arrow_copy(other):
        return remote(
            abuf.at[c], abuf.at[c], asend.at[other], arecv.at[c], t, peer_of(other)
        )

    def own_links(level, k):
        return done.at[k, pl.ds(link_top, 2 * LANES)] if level == 0 else stream.at[k]

    def own_side(level, k, at):
        if level == 0:
            return done.at[k, pl.ds(pl.multiple_of(link_top + at, LANES), LANES)]
        return stream.at[k, pl.ds(at, LANES)]

    def spread(src, place, level, side, k, action):
        for i, hop in enumerate(hops):
            action(remote(
                src, place.at[y, k], psend.at[level, side, 1 + i, k],
                precv.at[level, side, y, k], t, same_core(hop),
            ))
        if rings:
            @pl.when(k == count - 1)
            def _():
                action(remote(
                    src, place.at[y, k], psend.at[level, side, 3, k],
                    precv.at[level, side, y, k], t, same_core(2),
                ))

    def relay(place, level, side, k, action):
        if rings:
            @pl.when(k < count - 1)
            def _():
                source, target = relay_ends(k)
                tile = place.at[source, k]
                action(remote(
                    tile, tile, psend.at[level, side, 3, k],
                    precv.at[level, side, source, k], t, 2 * target + q,
                ))

    def relay_when_here(place, level, side, k):
        for hop in hops:
            slot = lax.rem(y + hop, chips)
            arrived(place.at[slot, k], precv.at[level, side, slot, k])
        relay(place, level, side, k, lambda copy: copy.start())

    def opposite_arrived(place, level, side, k):
        if rings:
            slot = lax.rem(y + 2, chips)
            arrived(place.at[slot, k], precv.at[level, side, slot, k])

    def pair_copy(level, k):
        return remote(
            own_links(level, k), pair.at[level, k],
            psend.at[level, 0, 0, k], precv.at[level, 0, chips, k], t, sibling,
        )

    def kept_copy(level, k):
        return remote(
            own_side(level, k, stream_at), kept_own.at[level, turn, k],
            psend.at[level, 1, 0, k], orecv.at[level, turn, k], toward_kept, c,
        )

    def helper_copy(k, side):
        return remote(
            done.at[k, pl.ds(link_top, 2 * LANES)], stream.at[k],
            psend.at[0, 0, side, k], orecv.at[1, 0, k], t - 1 + 2 * side, c,
        )

    def each_second(k, action):
        for side in range(2):
            @pl.when(t + 2 * side <= last)
            def _():
                action(helper_copy(k, side))

    def kept_pair_copy(level, side, k):
        return remote(
            kept_own.at[level, side, k], kept_pair.at[level, side, k],
            psend.at[level, side, 0, k], precv.at[level, side, chips, k], t, sibling,
        )

    def near_wait(k):
        for side in range(2):
            arrived(nbuf.at[side, k], nrecv.at[side, k])

    def product_copy(kind, m, p):
        tile = 2 * m + q
        src, send, col = gsrc.at[kind, p, m], gsend.at[kind, p, m], 2 * y + p
        if kind == 0:
            dst, recv, tm = nbuf.at[1 - turn, tile], nrecv.at[1 - turn, tile], toward_next
        elif kind == 1:
            dst, recv, tm = fbuf.at[turn, tile], frecv.at[turn, tile], toward_next
        else:
            dst, recv, tm = fbuf.at[1 - turn, tile], frecv.at[1 - turn, tile], toward_kept
        return remote(src, dst, send, recv, tm, col)

    def tip_copy(side):
        tm = t + step_size if side else t - step_size
        return remote(
            tsrc.at[side], tbuf.at[second, side], tsend.at[side], trecv.at[second, side], tm, c
        )

    def square_copy():
        return remote(zsrc, zbuf.at[turn], zsend, zrecv.at[turn], toward_next, c)

    group = lax.div(t, 4)

    def total_copy(other):
        place = tipbuf.at[group]
        return remote(
            place, place, bsend.at[other], brecv.at[group], lax.rem(t + other, blocks), c
        )

    def lanes_of(k):
        return pl.ds(pl.multiple_of(k * LANES, LANES), LANES)

    def exchange(level, k):
        spread(
            own_side(level, k, gather_at), peer.at[level], level, 0, k, lambda copy: copy.start()
        )
        pair_copy(level, k).start()

        @pl.when(kept_exists)
        def _():
            kept_copy(level, k).start()

        peer[level, y, k] = own_side(level, k, gather_at)[...]

    def pass_links(level, k):
        relay_when_here(peer.at[level], level, 0, k)

    def exchange_done(level, k):
        spread(
            own_side(level, k, gather_at), peer.at[level], level, 0, k,
            lambda copy: copy.wait_send(),
        )
        relay(peer.at[level], level, 0, k, lambda copy: copy.wait_send())
        pair_copy(level, k).wait_send()

        @pl.when(kept_exists)
        def _():
            kept_copy(level, k).wait_send()

    def collect(level, k):
        opposite_arrived(peer.at[level], level, 0, k)
        arrived(pair.at[level, k], precv.at[level, 0, chips, k])
        lanes = lanes_of(k)
        for slot in range(chips):
            high, low = split_two(peer[level, slot, k])
            to = slice(slot * LANES, (slot + 1) * LANES)
            col_high[to, lanes] = high
            col_low[to, lanes] = low
        for place, at in ((0, stream_at), (1, gather_at)):
            for index, value in (
                (q, own_side(level, k, at)[...]),
                (1 - q, pair[level, k, pl.ds(at, LANES), :]),
            ):
                high, low = split_two(value)
                to = pl.ds(pl.multiple_of((2 * place + index) * LANES, LANES), LANES)
                row_high[to, lanes] = high
                row_low[to, lanes] = low

    def kinds_of(level):
        near, far = slice(2 * LANES, 4 * LANES), slice(0, 2 * LANES)
        return ((0, near), (1, far)) if level == 0 else ((2, far),)

    def products_begin(level):
        collect(level, count - 2)
        for kind, rows in kinds_of(level):
            acc[min(kind, 1)] = dot_three(
                row_high[rows, :early], row_low[rows, :early],
                col_high[:, :early], col_low[:, :early],
            )

    def products_end(level):
        pass_links(level, count - 1)
        collect(level, count - 1)
        for kind, rows in kinds_of(level):
            value = acc[min(kind, 1)] + dot_three(
                row_high[rows, early:], row_low[rows, early:],
                col_high[:, early:], col_low[:, early:],
            )
            for m in range(chips):
                for p in range(2):
                    gsrc[kind, p, m] = -value[
                        p * LANES : (p + 1) * LANES, m * LANES : (m + 1) * LANES
                    ]
        for m in range(chips):
            for kind, rows in kinds_of(level):
                for p in range(2):
                    product_copy(kind, m, p).start()

    @pl.when(phase != 0)
    def _():
        @pl.when(odd == 1)
        def _():
            keep = jnp.where(t < last, 1.0, 0.0)
            for k in range(count):
                fbuf[1, k] = coup[0, :, k * LANES : (k + 1) * LANES] * keep

        def send_arrow():
            abuf[c] = arrow[0].T

            @pl.when(is_second)
            def _():
                for side in range(2):
                    arrived(tbuf.at[0, side], trecv.at[0, side])
                abuf[c] = abuf[c] + (tbuf[0, 0] + tbuf[0, 1])

            for other in range(1, cols):
                arrow_copy(other).start()

        def send_tile(k):
            dbuf[k, own_rows, :] = diag[0, :, lanes_of(k)]

            @pl.when(is_second)
            def _():
                near_wait(k)
                dbuf[k, own_rows, :] = dbuf[k, own_rows, :] + (nbuf[0, k] + nbuf[1, k])

            own_tile_copies(k, lambda copy: copy.start())

        send_tile(0)

        @pl.when(c >= 1)
        def _():
            send_tile(1)

        @pl.when(odd == 1)
        def _():
            send_arrow()

        relay_near(0)

        def step(k, carry):
            here = lanes_of(k)

            @pl.when(k + 1 < count)
            def _():
                relay_near(k + 1)

            @pl.when(k != c)
            def _():
                tile_arrived(k, k)

            start = dbuf[k, here, :] + accum[k, here, :]
            prepare_step(k, start - dot_nt(lhs[here, :], rhs[here, :]), work)
            factor_and_update(accum, work, lhs, rhs)

            @pl.when(k == 0)
            def _():
                relay_opposite(0)

                @pl.when(c >= 2)
                def _():
                    send_tile(2)

            @pl.when(k + 1 < count)
            def _():
                relay_opposite(k + 1)

            @pl.when(k + 3 <= c)
            def _():
                send_tile(k + 3)

            @pl.when((k == 0) & is_second)
            def _():
                send_arrow()

            for chip in range(chips):
                src = 2 * chip + 1 - q

                @pl.when(src > k)
                def _():
                    tile_arrived(src, k)

            @pl.when(k != c)
            def _():
                arrived(abuf.at[k], arecv.at[k])

            arrived(fbuf.at[0, k], frecv.at[0, k])

            @pl.when(is_second)
            def _():
                arrived(fbuf.at[1, k], frecv.at[1, k])

            source = jnp.concatenate([dbuf[k], fbuf[0, k], fbuf[1, k], abuf[k]], 0)
            solve_panel(k, accum[k] + source, done, work, lhs, rhs, nodes)

            def send_links():
                @pl.when(odd == 1)
                def _():
                    exchange(0, k)

                @pl.when(is_second)
                def _():
                    each_second(k, lambda copy: copy.start())

            send_links()

            @pl.when((k >= 1) & (odd == 1))
            def _():
                pass_links(0, k - 1)

            @pl.when((k >= 2) & (odd == 1))
            def _():
                collect(0, k - 2)

            return carry

        lax.fori_loop(0, count, step, 0)

        @pl.when(odd == 1)
        def _():
            products_begin(0)

        terms = jnp.zeros((tip_rows, 2 * LANES + tip_rows), jnp.float32)
        for k in range(count):
            terms = terms - dot_nt(
                wide_left(done[k, tip_top:, :]), wide_right(done[k, link_top:, :])
            )
        tsrc[0] = terms[:, :LANES]
        tsrc[1] = terms[:, LANES : 2 * LANES]
        square = jnp.concatenate(
            [terms[: tip_rows // 2, 2 * LANES :], terms[tip_rows // 2 :, 2 * LANES :]], 1
        )
        tip_copy(0).start()

        @pl.when(t + step_size <= last)
        def _():
            tip_copy(1).start()

        @pl.when(odd == 1)
        def _():
            zsrc[...] = square
            square_copy().start()
            products_end(0)

        @pl.when(is_second)
        def _():
            for slot in range(2):
                arrived(zbuf.at[slot], zrecv.at[slot])
            tipbuf[group] = square + (zbuf[0] + zbuf[1])
            for other in range(1, blocks):
                total_copy(other).start()

        for k in range(count):
            lanes = slice(k * LANES, (k + 1) * LANES)
            factor_out[0, :, lanes] = done[k, own_rows, :]
            for side in range(2):
                part = slice(link_top + side * LANES, link_top + (side + 1) * LANES)
                link_out[0, side, :, lanes] = done[k, part, :]
        arrow_out[0] = done[c, tip_top:, :].T

        @pl.when(helps)
        def _():
            def help_step(k, carry):
                arrived(stream.at[k], orecv.at[1, 0, k])
                exchange(1, k)

                @pl.when(k >= 1)
                def _():
                    pass_links(1, k - 1)

                @pl.when(k >= 2)
                def _():
                    collect(1, k - 2)

                return carry

            lax.fori_loop(0, count, help_step, 0)
            products_begin(1)
            products_end(1)

        def drain(k, carry):
            own_tile_copies(k, lambda copy: copy.wait_send())
            near_forwards(k, lambda src, copy: copy.wait_send())
            ring_forward(k, lambda copy: copy.wait_send())
            opposite_forward(k, lambda src, copy: copy.wait_send())

            @pl.when((k > c) & is_second)
            def _():
                near_wait(k)

            @pl.when(is_second)
            def _():
                each_second(k, lambda copy: copy.wait_send())

            @pl.when(odd == 1)
            def _():
                exchange_done(0, k)

            @pl.when(helps)
            def _():
                exchange_done(1, k)

            return carry

        lax.fori_loop(0, count, drain, 0)
        for other in range(1, cols):
            arrow_copy(other).wait_send()
        tip_copy(0).wait_send()

        @pl.when(t + step_size <= last)
        def _():
            tip_copy(1).wait_send()

        @pl.when(odd == 1)
        def _():
            square_copy().wait_send()
            for kind in range(2):
                for m in range(chips):
                    for p in range(2):
                        product_copy(kind, m, p).wait_send()

        @pl.when(helps)
        def _():
            for m in range(chips):
                for p in range(2):
                    product_copy(2, m, p).wait_send()

        @pl.when(is_second)
        def _():
            for other in range(1, blocks):
                total_copy(other).wait_send()

    @pl.when(phase == 0)
    def _():
        @pl.when(t == 0)
        def _():
            for level in range(2):
                tbuf[level, 1] = jnp.zeros(tbuf.shape[2:], jnp.float32)
            fbuf[0] = jnp.zeros(fbuf.shape[1:], jnp.float32)
            for ref in (kept_row_high, kept_row_low, kept_col_high, kept_col_low):
                ref[1] = jnp.zeros(ref.shape[1:], jnp.bfloat16)

        def each_side(action):
            action(0)

            @pl.when(t > 0)
            def _():
                action(1)

        def kept_pass(level, side, k):
            relay_when_here(kept_peer.at[level, side], level, side, k)

        def kept_collect(level, side, k):
            opposite_arrived(kept_peer.at[level, side], level, side, k)
            arrived(kept_pair.at[level, side, k], precv.at[level, side, chips, k])
            lanes = lanes_of(k)
            for slot in range(chips):
                high, low = split_two(kept_peer[level, side, slot, k])
                to = slice(slot * LANES, (slot + 1) * LANES)
                kept_col_high[side, to, lanes] = high
                kept_col_low[side, to, lanes] = low
            for index, value in (
                (q, kept_own[level, side, k]), (1 - q, kept_pair[level, side, k])
            ):
                high, low = split_two(value)
                to = pl.ds(pl.multiple_of(index * LANES, LANES), LANES)
                kept_row_high[side, to, lanes] = high
                kept_row_low[side, to, lanes] = low

        def kept_products(lanes):
            value = None
            for side in range(2):
                term = dot_three(
                    kept_row_high[side, :, lanes], kept_row_low[side, :, lanes],
                    kept_col_high[side, :, lanes], kept_col_low[side, :, lanes],
                )
                value = term if value is None else value + term
            return value

        for level in range(2):
            def kept_step(k, carry):
                def take(side):
                    arrived(kept_own.at[level, side, k], orecv.at[level, side, k])
                    spread(
                        kept_own.at[level, side, k], kept_peer.at[level, side], level, side, k,
                        lambda copy: copy.start(),
                    )
                    kept_pair_copy(level, side, k).start()
                    kept_peer[level, side, y, k] = kept_own[level, side, k]

                each_side(take)

                @pl.when(k >= 1)
                def _():
                    each_side(lambda side: kept_pass(level, side, k - 1))

                @pl.when(k >= 2)
                def _():
                    each_side(lambda side: kept_collect(level, side, k - 2))

                return carry

            lax.fori_loop(0, count, kept_step, 0)
            each_side(lambda side: kept_collect(level, side, count - 2))
            partial_sum = kept_products(slice(0, early))
            if level == 0:
                kept_acc[...] = partial_sum
            else:
                kept_acc[...] = kept_acc[...] + partial_sum
            each_side(lambda side: kept_pass(level, side, count - 1))
            each_side(lambda side: kept_collect(level, side, count - 1))
            kept_acc[...] = kept_acc[...] + kept_products(slice(early, nodes))

        def swap_copy():
            return remote(swap_src, swap_dst, ssend, srecv, t, sibling)

        other_rows = pl.ds(pl.multiple_of((1 - q) * LANES, LANES), LANES)
        for m in range(chips):
            swap_src[m] = kept_acc[other_rows, m * LANES : (m + 1) * LANES]
        swap_copy().start()
        my_rows = pl.ds(pl.multiple_of(q * LANES, LANES), LANES)
        for m in range(chips):
            lanes = lanes_of(2 * m + q)
            factor_out[0, :, lanes] = (
                diag[0, :, lanes] - kept_acc[my_rows, m * LANES : (m + 1) * LANES]
            )

        for level in range(2):
            each_side(lambda side: arrived(tbuf.at[level, side], trecv.at[level, side]))
        arrow_out[0] = arrow[0] + (
            (tbuf[0, 0] + tbuf[0, 1]) + (tbuf[1, 0] + tbuf[1, 1])
        ).T
        arrived(swap_dst, srecv)
        for m in range(chips):
            lanes = lanes_of(2 * m + 1 - q)
            factor_out[0, :, lanes] = diag[0, :, lanes] - swap_dst[m]
        for k in range(count):
            lanes = slice(k * LANES, (k + 1) * LANES)
            arrived(fbuf.at[1, k], frecv.at[1, k])
            link_out[0, 1, :, lanes] = fbuf[1, k]

            @pl.when(t > 0)
            def _():
                arrived(fbuf.at[0, k], frecv.at[0, k])

            link_out[0, 0, :, lanes] = fbuf[0, k]

        swap_copy().wait_send()

        def kept_drain(k, carry):
            def wait_all(side):
                for level in range(2):
                    spread(
                        kept_own.at[level, side, k], kept_peer.at[level, side], level, side, k,
                        lambda copy: copy.wait_send(),
                    )
                    relay(
                        kept_peer.at[level, side], level, side, k,
                        lambda copy: copy.wait_send(),
                    )
                    kept_pair_copy(level, side, k).wait_send()

            each_side(wait_all)
            return carry

        lax.fori_loop(0, count, kept_drain, 0)

    @pl.when(odd == 0)
    def _():
        for k in range(count):
            coupling_copy(k).wait_send()

    total = tip[...]
    for index in range(blocks // 4):
        @pl.when(t != 4 * index + 2)
        def _():
            arrived(tipbuf.at[index], brecv.at[index])

        part = tipbuf[index]
        total = total + jnp.concatenate([part[:, :tip_rows], part[:, tip_rows:]], 0)
    tip_out[...] = total


def body(diagonal, coupling, arrowhead, tip_matrix):
    cols = lax.axis_size("col")
    blocks = lax.axis_size("tm")
    chips = cols // 2
    nodes = diagonal.shape[2]
    tip_rows = tip_matrix.shape[0]
    total = nodes + 2 * LANES + tip_rows
    count = nodes // LANES
    half = chips * LANES
    f32, bf16, dma = jnp.float32, jnp.bfloat16, pltpu.SemaphoreType.DMA
    tile = (LANES, LANES)
    scratch = [
        pltpu.VMEM((count, total, LANES), f32),
        pltpu.VMEM((count, total, LANES), f32),
        pltpu.VMEM((count, nodes, LANES), f32),
        pltpu.VMEM((2, count) + tile, f32),
        pltpu.VMEM((2, count) + tile, f32),
        pltpu.VMEM((2, chips, count) + tile, f32),
        pltpu.VMEM((2, count, 2 * LANES, LANES), f32),
        pltpu.VMEM((count, 2 * LANES, LANES), f32),
        pltpu.VMEM((3, 2, chips) + tile, f32),
        pltpu.VMEM((2, 2 * LANES, half), f32),
        pltpu.VMEM((2, 2, chips, count) + tile, f32),
        pltpu.VMEM((2, 2, count) + tile, f32),
        pltpu.VMEM((2, 2, count) + tile, f32),
        pltpu.VMEM((2 * LANES, half), f32),
        pltpu.VMEM((chips,) + tile, f32),
        pltpu.VMEM((chips,) + tile, f32),
        pltpu.VMEM((cols, tip_rows, LANES), f32),
        pltpu.VMEM((2, 2, tip_rows, LANES), f32),
        pltpu.VMEM((2, tip_rows, LANES), f32),
        pltpu.VMEM((2, tip_rows // 2, LANES), f32),
        pltpu.VMEM((tip_rows // 2, LANES), f32),
        pltpu.VMEM((blocks // 4, tip_rows // 2, LANES), f32),
        pltpu.VMEM((LANES, 2 * LANES), f32),
        pltpu.VMEM((total, 3 * LANES), bf16),
        pltpu.VMEM((nodes, 3 * LANES), bf16),
        pltpu.VMEM((4 * LANES, nodes), bf16),
        pltpu.VMEM((4 * LANES, nodes), bf16),
        pltpu.VMEM((half, nodes), bf16),
        pltpu.VMEM((half, nodes), bf16),
        pltpu.VMEM((2, 2 * LANES, nodes), bf16),
        pltpu.VMEM((2, 2 * LANES, nodes), bf16),
        pltpu.VMEM((2, half, nodes), bf16),
        pltpu.VMEM((2, half, nodes), bf16),
        dma((11, count)),
        dma((cols, count)),
        dma((cols,)),
        dma((cols,)),
        dma((2, 2, 4, count)),
        dma((2, 2, chips + 1, count)),
        dma((2, 2, count)),
        dma((count,)),
        dma((2, count)),
        dma((3, 2, chips)),
        dma((2, count)),
        dma((2,)),
        dma((2, 2)),
        dma,
        dma((2,)),
        dma((blocks,)),
        dma((blocks // 4,)),
        dma,
        dma,
    ]

    def call(*refs):
        kernel(chips, tip_rows, blocks, *refs)

    return pl.pallas_call(
        call,
        out_shape=(
            jax.ShapeDtypeStruct(diagonal.shape, f32),
            jax.ShapeDtypeStruct((1, 2) + diagonal.shape[1:], f32),
            jax.ShapeDtypeStruct(arrowhead.shape, f32),
            jax.ShapeDtypeStruct(tip_matrix.shape, f32),
        ),
        in_specs=[pl.BlockSpec(memory_space=pltpu.VMEM)] * 4,
        out_specs=(pl.BlockSpec(memory_space=pltpu.VMEM),) * 4,
        scratch_shapes=scratch,
        compiler_params=pltpu.CompilerParams(
            collective_id=0, has_side_effects=True, vmem_limit_bytes=60 * 1024 * 1024
        ),
        name="cyclic_reduction",
    )(diagonal, coupling, arrowhead, tip_matrix)


def solution(mesh):
    in_specs = (P("tm", "col", None), P("tm", "col", None), P("tm", "col", None), P())
    out_specs = (P("tm", "col", None), P("tm", None, "col", None), P("tm", "col", None), P())
    return jax.shard_map(body, mesh=mesh, in_specs=in_specs, out_specs=out_specs, check_vma=False)
```

```python
import jax
import jax.numpy as jnp
from jax import lax
from jax.experimental import pallas as pl
from jax.experimental.pallas import tpu as pltpu
from jax.sharding import PartitionSpec as P

LANES = 128
PANEL = 32


def split_two(value):
    high = value.astype(jnp.bfloat16)
    low = (value - high.astype(jnp.float32)).astype(jnp.bfloat16)
    return high, low


def split_three(value):
    high = value.astype(jnp.bfloat16)
    rest = value - high.astype(jnp.float32)
    middle = rest.astype(jnp.bfloat16)
    low = (rest - middle.astype(jnp.float32)).astype(jnp.bfloat16)
    return high, middle, low


def spread_row(vec, row):
    return jnp.broadcast_to(vec[row : row + 1, :], (8, LANES))


def spread_lane(vec, lane):
    return jnp.take_along_axis(vec, jnp.full(vec.shape, lane, jnp.int32), axis=1)


def factor_tile(work, fill=lambda part: None):
    sub = lax.broadcasted_iota(jnp.int32, (8, LANES), 0)
    groups = PANEL // 8
    for panel in range(LANES // PANEL):
        first = panel * PANEL
        spans = [slice(first + 8 * g, first + 8 * g + 8) for g in range(groups)]
        left = [work[span, :LANES] for span in spans]
        right = [work[span, LANES:] for span in spans]
        cols = [
            [spread_lane(left[g], first + c) if g >= c // 8 else None for g in range(groups)]
            for c in range(PANEL)
        ]
        pivots = [None] * groups
        for r in range(PANEL):
            if r % 16 == 0:
                fill((first + r) // 16)
            h, q = r // 8, r % 8
            pivot = spread_row(cols[r][h], q)
            pivots[h] = pivot if q == 0 else jnp.where(sub == q, pivot, pivots[h])
            if r == PANEL - 1:
                break
            inverse = 1.0 / pivot
            coef, masked = [None] * groups, [None] * groups
            for g in range(h, groups):
                coef[g] = cols[r][g] * inverse
                masked[g] = jnp.where(sub > q, coef[g], 0.0) if g == h else coef[g]
            for c in range(r + 1, PANEL):
                entry = spread_row(cols[r][c // 8], c % 8)
                for g in range(c // 8, groups):
                    cols[c][g] = cols[c][g] - coef[g] * entry
            left_row, right_row = spread_row(left[h], q), spread_row(right[h], q)
            for g in range(h, groups):
                if g == h and q == 7:
                    continue
                left[g] = left[g] - masked[g] * left_row
                right[g] = right[g] - masked[g] * right_row
        rows = []
        for g in range(groups):
            scale = lax.rsqrt(pivots[g])
            rows.append(jnp.concatenate([left[g] * scale, right[g] * scale], 1))
        rows = jnp.concatenate(rows, 0)
        work[first : first + PANEL, :] = rows
        if first + PANEL < LANES:
            a, b, c = split_three(rows)
            lhs = jnp.concatenate([a, a, b, a, b, c], 0)[:, :LANES]
            rhs = jnp.concatenate([a, b, a, c, b, a], 0)
            update = lax.dot_general(
                lhs, rhs, (((0,), (0,)), ((), ())), preferred_element_type=jnp.float32
            )
            n = first + PANEL
            work[n:, :] = work[n:, :] - update[n:, :]


def dot_nt(left, right):
    return lax.dot_general(
        left, right, (((1,), (1,)), ((), ())), preferred_element_type=jnp.float32
    )


def wide_left(value):
    high, low = split_two(value)
    return jnp.concatenate([high, high, low], 1)


def wide_right(value):
    high, low = split_two(value)
    return jnp.concatenate([high, low, high], 1)


def prepare_step(k, start, work):
    row_id = lax.broadcasted_iota(jnp.int32, (LANES, LANES), 0)
    col_id = lax.broadcasted_iota(jnp.int32, (LANES, LANES), 1)
    work[:, :LANES] = start
    work[:, LANES:] = jnp.where(row_id == col_id, 1.0, 0.0)


def factor_and_update(acc, work, lhs, rhs):
    count, total, _ = acc.shape

    def fill(panel):
        pair, part = panel // 2, panel % 2
        if pair >= count // 2:
            return
        top = 2 * LANES * pair
        middle = top + (total - top) // 32 * 16
        rows = slice(top, middle) if part == 0 else slice(middle, total)
        update = dot_nt(lhs[rows, :], rhs[top : top + 2 * LANES, :])
        acc[2 * pair, rows, :] = acc[2 * pair, rows, :] - update[:, :LANES]
        acc[2 * pair + 1, rows, :] = acc[2 * pair + 1, rows, :] - update[:, LANES:]

    factor_tile(work, fill)


def solve_panel(k, column, done, work, lhs, rhs, nodes):
    total = column.shape[0]
    row_id = lax.broadcasted_iota(jnp.int32, (LANES, LANES), 0)
    col_id = lax.broadcasted_iota(jnp.int32, (LANES, LANES), 1)
    here = pl.ds(pl.multiple_of(k * LANES, LANES), LANES)
    solved = dot_nt(wide_left(column), wide_right(work[:, LANES:]))
    rows = lax.broadcasted_iota(jnp.int32, (total, LANES), 0)
    solved = jnp.where(rows >= (k + 1) * LANES, solved, 0.0)
    done[k] = solved
    done[k, here, :] = jnp.where(row_id <= col_id, work[:, :LANES], 0.0).T
    high, low = split_two(solved)
    lhs[...] = jnp.concatenate([high, high, low], 1)
    rhs[...] = jnp.concatenate([high[:nodes], low[:nodes], high[:nodes]], 1)


MESH = pl.DeviceIdType.MESH


def dot_three(left_high, left_low, right_high, right_low):
    value = dot_nt(left_high, right_high)
    value = value + dot_nt(left_high, right_low)
    return value + dot_nt(left_low, right_high)


def kernel(
    chips, tip_rows, blocks,
    diag, coup, arrow, tip,
    factor_out, link_out, arrow_out, tip_out,
    done, accum, dbuf, fbuf, nbuf, peer, pair, stream, gsrc, acc, kept_peer, kept_pair, kept_own,
    kept_acc, swap_src, swap_dst, abuf, tbuf, tsrc, zbuf, zsrc, tipbuf,
    work, lhs, rhs, row_high, row_low, col_high, col_low,
    kept_row_high, kept_row_low, kept_col_high, kept_col_low,
    dsend, drecv, asend, arecv, psend, precv, orecv, csend, frecv, gsend, nrecv,
    tsend, trecv, zsend, zrecv, bsend, brecv, ssend, srecv,
):
    t = lax.axis_index("tm")
    c = lax.axis_index("col")
    y, q = lax.div(c, 2), lax.rem(c, 2)
    sibling = c + 1 - 2 * q
    cols = 2 * chips
    count = cols
    nodes = count * LANES
    link_top, tip_top = nodes, nodes + 2 * LANES
    phase = lax.rem(t, 4)
    odd = lax.rem(t, 2)
    second = 1 - odd
    step_size = 2 - odd
    is_second = phase == 2
    last = blocks - 1
    early = nodes - LANES
    toward_next, toward_kept = t + 2 - phase, t - 2 + phase
    turn = lax.div(phase, 2)
    gather_at = pl.multiple_of(LANES * (1 - turn), LANES)
    stream_at = pl.multiple_of(LANES * turn, LANES)
    kept_exists = toward_kept <= last
    helps = (odd == 1) & kept_exists
    own_rows = pl.ds(pl.multiple_of(c * LANES, LANES), LANES)

    def remote(src, dst, send, recv, tm, col):
        return pltpu.make_async_remote_copy(
            src_ref=src, dst_ref=dst, send_sem=send, recv_sem=recv,
            device_id={"tm": tm, "col": col}, device_id_type=MESH,
        )

    def arrived(dst, recv):
        remote(dst, dst, recv, recv, t, sibling).wait_recv()

    barrier = pltpu.get_barrier_semaphore()

    def greet(tm, col):
        pl.semaphore_signal(
            barrier, inc=1, device_id={"tm": tm, "col": col}, device_id_type=MESH
        )

    for other in range(1, cols):
        greet(t, lax.rem(c + other, cols))
    for other in range(1, blocks):
        greet(lax.rem(t + other, blocks), c)
    for other in (1, blocks - 1):
        greet(lax.rem(t + other, blocks), sibling)
    for k in range(count):
        accum[k] = jnp.zeros(accum.shape[1:], jnp.float32)
    lhs[...] = jnp.zeros(lhs.shape, jnp.bfloat16)
    rhs[...] = jnp.zeros(rhs.shape, jnp.bfloat16)
    pl.semaphore_wait(barrier, cols - 1 + blocks - 1 + 2)

    def coupling_copy(k):
        return remote(
            coup.at[0, :, pl.ds(k * LANES, LANES)], fbuf.at[0, k],
            csend.at[k], frecv.at[0, k], t + 1, c,
        )

    @pl.when(odd == 0)
    def _():
        for k in range(count):
            coupling_copy(k).start()

    def peer_of(other):
        return lax.rem(c + other, cols)

    def same_core(other):
        return 2 * lax.rem(y + other, chips) + q

    hops = [1, chips - 1] if chips > 2 else list(range(1, chips))
    rings = chips == 4

    def relay_ends(k):
        turn_at = 1 - 2 * lax.rem(y + k, 2)
        return lax.rem(y + turn_at + chips, chips), lax.rem(y - turn_at + chips, chips)

    def tile_copy(src_col, k, slot, target):
        place = dbuf.at[k, pl.ds(pl.multiple_of(src_col * LANES, LANES), LANES)]
        return remote(place, place, dsend.at[slot, k], drecv.at[src_col, k], t, target)

    def tile_arrived(src_col, k):
        place = dbuf.at[k, pl.ds(pl.multiple_of(src_col * LANES, LANES), LANES)]
        arrived(place, drecv.at[src_col, k])

    def by_ring(src, k):
        return (src > k) | ((src == k) & (k > 0))

    def own_tile_copies(k, action):
        @pl.when((c == k) & (k == 0))
        def _():
            for other in range(1, cols):
                action(tile_copy(c, k, other - 1, peer_of(other)))

        @pl.when(by_ring(c, k))
        def _():
            action(tile_copy(c, k, 0, sibling))
            for i, hop in enumerate(hops):
                action(tile_copy(c, k, 1 + i, same_core(hop)))

    def near_forwards(k, action):
        for i, hop in enumerate(hops):
            src = same_core(hop)

            @pl.when(by_ring(src, k))
            def _():
                action(src, tile_copy(src, k, 7 + i, sibling))

    def ring_forward(k, action):
        if rings:
            source, target = relay_ends(k)
            src = 2 * source + q

            @pl.when(by_ring(src, k))
            def _():
                action(tile_copy(src, k, 10, 2 * target + q))

    def opposite_forward(k, action):
        if rings:
            src = same_core(2)

            @pl.when(by_ring(src, k))
            def _():
                action(src, tile_copy(src, k, 9, sibling))

    def pass_on(src, k, copy):
        tile_arrived(src, k)
        copy.start()

    def relay_near(k):
        near_forwards(k, lambda src, copy: pass_on(src, k, copy))
        ring_forward(k, lambda copy: copy.start())

    def relay_opposite(k):
        opposite_forward(k, lambda src, copy: pass_on(src, k, copy))

    def arrow_copy(other):
        return remote(
            abuf.at[c], abuf.at[c], asend.at[other], arecv.at[c], t, peer_of(other)
        )

    def own_links(level, k):
        return done.at[k, pl.ds(link_top, 2 * LANES)] if level == 0 else stream.at[k]

    def own_side(level, k, at):
        if level == 0:
            return done.at[k, pl.ds(pl.multiple_of(link_top + at, LANES), LANES)]
        return stream.at[k, pl.ds(at, LANES)]

    def spread(src, place, level, side, k, action):
        for i, hop in enumerate(hops):
            action(remote(
                src, place.at[y, k], psend.at[level, side, 1 + i, k],
                precv.at[level, side, y, k], t, same_core(hop),
            ))
        if rings:
            @pl.when(k == count - 1)
            def _():
                action(remote(
                    src, place.at[y, k], psend.at[level, side, 3, k],
                    precv.at[level, side, y, k], t, same_core(2),
                ))

    def relay(place, level, side, k, action):
        if rings:
            @pl.when(k < count - 1)
            def _():
                source, target = relay_ends(k)
                tile = place.at[source, k]
                action(remote(
                    tile, tile, psend.at[level, side, 3, k],
                    precv.at[level, side, source, k], t, 2 * target + q,
                ))

    def relay_when_here(place, level, side, k):
        for hop in hops:
            slot = lax.rem(y + hop, chips)
            arrived(place.at[slot, k], precv.at[level, side, slot, k])
        relay(place, level, side, k, lambda copy: copy.start())

    def opposite_arrived(place, level, side, k):
        if rings:
            slot = lax.rem(y + 2, chips)
            arrived(place.at[slot, k], precv.at[level, side, slot, k])

    def pair_copy(level, k):
        return remote(
            own_links(level, k), pair.at[level, k],
            psend.at[level, 0, 0, k], precv.at[level, 0, chips, k], t, sibling,
        )

    def kept_copy(level, k):
        return remote(
            own_side(level, k, stream_at), kept_own.at[level, turn, k],
            psend.at[level, 1, 0, k], orecv.at[level, turn, k], toward_kept, c,
        )

    def helper_copy(k, side):
        return remote(
            done.at[k, pl.ds(link_top, 2 * LANES)], stream.at[k],
            psend.at[0, 0, side, k], orecv.at[1, 0, k], t - 1 + 2 * side, c,
        )

    def each_second(k, action):
        for side in range(2):
            @pl.when(t + 2 * side <= last)
            def _():
                action(helper_copy(k, side))

    def kept_pair_copy(level, side, k):
        return remote(
            kept_own.at[level, side, k], kept_pair.at[level, side, k],
            psend.at[level, side, 0, k], precv.at[level, side, chips, k], t, sibling,
        )

    def near_wait(k):
        for side in range(2):
            arrived(nbuf.at[side, k], nrecv.at[side, k])

    def product_copy(kind, m, p):
        tile = 2 * m + q
        src, send, col = gsrc.at[kind, p, m], gsend.at[kind, p, m], 2 * y + p
        if kind == 0:
            dst, recv, tm = nbuf.at[1 - turn, tile], nrecv.at[1 - turn, tile], toward_next
        elif kind == 1:
            dst, recv, tm = fbuf.at[turn, tile], frecv.at[turn, tile], toward_next
        else:
            dst, recv, tm = fbuf.at[1 - turn, tile], frecv.at[1 - turn, tile], toward_kept
        return remote(src, dst, send, recv, tm, col)

    def tip_copy(side):
        tm = t + step_size if side else t - step_size
        return remote(
            tsrc.at[side], tbuf.at[second, side], tsend.at[side], trecv.at[second, side], tm, c
        )

    def square_copy():
        return remote(zsrc, zbuf.at[turn], zsend, zrecv.at[turn], toward_next, c)

    group = lax.div(t, 4)

    def total_copy(other):
        place = tipbuf.at[group]
        return remote(
            place, place, bsend.at[other], brecv.at[group], lax.rem(t + other, blocks), c
        )

    def lanes_of(k):
        return pl.ds(pl.multiple_of(k * LANES, LANES), LANES)

    def exchange(level, k):
        spread(
            own_side(level, k, gather_at), peer.at[level], level, 0, k, lambda copy: copy.start()
        )
        pair_copy(level, k).start()

        @pl.when(kept_exists)
        def _():
            kept_copy(level, k).start()

        peer[level, y, k] = own_side(level, k, gather_at)[...]

    def pass_links(level, k):
        relay_when_here(peer.at[level], level, 0, k)

    def exchange_done(level, k):
        spread(
            own_side(level, k, gather_at), peer.at[level], level, 0, k,
            lambda copy: copy.wait_send(),
        )
        relay(peer.at[level], level, 0, k, lambda copy: copy.wait_send())
        pair_copy(level, k).wait_send()

        @pl.when(kept_exists)
        def _():
            kept_copy(level, k).wait_send()

    def collect(level, k):
        opposite_arrived(peer.at[level], level, 0, k)
        arrived(pair.at[level, k], precv.at[level, 0, chips, k])
        lanes = lanes_of(k)
        for slot in range(chips):
            high, low = split_two(peer[level, slot, k])
            to = slice(slot * LANES, (slot + 1) * LANES)
            col_high[to, lanes] = high
            col_low[to, lanes] = low
        for place, at in ((0, stream_at), (1, gather_at)):
            for index, value in (
                (q, own_side(level, k, at)[...]),
                (1 - q, pair[level, k, pl.ds(at, LANES), :]),
            ):
                high, low = split_two(value)
                to = pl.ds(pl.multiple_of((2 * place + index) * LANES, LANES), LANES)
                row_high[to, lanes] = high
                row_low[to, lanes] = low

    def kinds_of(level):
        near, far = slice(2 * LANES, 4 * LANES), slice(0, 2 * LANES)
        return ((0, near), (1, far)) if level == 0 else ((2, far),)

    def products_begin(level):
        collect(level, count - 2)
        for kind, rows in kinds_of(level):
            acc[min(kind, 1)] = dot_three(
                row_high[rows, :early], row_low[rows, :early],
                col_high[:, :early], col_low[:, :early],
            )

    def products_end(level):
        pass_links(level, count - 1)
        collect(level, count - 1)
        for kind, rows in kinds_of(level):
            value = acc[min(kind, 1)] + dot_three(
                row_high[rows, early:], row_low[rows, early:],
                col_high[:, early:], col_low[:, early:],
            )
            for m in range(chips):
                for p in range(2):
                    gsrc[kind, p, m] = -value[
                        p * LANES : (p + 1) * LANES, m * LANES : (m + 1) * LANES
                    ]
        order = [(m, kind) for m in range(chips) for kind, _ in kinds_of(level)]
        if level == 0 and chips == 4:
            order = [(0, 0), (0, 1), (1, 0), (2, 0), (1, 1), (3, 0), (2, 1), (3, 1)]
        for m, kind in order:
            for p in range(2):
                product_copy(kind, m, p).start()

    @pl.when(phase != 0)
    def _():
        @pl.when(odd == 1)
        def _():
            keep = jnp.where(t < last, 1.0, 0.0)
            for k in range(count):
                fbuf[1, k] = coup[0, :, k * LANES : (k + 1) * LANES] * keep

        def send_arrow():
            abuf[c] = arrow[0]

            @pl.when(is_second)
            def _():
                for side in range(2):
                    arrived(tbuf.at[0, side], trecv.at[0, side])
                abuf[c] = abuf[c] + (tbuf[0, 0] + tbuf[0, 1])

            for other in range(1, cols):
                arrow_copy(other).start()

        def send_tile(k):
            dbuf[k, own_rows, :] = diag[0, :, lanes_of(k)]

            @pl.when(is_second)
            def _():
                near_wait(k)
                dbuf[k, own_rows, :] = dbuf[k, own_rows, :] + (nbuf[0, k] + nbuf[1, k])

            own_tile_copies(k, lambda copy: copy.start())

        send_tile(0)

        @pl.when(c >= 1)
        def _():
            send_tile(1)

        @pl.when(c == 0)
        def _():
            send_arrow()

        relay_near(0)

        def step(k, carry):
            here = lanes_of(k)

            @pl.when(k + 1 < count)
            def _():
                relay_near(k + 1)

            @pl.when(((k == 0) & (c != 0)) | ((k > 0) & (lax.rem(k, 2) != q)))
            def _():
                tile_arrived(k, k)

            start = dbuf[k, here, :] + accum[k, here, :]
            prepare_step(k, start - dot_nt(lhs[here, :], rhs[here, :]), work)
            factor_and_update(accum, work, lhs, rhs)

            @pl.when(k == 0)
            def _():
                relay_opposite(0)

                @pl.when(c >= 2)
                def _():
                    send_tile(2)

            @pl.when(k + 1 < count)
            def _():
                relay_opposite(k + 1)

            @pl.when(k + 3 <= c)
            def _():
                send_tile(k + 3)

            @pl.when((c == k + 2) | ((k == 0) & (c == 1)))
            def _():
                send_arrow()

            for chip in range(chips):
                src = 2 * chip + 1 - q

                @pl.when(src > k)
                def _():
                    tile_arrived(src, k)

            @pl.when(k != c)
            def _():
                arrived(abuf.at[k], arecv.at[k])

            arrived(fbuf.at[0, k], frecv.at[0, k])

            @pl.when(is_second)
            def _():
                arrived(fbuf.at[1, k], frecv.at[1, k])

            source = jnp.concatenate([dbuf[k], fbuf[0, k], fbuf[1, k], abuf[k]], 0)
            solve_panel(k, accum[k] + source, done, work, lhs, rhs, nodes)

            def send_links():
                @pl.when(odd == 1)
                def _():
                    exchange(0, k)

                @pl.when(is_second)
                def _():
                    each_second(k, lambda copy: copy.start())

            send_links()

            @pl.when((k >= 1) & (odd == 1))
            def _():
                pass_links(0, k - 1)

            @pl.when((k >= 2) & (odd == 1))
            def _():
                collect(0, k - 2)

            return carry

        lax.fori_loop(0, count, step, 0)

        @pl.when(odd == 1)
        def _():
            products_begin(0)

        terms = jnp.zeros((tip_rows, 2 * LANES + tip_rows), jnp.float32)
        for k in range(count):
            terms = terms - dot_nt(
                wide_left(done[k, tip_top:, :]), wide_right(done[k, link_top:, :])
            )
        tsrc[0] = terms[:, :LANES]
        tsrc[1] = terms[:, LANES : 2 * LANES]
        square = jnp.concatenate(
            [terms[: tip_rows // 2, 2 * LANES :], terms[tip_rows // 2 :, 2 * LANES :]], 1
        )
        tip_copy(0).start()

        @pl.when(t + step_size <= last)
        def _():
            tip_copy(1).start()

        @pl.when(odd == 1)
        def _():
            zsrc[...] = square
            square_copy().start()
            products_end(0)

        @pl.when(is_second)
        def _():
            for slot in range(2):
                arrived(zbuf.at[slot], zrecv.at[slot])
            tipbuf[group] = square + (zbuf[0] + zbuf[1])
            for other in range(1, blocks):
                total_copy(other).start()

        for k in range(count):
            lanes = slice(k * LANES, (k + 1) * LANES)
            factor_out[0, :, lanes] = done[k, own_rows, :]
            for side in range(2):
                part = slice(link_top + side * LANES, link_top + (side + 1) * LANES)
                link_out[0, side, :, lanes] = done[k, part, :]
        arrow_out[0] = done[c, tip_top:, :]

        @pl.when(helps)
        def _():
            def help_step(k, carry):
                arrived(stream.at[k], orecv.at[1, 0, k])
                exchange(1, k)

                @pl.when(k >= 1)
                def _():
                    pass_links(1, k - 1)

                @pl.when(k >= 2)
                def _():
                    collect(1, k - 2)

                return carry

            lax.fori_loop(0, count, help_step, 0)
            products_begin(1)
            products_end(1)

        def drain(k, carry):
            own_tile_copies(k, lambda copy: copy.wait_send())
            near_forwards(k, lambda src, copy: copy.wait_send())
            ring_forward(k, lambda copy: copy.wait_send())
            opposite_forward(k, lambda src, copy: copy.wait_send())

            @pl.when((k > c) & is_second)
            def _():
                near_wait(k)

            @pl.when(is_second)
            def _():
                each_second(k, lambda copy: copy.wait_send())

            @pl.when(odd == 1)
            def _():
                exchange_done(0, k)

            @pl.when(helps)
            def _():
                exchange_done(1, k)

            return carry

        lax.fori_loop(0, count, drain, 0)
        for other in range(1, cols):
            arrow_copy(other).wait_send()
        tip_copy(0).wait_send()

        @pl.when(t + step_size <= last)
        def _():
            tip_copy(1).wait_send()

        @pl.when(odd == 1)
        def _():
            square_copy().wait_send()
            for kind in range(2):
                for m in range(chips):
                    for p in range(2):
                        product_copy(kind, m, p).wait_send()

        @pl.when(helps)
        def _():
            for m in range(chips):
                for p in range(2):
                    product_copy(2, m, p).wait_send()

        @pl.when(is_second)
        def _():
            for other in range(1, blocks):
                total_copy(other).wait_send()

    @pl.when(phase == 0)
    def _():
        @pl.when(t == 0)
        def _():
            for level in range(2):
                tbuf[level, 1] = jnp.zeros(tbuf.shape[2:], jnp.float32)
            fbuf[0] = jnp.zeros(fbuf.shape[1:], jnp.float32)
            for ref in (kept_row_high, kept_row_low, kept_col_high, kept_col_low):
                ref[1] = jnp.zeros(ref.shape[1:], jnp.bfloat16)

        def each_side(action):
            action(0)

            @pl.when(t > 0)
            def _():
                action(1)

        def kept_pass(level, side, k):
            relay_when_here(kept_peer.at[level, side], level, side, k)

        def kept_collect(level, side, k):
            opposite_arrived(kept_peer.at[level, side], level, side, k)
            arrived(kept_pair.at[level, side, k], precv.at[level, side, chips, k])
            lanes = lanes_of(k)
            for slot in range(chips):
                high, low = split_two(kept_peer[level, side, slot, k])
                to = slice(slot * LANES, (slot + 1) * LANES)
                kept_col_high[side, to, lanes] = high
                kept_col_low[side, to, lanes] = low
            for index, value in (
                (q, kept_own[level, side, k]), (1 - q, kept_pair[level, side, k])
            ):
                high, low = split_two(value)
                to = pl.ds(pl.multiple_of(index * LANES, LANES), LANES)
                kept_row_high[side, to, lanes] = high
                kept_row_low[side, to, lanes] = low

        def kept_products(lanes):
            value = None
            for side in range(2):
                term = dot_three(
                    kept_row_high[side, :, lanes], kept_row_low[side, :, lanes],
                    kept_col_high[side, :, lanes], kept_col_low[side, :, lanes],
                )
                value = term if value is None else value + term
            return value

        for level in range(2):
            def kept_step(k, carry):
                def take(side):
                    arrived(kept_own.at[level, side, k], orecv.at[level, side, k])
                    spread(
                        kept_own.at[level, side, k], kept_peer.at[level, side], level, side, k,
                        lambda copy: copy.start(),
                    )
                    kept_pair_copy(level, side, k).start()
                    kept_peer[level, side, y, k] = kept_own[level, side, k]

                each_side(take)

                @pl.when(k >= 1)
                def _():
                    each_side(lambda side: kept_pass(level, side, k - 1))

                @pl.when(k >= 2)
                def _():
                    each_side(lambda side: kept_collect(level, side, k - 2))

                return carry

            lax.fori_loop(0, count, kept_step, 0)
            each_side(lambda side: kept_collect(level, side, count - 2))
            partial_sum = kept_products(slice(0, early))
            if level == 0:
                kept_acc[...] = partial_sum
            else:
                kept_acc[...] = kept_acc[...] + partial_sum
            each_side(lambda side: kept_pass(level, side, count - 1))
            each_side(lambda side: kept_collect(level, side, count - 1))
            kept_acc[...] = kept_acc[...] + kept_products(slice(early, nodes))

        def swap_copy():
            return remote(swap_src, swap_dst, ssend, srecv, t, sibling)

        other_rows = pl.ds(pl.multiple_of((1 - q) * LANES, LANES), LANES)
        for m in range(chips):
            swap_src[m] = kept_acc[other_rows, m * LANES : (m + 1) * LANES]
        swap_copy().start()
        my_rows = pl.ds(pl.multiple_of(q * LANES, LANES), LANES)
        for m in range(chips):
            lanes = lanes_of(2 * m + q)
            factor_out[0, :, lanes] = (
                diag[0, :, lanes] - kept_acc[my_rows, m * LANES : (m + 1) * LANES]
            )

        for level in range(2):
            each_side(lambda side: arrived(tbuf.at[level, side], trecv.at[level, side]))
        arrow_out[0] = arrow[0] + (
            (tbuf[0, 0] + tbuf[0, 1]) + (tbuf[1, 0] + tbuf[1, 1])
        )
        arrived(swap_dst, srecv)
        for m in range(chips):
            lanes = lanes_of(2 * m + 1 - q)
            factor_out[0, :, lanes] = diag[0, :, lanes] - swap_dst[m]
        for k in range(count):
            lanes = slice(k * LANES, (k + 1) * LANES)
            arrived(fbuf.at[1, k], frecv.at[1, k])
            link_out[0, 1, :, lanes] = fbuf[1, k]

            @pl.when(t > 0)
            def _():
                arrived(fbuf.at[0, k], frecv.at[0, k])

            link_out[0, 0, :, lanes] = fbuf[0, k]

        swap_copy().wait_send()

        def kept_drain(k, carry):
            def wait_all(side):
                for level in range(2):
                    spread(
                        kept_own.at[level, side, k], kept_peer.at[level, side], level, side, k,
                        lambda copy: copy.wait_send(),
                    )
                    relay(
                        kept_peer.at[level, side], level, side, k,
                        lambda copy: copy.wait_send(),
                    )
                    kept_pair_copy(level, side, k).wait_send()

            each_side(wait_all)
            return carry

        lax.fori_loop(0, count, kept_drain, 0)

    @pl.when(odd == 0)
    def _():
        for k in range(count):
            coupling_copy(k).wait_send()

    total = tip[...]
    for index in range(blocks // 4):
        @pl.when(t != 4 * index + 2)
        def _():
            arrived(tipbuf.at[index], brecv.at[index])

        part = tipbuf[index]
        total = total + jnp.concatenate([part[:, :tip_rows], part[:, tip_rows:]], 0)
    tip_out[...] = total


def publish_kernel(*refs):
    half = len(refs) // 2
    sources, targets, sems = refs[:half], refs[half : 2 * half], refs[-1]
    copies = [
        pltpu.make_async_copy(source, target, sems.at[index])
        for index, (source, target) in enumerate(zip(sources, targets))
    ]
    for copy in copies:
        copy.start()
    for copy in copies:
        copy.wait()


def publish(results):
    return pl.pallas_call(
        publish_kernel,
        out_shape=tuple(jax.ShapeDtypeStruct(r.shape, r.dtype) for r in results),
        in_specs=[pl.BlockSpec(memory_space=pltpu.VMEM)] * len(results),
        out_specs=(pl.BlockSpec(memory_space=pl.ANY),) * len(results),
        scratch_shapes=[pltpu.SemaphoreType.DMA((len(results),))],
        name="publish",
    )(*results)


def body(diagonal, coupling, arrowhead, tip_matrix):
    cols = lax.axis_size("col")
    blocks = lax.axis_size("tm")
    chips = cols // 2
    nodes = diagonal.shape[2]
    tip_rows = tip_matrix.shape[0]
    total = nodes + 2 * LANES + tip_rows
    count = nodes // LANES
    half = chips * LANES
    f32, bf16, dma = jnp.float32, jnp.bfloat16, pltpu.SemaphoreType.DMA
    tile = (LANES, LANES)
    scratch = [
        pltpu.VMEM((count, total, LANES), f32),
        pltpu.VMEM((count, total, LANES), f32),
        pltpu.VMEM((count, nodes, LANES), f32),
        pltpu.VMEM((2, count) + tile, f32),
        pltpu.VMEM((2, count) + tile, f32),
        pltpu.VMEM((2, chips, count) + tile, f32),
        pltpu.VMEM((2, count, 2 * LANES, LANES), f32),
        pltpu.VMEM((count, 2 * LANES, LANES), f32),
        pltpu.VMEM((3, 2, chips) + tile, f32),
        pltpu.VMEM((2, 2 * LANES, half), f32),
        pltpu.VMEM((2, 2, chips, count) + tile, f32),
        pltpu.VMEM((2, 2, count) + tile, f32),
        pltpu.VMEM((2, 2, count) + tile, f32),
        pltpu.VMEM((2 * LANES, half), f32),
        pltpu.VMEM((chips,) + tile, f32),
        pltpu.VMEM((chips,) + tile, f32),
        pltpu.VMEM((cols, tip_rows, LANES), f32),
        pltpu.VMEM((2, 2, tip_rows, LANES), f32),
        pltpu.VMEM((2, tip_rows, LANES), f32),
        pltpu.VMEM((2, tip_rows // 2, LANES), f32),
        pltpu.VMEM((tip_rows // 2, LANES), f32),
        pltpu.VMEM((blocks // 4, tip_rows // 2, LANES), f32),
        pltpu.VMEM((LANES, 2 * LANES), f32),
        pltpu.VMEM((total, 3 * LANES), bf16),
        pltpu.VMEM((nodes, 3 * LANES), bf16),
        pltpu.VMEM((4 * LANES, nodes), bf16),
        pltpu.VMEM((4 * LANES, nodes), bf16),
        pltpu.VMEM((half, nodes), bf16),
        pltpu.VMEM((half, nodes), bf16),
        pltpu.VMEM((2, 2 * LANES, nodes), bf16),
        pltpu.VMEM((2, 2 * LANES, nodes), bf16),
        pltpu.VMEM((2, half, nodes), bf16),
        pltpu.VMEM((2, half, nodes), bf16),
        dma((11, count)),
        dma((cols, count)),
        dma((cols,)),
        dma((cols,)),
        dma((2, 2, 4, count)),
        dma((2, 2, chips + 1, count)),
        dma((2, 2, count)),
        dma((count,)),
        dma((2, count)),
        dma((3, 2, chips)),
        dma((2, count)),
        dma((2,)),
        dma((2, 2)),
        dma,
        dma((2,)),
        dma((blocks,)),
        dma((blocks // 4,)),
        dma,
        dma,
    ]

    def call(*refs):
        kernel(chips, tip_rows, blocks, *refs)

    arrow_t = jnp.swapaxes(arrowhead, 1, 2)
    results = pl.pallas_call(
        call,
        out_shape=(
            jax.ShapeDtypeStruct(diagonal.shape, f32),
            jax.ShapeDtypeStruct((1, 2) + diagonal.shape[1:], f32),
            jax.ShapeDtypeStruct(arrow_t.shape, f32),
            jax.ShapeDtypeStruct(tip_matrix.shape, f32),
        ),
        in_specs=[pl.BlockSpec(memory_space=pltpu.VMEM)] * 4,
        out_specs=(pl.BlockSpec(memory_space=pltpu.VMEM),) * 4,
        scratch_shapes=scratch,
        compiler_params=pltpu.CompilerParams(
            collective_id=0, has_side_effects=True, vmem_limit_bytes=60 * 1024 * 1024
        ),
        name="cyclic_reduction",
    )(diagonal, coupling, arrow_t, tip_matrix)
    factors, links, arrows, reduced = publish(results)
    return factors, links, jnp.swapaxes(arrows, 1, 2), reduced


def solution(mesh):
    in_specs = (P("tm", "col", None), P("tm", "col", None), P("tm", "col", None), P())
    out_specs = (P("tm", "col", None), P("tm", None, "col", None), P("tm", "col", None), P())
    return jax.shard_map(body, mesh=mesh, in_specs=in_specs, out_specs=out_specs, check_vma=False)
```

```python
import jax
import jax.numpy as jnp
from jax import lax
from jax.experimental import pallas as pl
from jax.experimental.pallas import tpu as pltpu
from jax.sharding import PartitionSpec as P

LANES = 128
PANEL = 32
SPREAD = 16


def split_two(value):
    high = value.astype(jnp.bfloat16)
    low = (value - high.astype(jnp.float32)).astype(jnp.bfloat16)
    return high, low


def split_three(value):
    high = value.astype(jnp.bfloat16)
    rest = value - high.astype(jnp.float32)
    middle = rest.astype(jnp.bfloat16)
    low = (rest - middle.astype(jnp.float32)).astype(jnp.bfloat16)
    return high, middle, low


def spread_row(vec, row):
    return jnp.broadcast_to(vec[row : row + 1, :], (8, LANES))


def spread_lane(vec, lane):
    return jnp.take_along_axis(vec, jnp.full(vec.shape, lane, jnp.int32), axis=1)


def factor_tile(work, fill=lambda part: None):
    sub = lax.broadcasted_iota(jnp.int32, (8, LANES), 0)
    groups = PANEL // 8
    for panel in range(LANES // PANEL):
        first = panel * PANEL
        spans = [slice(first + 8 * g, first + 8 * g + 8) for g in range(groups)]
        left = [work[span, :LANES] for span in spans]
        right = [work[span, LANES:] for span in spans]
        pivots = [None] * groups
        pivot = None
        for r in range(PANEL):
            if r % SPREAD == 0:
                cols = {
                    c: [
                        spread_lane(left[g], first + c) if g >= c // 8 else None
                        for g in range(groups)
                    ]
                    for c in range(r, r + SPREAD)
                }
                fill((first + r) // SPREAD)
            h, q = r // 8, r % 8
            if r % SPREAD == 0:
                pivot = spread_row(cols[r][h], q)
            pivots[h] = pivot if q == 0 else jnp.where(sub == q, pivot, pivots[h])
            if r == PANEL - 1:
                break
            inverse = 1.0 / pivot
            if (r + 1) % SPREAD:
                h_next, q_next = (r + 1) // 8, (r + 1) % 8
                entry = spread_row(cols[r][h_next], q_next)
                pivot = spread_row(cols[r + 1][h_next], q_next) - (entry * inverse) * entry
            coef, masked = [None] * groups, [None] * groups
            for g in range(h, groups):
                coef[g] = cols[r][g] * inverse
                masked[g] = jnp.where(sub > q, coef[g], 0.0) if g == h else coef[g]
            for c in range(r + 1, r - r % SPREAD + SPREAD):
                entry = spread_row(cols[r][c // 8], c % 8)
                for g in range(c // 8, groups):
                    cols[c][g] = cols[c][g] - coef[g] * entry
            left_row, right_row = spread_row(left[h], q), spread_row(right[h], q)
            for g in range(h, groups):
                if g == h and q == 7:
                    continue
                left[g] = left[g] - masked[g] * left_row
                right[g] = right[g] - masked[g] * right_row
        rows = []
        for g in range(groups):
            scale = lax.rsqrt(pivots[g])
            rows.append(jnp.concatenate([left[g] * scale, right[g] * scale], 1))
        rows = jnp.concatenate(rows, 0)
        work[first : first + PANEL, :] = rows
        if first + PANEL < LANES:
            a, b, c = split_three(rows)
            lhs = jnp.concatenate([a, a, b, a, b, c], 0)[:, :LANES]
            rhs = jnp.concatenate([a, b, a, c, b, a], 0)
            update = lax.dot_general(
                lhs, rhs, (((0,), (0,)), ((), ())), preferred_element_type=jnp.float32
            )
            n = first + PANEL
            work[n:, :] = work[n:, :] - update[n:, :]


def dot_nt(left, right):
    return lax.dot_general(
        left, right, (((1,), (1,)), ((), ())), preferred_element_type=jnp.float32
    )


def wide_left(value):
    high, low = split_two(value)
    return jnp.concatenate([high, high, low], 1)


def wide_right(value):
    high, low = split_two(value)
    return jnp.concatenate([high, low, high], 1)


def prepare_step(k, start, work):
    row_id = lax.broadcasted_iota(jnp.int32, (LANES, LANES), 0)
    col_id = lax.broadcasted_iota(jnp.int32, (LANES, LANES), 1)
    work[:, :LANES] = start
    work[:, LANES:] = jnp.where(row_id == col_id, 1.0, 0.0)


def factor_and_update(acc, work, lhs, rhs):
    count, total, _ = acc.shape

    def fill(panel):
        pair, part = panel // 2, panel % 2
        if pair >= count // 2:
            return
        top = 2 * LANES * pair
        middle = top + (total - top) // 32 * 16
        rows = slice(top, middle) if part == 0 else slice(middle, total)
        update = dot_nt(lhs[rows, :], rhs[top : top + 2 * LANES, :])
        acc[2 * pair, rows, :] = acc[2 * pair, rows, :] - update[:, :LANES]
        acc[2 * pair + 1, rows, :] = acc[2 * pair + 1, rows, :] - update[:, LANES:]

    factor_tile(work, fill)


def solve_panel(k, column, done, work, lhs, rhs, nodes):
    total = column.shape[0]
    row_id = lax.broadcasted_iota(jnp.int32, (LANES, LANES), 0)
    col_id = lax.broadcasted_iota(jnp.int32, (LANES, LANES), 1)
    here = pl.ds(pl.multiple_of(k * LANES, LANES), LANES)
    solved = dot_nt(wide_left(column), wide_right(work[:, LANES:]))
    rows = lax.broadcasted_iota(jnp.int32, (total, LANES), 0)
    solved = jnp.where(rows >= (k + 1) * LANES, solved, 0.0)
    done[k] = solved
    done[k, here, :] = jnp.where(row_id <= col_id, work[:, :LANES], 0.0).T
    high, low = split_two(solved)
    lhs[...] = jnp.concatenate([high, high, low], 1)
    rhs[...] = jnp.concatenate([high[:nodes], low[:nodes], high[:nodes]], 1)


MESH = pl.DeviceIdType.MESH


def dot_three(left_high, left_low, right_high, right_low):
    value = dot_nt(left_high, right_high)
    value = value + dot_nt(left_high, right_low)
    return value + dot_nt(left_low, right_high)


def kernel(
    chips, tip_rows, blocks,
    diag, coup, arrow, tip,
    factor_out, link_out, arrow_out, tip_out,
    done, accum, dbuf, fbuf, nbuf, peer, pair, stream, gsrc, acc, kept_peer, kept_pair, kept_own,
    kept_acc, swap_src, swap_dst, abuf, tbuf, tsrc, zbuf, zsrc, tipbuf,
    work, lhs, rhs, row_high, row_low, col_high, col_low,
    kept_row_high, kept_row_low, kept_col_high, kept_col_low,
    dsend, drecv, asend, arecv, psend, precv, orecv, csend, frecv, gsend, nrecv,
    tsend, trecv, zsend, zrecv, bsend, brecv, ssend, srecv,
):
    t = lax.axis_index("tm")
    c = lax.axis_index("col")
    y, q = lax.div(c, 2), lax.rem(c, 2)
    sibling = c + 1 - 2 * q
    cols = 2 * chips
    count = cols
    nodes = count * LANES
    link_top, tip_top = nodes, nodes + 2 * LANES
    phase = lax.rem(t, 4)
    odd = lax.rem(t, 2)
    second = 1 - odd
    step_size = 2 - odd
    is_second = phase == 2
    last = blocks - 1
    early = nodes - LANES
    toward_next, toward_kept = t + 2 - phase, t - 2 + phase
    turn = lax.div(phase, 2)
    gather_at = pl.multiple_of(LANES * (1 - turn), LANES)
    stream_at = pl.multiple_of(LANES * turn, LANES)
    kept_exists = toward_kept <= last
    helps = (odd == 1) & kept_exists
    own_rows = pl.ds(pl.multiple_of(c * LANES, LANES), LANES)

    def remote(src, dst, send, recv, tm, col):
        return pltpu.make_async_remote_copy(
            src_ref=src, dst_ref=dst, send_sem=send, recv_sem=recv,
            device_id={"tm": tm, "col": col}, device_id_type=MESH,
        )

    def arrived(dst, recv):
        remote(dst, dst, recv, recv, t, sibling).wait_recv()

    barrier = pltpu.get_barrier_semaphore()

    def greet(tm, col):
        pl.semaphore_signal(
            barrier, inc=1, device_id={"tm": tm, "col": col}, device_id_type=MESH
        )

    for other in range(1, cols):
        greet(t, lax.rem(c + other, cols))
    for other in range(1, blocks):
        greet(lax.rem(t + other, blocks), c)
    for other in (1, blocks - 1):
        greet(lax.rem(t + other, blocks), sibling)
    for k in range(count):
        accum[k] = jnp.zeros(accum.shape[1:], jnp.float32)
    lhs[...] = jnp.zeros(lhs.shape, jnp.bfloat16)
    rhs[...] = jnp.zeros(rhs.shape, jnp.bfloat16)
    pl.semaphore_wait(barrier, cols - 1 + blocks - 1 + 2)

    def coupling_copy(k):
        return remote(
            coup.at[0, :, pl.ds(k * LANES, LANES)], fbuf.at[0, k],
            csend.at[k], frecv.at[0, k], t + 1, c,
        )

    @pl.when(odd == 0)
    def _():
        for k in range(count):
            coupling_copy(k).start()

    def peer_of(other):
        return lax.rem(c + other, cols)

    def same_core(other):
        return 2 * lax.rem(y + other, chips) + q

    hops = [1, chips - 1] if chips > 2 else list(range(1, chips))
    rings = chips == 4

    def relay_ends(k):
        turn_at = 1 - 2 * lax.rem(y + k, 2)
        return lax.rem(y + turn_at + chips, chips), lax.rem(y - turn_at + chips, chips)

    def tile_copy(src_col, k, slot, target):
        place = dbuf.at[k, pl.ds(pl.multiple_of(src_col * LANES, LANES), LANES)]
        return remote(place, place, dsend.at[slot, k], drecv.at[src_col, k], t, target)

    def tile_arrived(src_col, k):
        place = dbuf.at[k, pl.ds(pl.multiple_of(src_col * LANES, LANES), LANES)]
        arrived(place, drecv.at[src_col, k])

    def by_ring(src, k):
        return (src > k) | ((src == k) & (k > 0))

    def own_tile_copies(k, action):
        @pl.when((c == k) & (k == 0))
        def _():
            for other in range(1, cols):
                action(tile_copy(c, k, other - 1, peer_of(other)))

        @pl.when(by_ring(c, k))
        def _():
            action(tile_copy(c, k, 0, sibling))
            for i, hop in enumerate(hops):
                action(tile_copy(c, k, 1 + i, same_core(hop)))

    def near_forwards(k, action):
        for i, hop in enumerate(hops):
            src = same_core(hop)

            @pl.when(by_ring(src, k))
            def _():
                action(src, tile_copy(src, k, 7 + i, sibling))

    def ring_forward(k, action):
        if rings:
            source, target = relay_ends(k)
            src = 2 * source + q

            @pl.when(by_ring(src, k))
            def _():
                action(tile_copy(src, k, 10, 2 * target + q))

    def opposite_forward(k, action):
        if rings:
            src = same_core(2)

            @pl.when(by_ring(src, k))
            def _():
                action(src, tile_copy(src, k, 9, sibling))

    def pass_on(src, k, copy):
        tile_arrived(src, k)
        copy.start()

    def relay_near(k):
        near_forwards(k, lambda src, copy: pass_on(src, k, copy))
        ring_forward(k, lambda copy: copy.start())

    def relay_opposite(k):
        opposite_forward(k, lambda src, copy: pass_on(src, k, copy))

    def arrow_copy(other):
        return remote(
            abuf.at[c], abuf.at[c], asend.at[other], arecv.at[c], t, peer_of(other)
        )

    def own_links(level, k):
        return done.at[k, pl.ds(link_top, 2 * LANES)] if level == 0 else stream.at[k]

    def own_side(level, k, at):
        if level == 0:
            return done.at[k, pl.ds(pl.multiple_of(link_top + at, LANES), LANES)]
        return stream.at[k, pl.ds(at, LANES)]

    def spread(src, place, level, side, k, action):
        for i, hop in enumerate(hops):
            action(remote(
                src, place.at[y, k], psend.at[level, side, 1 + i, k],
                precv.at[level, side, y, k], t, same_core(hop),
            ))
        if rings:
            @pl.when(k == count - 1)
            def _():
                action(remote(
                    src, place.at[y, k], psend.at[level, side, 3, k],
                    precv.at[level, side, y, k], t, same_core(2),
                ))

    def relay(place, level, side, k, action):
        if rings:
            @pl.when(k < count - 1)
            def _():
                source, target = relay_ends(k)
                tile = place.at[source, k]
                action(remote(
                    tile, tile, psend.at[level, side, 3, k],
                    precv.at[level, side, source, k], t, 2 * target + q,
                ))

    def relay_when_here(place, level, side, k):
        for hop in hops:
            slot = lax.rem(y + hop, chips)
            arrived(place.at[slot, k], precv.at[level, side, slot, k])
        relay(place, level, side, k, lambda copy: copy.start())

    def opposite_arrived(place, level, side, k):
        if rings:
            slot = lax.rem(y + 2, chips)
            arrived(place.at[slot, k], precv.at[level, side, slot, k])

    def pair_copy(level, k):
        return remote(
            own_links(level, k), pair.at[level, k],
            psend.at[level, 0, 0, k], precv.at[level, 0, chips, k], t, sibling,
        )

    def kept_copy(level, k):
        return remote(
            own_side(level, k, stream_at), kept_own.at[level, turn, k],
            psend.at[level, 1, 0, k], orecv.at[level, turn, k], toward_kept, c,
        )

    def helper_copy(k, side, part):
        at = LANES * (1 - side if part == 0 else side)
        return remote(
            done.at[k, pl.ds(link_top + at, LANES)], stream.at[k, pl.ds(at, LANES)],
            psend.at[0, part, side, k], orecv.at[1, part, k], t - 1 + 2 * side, c,
        )

    def each_second(k, action):
        for part, side in ((0, 0), (0, 1), (1, 0), (1, 1)):
            @pl.when(t + 2 * side <= last)
            def _():
                action(helper_copy(k, side, part))

    def kept_pair_copy(level, side, k):
        return remote(
            kept_own.at[level, side, k], kept_pair.at[level, side, k],
            psend.at[level, side, 0, k], precv.at[level, side, chips, k], t, sibling,
        )

    def near_wait(k):
        for side in range(2):
            arrived(nbuf.at[side, k], nrecv.at[side, k])

    def product_copy(kind, m, p):
        tile = 2 * m + q
        src, send, col = gsrc.at[kind, p, m], gsend.at[kind, p, m], 2 * y + p
        if kind == 0:
            dst, recv, tm = nbuf.at[1 - turn, tile], nrecv.at[1 - turn, tile], toward_next
        elif kind == 1:
            dst, recv, tm = fbuf.at[turn, tile], frecv.at[turn, tile], toward_next
        else:
            dst, recv, tm = fbuf.at[1 - turn, tile], frecv.at[1 - turn, tile], toward_kept
        return remote(src, dst, send, recv, tm, col)

    def tip_copy(side):
        tm = t + step_size if side else t - step_size
        return remote(
            tsrc.at[side], tbuf.at[second, side], tsend.at[side], trecv.at[second, side], tm, c
        )

    def square_copy():
        return remote(zsrc, zbuf.at[turn], zsend, zrecv.at[turn], toward_next, c)

    group = lax.div(t, 4)

    def total_copy(other):
        place = tipbuf.at[group]
        return remote(
            place, place, bsend.at[other], brecv.at[group], lax.rem(t + other, blocks), c
        )

    def lanes_of(k):
        return pl.ds(pl.multiple_of(k * LANES, LANES), LANES)

    def exchange(level, k):
        if level == 1:
            arrived(stream.at[k, pl.ds(gather_at, LANES)], orecv.at[1, 0, k])
        spread(
            own_side(level, k, gather_at), peer.at[level], level, 0, k, lambda copy: copy.start()
        )
        if level == 1:
            arrived(stream.at[k, pl.ds(stream_at, LANES)], orecv.at[1, 1, k])
        pair_copy(level, k).start()

        @pl.when(kept_exists)
        def _():
            kept_copy(level, k).start()

        peer[level, y, k] = own_side(level, k, gather_at)[...]

    def pass_links(level, k):
        relay_when_here(peer.at[level], level, 0, k)

    def exchange_done(level, k):
        spread(
            own_side(level, k, gather_at), peer.at[level], level, 0, k,
            lambda copy: copy.wait_send(),
        )
        relay(peer.at[level], level, 0, k, lambda copy: copy.wait_send())
        pair_copy(level, k).wait_send()

        @pl.when(kept_exists)
        def _():
            kept_copy(level, k).wait_send()

    def collect(level, k):
        opposite_arrived(peer.at[level], level, 0, k)
        arrived(pair.at[level, k], precv.at[level, 0, chips, k])
        lanes = lanes_of(k)
        for slot in range(chips):
            high, low = split_two(peer[level, slot, k])
            to = slice(slot * LANES, (slot + 1) * LANES)
            col_high[to, lanes] = high
            col_low[to, lanes] = low
        for place, at in ((0, stream_at), (1, gather_at)):
            for index, value in (
                (q, own_side(level, k, at)[...]),
                (1 - q, pair[level, k, pl.ds(at, LANES), :]),
            ):
                high, low = split_two(value)
                to = pl.ds(pl.multiple_of((2 * place + index) * LANES, LANES), LANES)
                row_high[to, lanes] = high
                row_low[to, lanes] = low

    def kinds_of(level):
        near, far = slice(2 * LANES, 4 * LANES), slice(0, 2 * LANES)
        return ((0, near), (1, far)) if level == 0 else ((2, far),)

    def products_begin(level):
        collect(level, count - 2)
        for kind, rows in kinds_of(level):
            acc[min(kind, 1)] = dot_three(
                row_high[rows, :early], row_low[rows, :early],
                col_high[:, :early], col_low[:, :early],
            )

    def products_end(level):
        pass_links(level, count - 1)
        collect(level, count - 1)
        for kind, rows in kinds_of(level):
            value = acc[min(kind, 1)] + dot_three(
                row_high[rows, early:], row_low[rows, early:],
                col_high[:, early:], col_low[:, early:],
            )
            for m in range(chips):
                for p in range(2):
                    gsrc[kind, p, m] = -value[
                        p * LANES : (p + 1) * LANES, m * LANES : (m + 1) * LANES
                    ]
        order = [(m, kind) for m in range(chips) for kind, _ in kinds_of(level)]
        if level == 0 and chips == 4:
            order = [(0, 0), (0, 1), (1, 0), (2, 0), (1, 1), (3, 0), (2, 1), (3, 1)]
        for m, kind in order:
            for p in range(2):
                product_copy(kind, m, p).start()

    @pl.when(phase != 0)
    def _():
        @pl.when(odd == 1)
        def _():
            keep = jnp.where(t < last, 1.0, 0.0)
            for k in range(count):
                fbuf[1, k] = coup[0, :, k * LANES : (k + 1) * LANES] * keep

        def send_arrow():
            abuf[c] = arrow[0]

            @pl.when(is_second)
            def _():
                for side in range(2):
                    arrived(tbuf.at[0, side], trecv.at[0, side])
                abuf[c] = abuf[c] + (tbuf[0, 0] + tbuf[0, 1])

            for other in range(1, cols):
                arrow_copy(other).start()

        def send_tile(k):
            dbuf[k, own_rows, :] = diag[0, :, lanes_of(k)]

            @pl.when(is_second)
            def _():
                near_wait(k)
                dbuf[k, own_rows, :] = dbuf[k, own_rows, :] + (nbuf[0, k] + nbuf[1, k])

            own_tile_copies(k, lambda copy: copy.start())

        send_tile(0)

        @pl.when(c >= 1)
        def _():
            send_tile(1)

        @pl.when(c == 0)
        def _():
            send_arrow()

        relay_near(0)
        relay_near(1)

        def step(k, carry):
            here = lanes_of(k)

            if count > 2:
                @pl.when(k == 1)
                def _():
                    relay_near(2)

            @pl.when((k >= 2) & (k + 2 < count))
            def _():
                relay_near(k + 2)

            @pl.when((k >= 3) & (k + 1 < count))
            def _():
                relay_opposite(k + 1)

            @pl.when(((k == 0) & (c != 0)) | ((k > 0) & (lax.rem(k, 2) != q)))
            def _():
                tile_arrived(k, k)

            start = dbuf[k, here, :] + accum[k, here, :]
            prepare_step(k, start - dot_nt(lhs[here, :], rhs[here, :]), work)
            factor_and_update(accum, work, lhs, rhs)

            @pl.when(k == 0)
            def _():
                relay_opposite(0)
                relay_opposite(1)
                for first in (2, 3):
                    if first < count:
                        @pl.when(c >= first)
                        def _():
                            send_tile(first)

            if count > 3:
                @pl.when(k == 1)
                def _():
                    relay_near(3)

            @pl.when((k >= 1) & (k + 1 < count) & (k <= 2))
            def _():
                relay_opposite(k + 1)

            @pl.when(k + 4 <= c)
            def _():
                send_tile(k + 4)

            @pl.when((c == k + 2) | ((k == 0) & (c == 1)))
            def _():
                send_arrow()

            for chip in range(chips):
                src = 2 * chip + 1 - q

                @pl.when(src > k)
                def _():
                    tile_arrived(src, k)

            @pl.when(k != c)
            def _():
                arrived(abuf.at[k], arecv.at[k])

            arrived(fbuf.at[0, k], frecv.at[0, k])

            @pl.when(is_second)
            def _():
                arrived(fbuf.at[1, k], frecv.at[1, k])

            source = jnp.concatenate([dbuf[k], fbuf[0, k], fbuf[1, k], abuf[k]], 0)
            solve_panel(k, accum[k] + source, done, work, lhs, rhs, nodes)

            def send_links():
                @pl.when(odd == 1)
                def _():
                    exchange(0, k)

                @pl.when(is_second)
                def _():
                    each_second(k, lambda copy: copy.start())

            send_links()

            @pl.when((k >= 1) & (odd == 1))
            def _():
                pass_links(0, k - 1)

            @pl.when((k >= 2) & (odd == 1))
            def _():
                collect(0, k - 2)

            return carry

        lax.fori_loop(0, count, step, 0)

        @pl.when(odd == 1)
        def _():
            products_begin(0)

        terms = jnp.zeros((tip_rows, 2 * LANES + tip_rows), jnp.float32)
        for k in range(count):
            terms = terms - dot_nt(
                wide_left(done[k, tip_top:, :]), wide_right(done[k, link_top:, :])
            )
        tsrc[0] = terms[:, :LANES]
        tsrc[1] = terms[:, LANES : 2 * LANES]
        square = jnp.concatenate(
            [terms[: tip_rows // 2, 2 * LANES :], terms[tip_rows // 2 :, 2 * LANES :]], 1
        )
        tip_copy(0).start()

        @pl.when(t + step_size <= last)
        def _():
            tip_copy(1).start()

        @pl.when(odd == 1)
        def _():
            zsrc[...] = square
            square_copy().start()
            products_end(0)

        @pl.when(is_second)
        def _():
            for slot in range(2):
                arrived(zbuf.at[slot], zrecv.at[slot])
            tipbuf[group] = square + (zbuf[0] + zbuf[1])
            for other in range(1, blocks):
                total_copy(other).start()

        for k in range(count):
            lanes = slice(k * LANES, (k + 1) * LANES)
            factor_out[0, :, lanes] = done[k, own_rows, :]
            for side in range(2):
                part = slice(link_top + side * LANES, link_top + (side + 1) * LANES)
                link_out[0, side, :, lanes] = done[k, part, :]
        arrow_out[0] = done[c, tip_top:, :]

        @pl.when(helps)
        def _():
            def help_step(k, carry):
                exchange(1, k)

                @pl.when(k >= 1)
                def _():
                    pass_links(1, k - 1)

                @pl.when(k >= 2)
                def _():
                    collect(1, k - 2)

                return carry

            lax.fori_loop(0, count, help_step, 0)
            products_begin(1)
            products_end(1)

        def drain(k, carry):
            own_tile_copies(k, lambda copy: copy.wait_send())
            near_forwards(k, lambda src, copy: copy.wait_send())
            ring_forward(k, lambda copy: copy.wait_send())
            opposite_forward(k, lambda src, copy: copy.wait_send())

            @pl.when((k > c) & is_second)
            def _():
                near_wait(k)

            @pl.when(is_second)
            def _():
                each_second(k, lambda copy: copy.wait_send())

            @pl.when(odd == 1)
            def _():
                exchange_done(0, k)

            @pl.when(helps)
            def _():
                exchange_done(1, k)

            return carry

        lax.fori_loop(0, count, drain, 0)
        for other in range(1, cols):
            arrow_copy(other).wait_send()
        tip_copy(0).wait_send()

        @pl.when(t + step_size <= last)
        def _():
            tip_copy(1).wait_send()

        @pl.when(odd == 1)
        def _():
            square_copy().wait_send()
            for kind in range(2):
                for m in range(chips):
                    for p in range(2):
                        product_copy(kind, m, p).wait_send()

        @pl.when(helps)
        def _():
            for m in range(chips):
                for p in range(2):
                    product_copy(2, m, p).wait_send()

        @pl.when(is_second)
        def _():
            for other in range(1, blocks):
                total_copy(other).wait_send()

    @pl.when(phase == 0)
    def _():
        @pl.when(t == 0)
        def _():
            for level in range(2):
                tbuf[level, 1] = jnp.zeros(tbuf.shape[2:], jnp.float32)
            fbuf[0] = jnp.zeros(fbuf.shape[1:], jnp.float32)
            for ref in (kept_row_high, kept_row_low, kept_col_high, kept_col_low):
                ref[1] = jnp.zeros(ref.shape[1:], jnp.bfloat16)

        def each_side(action):
            action(0)

            @pl.when(t > 0)
            def _():
                action(1)

        def kept_pass(level, side, k):
            relay_when_here(kept_peer.at[level, side], level, side, k)

        def kept_collect(level, side, k):
            opposite_arrived(kept_peer.at[level, side], level, side, k)
            arrived(kept_pair.at[level, side, k], precv.at[level, side, chips, k])
            lanes = lanes_of(k)
            for slot in range(chips):
                high, low = split_two(kept_peer[level, side, slot, k])
                to = slice(slot * LANES, (slot + 1) * LANES)
                kept_col_high[side, to, lanes] = high
                kept_col_low[side, to, lanes] = low
            for index, value in (
                (q, kept_own[level, side, k]), (1 - q, kept_pair[level, side, k])
            ):
                high, low = split_two(value)
                to = pl.ds(pl.multiple_of(index * LANES, LANES), LANES)
                kept_row_high[side, to, lanes] = high
                kept_row_low[side, to, lanes] = low

        def kept_products(lanes):
            value = None
            for side in range(2):
                term = dot_three(
                    kept_row_high[side, :, lanes], kept_row_low[side, :, lanes],
                    kept_col_high[side, :, lanes], kept_col_low[side, :, lanes],
                )
                value = term if value is None else value + term
            return value

        for level in range(2):
            def kept_step(k, carry):
                def take(side):
                    arrived(kept_own.at[level, side, k], orecv.at[level, side, k])
                    spread(
                        kept_own.at[level, side, k], kept_peer.at[level, side], level, side, k,
                        lambda copy: copy.start(),
                    )
                    kept_pair_copy(level, side, k).start()
                    kept_peer[level, side, y, k] = kept_own[level, side, k]

                each_side(take)

                @pl.when(k >= 1)
                def _():
                    each_side(lambda side: kept_pass(level, side, k - 1))

                @pl.when(k >= 2)
                def _():
                    each_side(lambda side: kept_collect(level, side, k - 2))

                return carry

            lax.fori_loop(0, count, kept_step, 0)
            each_side(lambda side: kept_collect(level, side, count - 2))
            partial_sum = kept_products(slice(0, early))
            if level == 0:
                kept_acc[...] = partial_sum
            else:
                kept_acc[...] = kept_acc[...] + partial_sum
            each_side(lambda side: kept_pass(level, side, count - 1))
            each_side(lambda side: kept_collect(level, side, count - 1))
            kept_acc[...] = kept_acc[...] + kept_products(slice(early, nodes))

        def swap_copy():
            return remote(swap_src, swap_dst, ssend, srecv, t, sibling)

        other_rows = pl.ds(pl.multiple_of((1 - q) * LANES, LANES), LANES)
        for m in range(chips):
            swap_src[m] = kept_acc[other_rows, m * LANES : (m + 1) * LANES]
        swap_copy().start()
        my_rows = pl.ds(pl.multiple_of(q * LANES, LANES), LANES)
        for m in range(chips):
            lanes = lanes_of(2 * m + q)
            factor_out[0, :, lanes] = (
                diag[0, :, lanes] - kept_acc[my_rows, m * LANES : (m + 1) * LANES]
            )

        for level in range(2):
            each_side(lambda side: arrived(tbuf.at[level, side], trecv.at[level, side]))
        arrow_out[0] = arrow[0] + (
            (tbuf[0, 0] + tbuf[0, 1]) + (tbuf[1, 0] + tbuf[1, 1])
        )
        arrived(swap_dst, srecv)
        for m in range(chips):
            lanes = lanes_of(2 * m + 1 - q)
            factor_out[0, :, lanes] = diag[0, :, lanes] - swap_dst[m]
        for k in range(count):
            lanes = slice(k * LANES, (k + 1) * LANES)
            arrived(fbuf.at[1, k], frecv.at[1, k])
            link_out[0, 1, :, lanes] = fbuf[1, k]

            @pl.when(t > 0)
            def _():
                arrived(fbuf.at[0, k], frecv.at[0, k])

            link_out[0, 0, :, lanes] = fbuf[0, k]

        swap_copy().wait_send()

        def kept_drain(k, carry):
            def wait_all(side):
                for level in range(2):
                    spread(
                        kept_own.at[level, side, k], kept_peer.at[level, side], level, side, k,
                        lambda copy: copy.wait_send(),
                    )
                    relay(
                        kept_peer.at[level, side], level, side, k,
                        lambda copy: copy.wait_send(),
                    )
                    kept_pair_copy(level, side, k).wait_send()

            each_side(wait_all)
            return carry

        lax.fori_loop(0, count, kept_drain, 0)

    @pl.when(odd == 0)
    def _():
        for k in range(count):
            coupling_copy(k).wait_send()

    total = tip[...]
    for index in range(blocks // 4):
        @pl.when(t != 4 * index + 2)
        def _():
            arrived(tipbuf.at[index], brecv.at[index])

        part = tipbuf[index]
        total = total + jnp.concatenate([part[:, :tip_rows], part[:, tip_rows:]], 0)
    tip_out[...] = total


def publish_kernel(*refs):
    half = len(refs) // 2
    sources, targets, sems = refs[:half], refs[half : 2 * half], refs[-1]
    copies = [
        pltpu.make_async_copy(source, target, sems.at[index])
        for index, (source, target) in enumerate(zip(sources, targets))
    ]
    for copy in copies:
        copy.start()
    for copy in copies:
        copy.wait()


def publish(results):
    return pl.pallas_call(
        publish_kernel,
        out_shape=tuple(jax.ShapeDtypeStruct(r.shape, r.dtype) for r in results),
        in_specs=[pl.BlockSpec(memory_space=pltpu.VMEM)] * len(results),
        out_specs=(pl.BlockSpec(memory_space=pl.ANY),) * len(results),
        scratch_shapes=[pltpu.SemaphoreType.DMA((len(results),))],
        name="publish",
    )(*results)


def body(diagonal, coupling, arrowhead, tip_matrix):
    cols = lax.axis_size("col")
    blocks = lax.axis_size("tm")
    chips = cols // 2
    nodes = diagonal.shape[2]
    tip_rows = tip_matrix.shape[0]
    total = nodes + 2 * LANES + tip_rows
    count = nodes // LANES
    half = chips * LANES
    f32, bf16, dma = jnp.float32, jnp.bfloat16, pltpu.SemaphoreType.DMA
    tile = (LANES, LANES)
    scratch = [
        pltpu.VMEM((count, total, LANES), f32),
        pltpu.VMEM((count, total, LANES), f32),
        pltpu.VMEM((count, nodes, LANES), f32),
        pltpu.VMEM((2, count) + tile, f32),
        pltpu.VMEM((2, count) + tile, f32),
        pltpu.VMEM((2, chips, count) + tile, f32),
        pltpu.VMEM((2, count, 2 * LANES, LANES), f32),
        pltpu.VMEM((count, 2 * LANES, LANES), f32),
        pltpu.VMEM((3, 2, chips) + tile, f32),
        pltpu.VMEM((2, 2 * LANES, half), f32),
        pltpu.VMEM((2, 2, chips, count) + tile, f32),
        pltpu.VMEM((2, 2, count) + tile, f32),
        pltpu.VMEM((2, 2, count) + tile, f32),
        pltpu.VMEM((2 * LANES, half), f32),
        pltpu.VMEM((chips,) + tile, f32),
        pltpu.VMEM((chips,) + tile, f32),
        pltpu.VMEM((cols, tip_rows, LANES), f32),
        pltpu.VMEM((2, 2, tip_rows, LANES), f32),
        pltpu.VMEM((2, tip_rows, LANES), f32),
        pltpu.VMEM((2, tip_rows // 2, LANES), f32),
        pltpu.VMEM((tip_rows // 2, LANES), f32),
        pltpu.VMEM((blocks // 4, tip_rows // 2, LANES), f32),
        pltpu.VMEM((LANES, 2 * LANES), f32),
        pltpu.VMEM((total, 3 * LANES), bf16),
        pltpu.VMEM((nodes, 3 * LANES), bf16),
        pltpu.VMEM((4 * LANES, nodes), bf16),
        pltpu.VMEM((4 * LANES, nodes), bf16),
        pltpu.VMEM((half, nodes), bf16),
        pltpu.VMEM((half, nodes), bf16),
        pltpu.VMEM((2, 2 * LANES, nodes), bf16),
        pltpu.VMEM((2, 2 * LANES, nodes), bf16),
        pltpu.VMEM((2, half, nodes), bf16),
        pltpu.VMEM((2, half, nodes), bf16),
        dma((11, count)),
        dma((cols, count)),
        dma((cols,)),
        dma((cols,)),
        dma((2, 2, 4, count)),
        dma((2, 2, chips + 1, count)),
        dma((2, 2, count)),
        dma((count,)),
        dma((2, count)),
        dma((3, 2, chips)),
        dma((2, count)),
        dma((2,)),
        dma((2, 2)),
        dma,
        dma((2,)),
        dma((blocks,)),
        dma((blocks // 4,)),
        dma,
        dma,
    ]

    def call(*refs):
        kernel(chips, tip_rows, blocks, *refs)

    arrow_t = jnp.swapaxes(arrowhead, 1, 2)
    results = pl.pallas_call(
        call,
        out_shape=(
            jax.ShapeDtypeStruct(diagonal.shape, f32),
            jax.ShapeDtypeStruct((1, 2) + diagonal.shape[1:], f32),
            jax.ShapeDtypeStruct(arrow_t.shape, f32),
            jax.ShapeDtypeStruct(tip_matrix.shape, f32),
        ),
        in_specs=[pl.BlockSpec(memory_space=pltpu.VMEM)] * 4,
        out_specs=(pl.BlockSpec(memory_space=pltpu.VMEM),) * 4,
        scratch_shapes=scratch,
        compiler_params=pltpu.CompilerParams(
            collective_id=0, has_side_effects=True, vmem_limit_bytes=60 * 1024 * 1024
        ),
        name="cyclic_reduction",
    )(diagonal, coupling, arrow_t, tip_matrix)
    factors, links, arrows, reduced = publish(results)
    return factors, links, jnp.swapaxes(arrows, 1, 2), reduced


def solution(mesh):
    in_specs = (P("tm", "col", None), P("tm", "col", None), P("tm", "col", None), P())
    out_specs = (P("tm", "col", None), P("tm", None, "col", None), P("tm", "col", None), P())
    return jax.shard_map(body, mesh=mesh, in_specs=in_specs, out_specs=out_specs, check_vma=False)
```

```python
import jax
import jax.numpy as jnp
from jax import lax
from jax.experimental import pallas as pl
from jax.experimental.pallas import tpu as pltpu
from jax.sharding import PartitionSpec as P

LANES = 128
PANEL = 32
SPREAD = 16


def split_two(value):
    high = value.astype(jnp.bfloat16)
    low = (value - high.astype(jnp.float32)).astype(jnp.bfloat16)
    return high, low


def split_three(value):
    high = value.astype(jnp.bfloat16)
    rest = value - high.astype(jnp.float32)
    middle = rest.astype(jnp.bfloat16)
    low = (rest - middle.astype(jnp.float32)).astype(jnp.bfloat16)
    return high, middle, low


def spread_row(vec, row):
    return jnp.broadcast_to(vec[row : row + 1, :], (8, LANES))


def spread_lane(vec, lane):
    return jnp.take_along_axis(vec, jnp.full(vec.shape, lane, jnp.int32), axis=1)


def factor_tile(work, fill=lambda part: None):
    sub = lax.broadcasted_iota(jnp.int32, (8, LANES), 0)
    groups = PANEL // 8
    for panel in range(LANES // PANEL):
        first = panel * PANEL
        spans = [slice(first + 8 * g, first + 8 * g + 8) for g in range(groups)]
        left = [work[span, :LANES] for span in spans]
        right = [work[span, LANES:] for span in spans]
        pivots = [None] * groups
        pivot = None
        for r in range(PANEL):
            if r % SPREAD == 0:
                cols = {
                    c: [
                        spread_lane(left[g], first + c) if g >= c // 8 else None
                        for g in range(groups)
                    ]
                    for c in range(r, r + SPREAD)
                }
                fill((first + r) // SPREAD)
            h, q = r // 8, r % 8
            if r % SPREAD == 0:
                pivot = spread_row(cols[r][h], q)
            pivots[h] = pivot if q == 0 else jnp.where(sub == q, pivot, pivots[h])
            if r == PANEL - 1:
                break
            inverse = 1.0 / pivot
            if (r + 1) % SPREAD:
                h_next, q_next = (r + 1) // 8, (r + 1) % 8
                entry = spread_row(cols[r][h_next], q_next)
                pivot = spread_row(cols[r + 1][h_next], q_next) - (entry * inverse) * entry
            coef, masked = [None] * groups, [None] * groups
            for g in range(h, groups):
                coef[g] = cols[r][g] * inverse
                masked[g] = jnp.where(sub > q, coef[g], 0.0) if g == h else coef[g]
            for c in range(r + 1, r - r % SPREAD + SPREAD):
                entry = spread_row(cols[r][c // 8], c % 8)
                for g in range(c // 8, groups):
                    cols[c][g] = cols[c][g] - coef[g] * entry
            left_row, right_row = spread_row(left[h], q), spread_row(right[h], q)
            for g in range(h, groups):
                if g == h and q == 7:
                    continue
                left[g] = left[g] - masked[g] * left_row
                right[g] = right[g] - masked[g] * right_row
        rows = []
        for g in range(groups):
            scale = lax.rsqrt(pivots[g])
            rows.append(jnp.concatenate([left[g] * scale, right[g] * scale], 1))
        rows = jnp.concatenate(rows, 0)
        work[first : first + PANEL, :] = rows
        if first + PANEL < LANES:
            a, b, c = split_three(rows)
            lhs = jnp.concatenate([a, a, b, a, b, c], 0)[:, :LANES]
            rhs = jnp.concatenate([a, b, a, c, b, a], 0)
            update = lax.dot_general(
                lhs, rhs, (((0,), (0,)), ((), ())), preferred_element_type=jnp.float32
            )
            n = first + PANEL
            work[n:, :] = work[n:, :] - update[n:, :]


def dot_nt(left, right):
    return lax.dot_general(
        left, right, (((1,), (1,)), ((), ())), preferred_element_type=jnp.float32
    )


def wide_left(value):
    high, low = split_two(value)
    return jnp.concatenate([high, high, low], 1)


def wide_right(value):
    high, low = split_two(value)
    return jnp.concatenate([high, low, high], 1)


def prepare_step(k, start, work):
    row_id = lax.broadcasted_iota(jnp.int32, (LANES, LANES), 0)
    col_id = lax.broadcasted_iota(jnp.int32, (LANES, LANES), 1)
    work[:, :LANES] = start
    work[:, LANES:] = jnp.where(row_id == col_id, 1.0, 0.0)


def factor_and_update(acc, work, lhs, rhs):
    count, total, _ = acc.shape

    def fill(panel):
        pair, part = panel // 2, panel % 2
        if pair >= count // 2:
            return
        top = 2 * LANES * pair
        middle = top + (total - top) // 32 * 16
        rows = slice(top, middle) if part == 0 else slice(middle, total)
        update = dot_nt(lhs[rows, :], rhs[top : top + 2 * LANES, :])
        acc[2 * pair, rows, :] = acc[2 * pair, rows, :] - update[:, :LANES]
        acc[2 * pair + 1, rows, :] = acc[2 * pair + 1, rows, :] - update[:, LANES:]

    factor_tile(work, fill)


def solve_panel(k, column, done, work, lhs, rhs, nodes):
    total = column.shape[0]
    row_id = lax.broadcasted_iota(jnp.int32, (LANES, LANES), 0)
    col_id = lax.broadcasted_iota(jnp.int32, (LANES, LANES), 1)
    here = pl.ds(pl.multiple_of(k * LANES, LANES), LANES)
    solved = dot_nt(wide_left(column), wide_right(work[:, LANES:]))
    rows = lax.broadcasted_iota(jnp.int32, (total, LANES), 0)
    solved = jnp.where(rows >= (k + 1) * LANES, solved, 0.0)
    done[k] = solved
    done[k, here, :] = jnp.where(row_id <= col_id, work[:, :LANES], 0.0).T
    high, low = split_two(solved)
    lhs[...] = jnp.concatenate([high, high, low], 1)
    rhs[...] = jnp.concatenate([high[:nodes], low[:nodes], high[:nodes]], 1)


MESH = pl.DeviceIdType.MESH


def dot_three(left_high, left_low, right_high, right_low):
    value = dot_nt(left_high, right_high)
    value = value + dot_nt(left_high, right_low)
    return value + dot_nt(left_low, right_high)


def kernel(
    chips, tip_rows, blocks,
    diag, coup, arrow, tip,
    factor_out, link_out, arrow_out, tip_out,
    done, accum, dbuf, fbuf, nbuf, peer, pair, stream, gsrc, acc, kept_peer, kept_pair, kept_own,
    kept_acc, swap_src, swap_dst, abuf, tbuf, tsrc, zbuf, zsrc, tipbuf,
    work, lhs, rhs, row_high, row_low, col_high, col_low,
    kept_row_high, kept_row_low, kept_col_high, kept_col_low,
    dsend, drecv, asend, arecv, psend, precv, orecv, csend, frecv, gsend, nrecv,
    tsend, trecv, zsend, zrecv, bsend, brecv, ssend, srecv,
):
    t = lax.axis_index("tm")
    c = lax.axis_index("col")
    y, q = lax.div(c, 2), lax.rem(c, 2)
    sibling = c + 1 - 2 * q
    cols = 2 * chips
    count = cols
    nodes = count * LANES
    link_top, tip_top = nodes, nodes + 2 * LANES
    phase = lax.rem(t, 4)
    odd = lax.rem(t, 2)
    second = 1 - odd
    step_size = 2 - odd
    is_second = phase == 2
    last = blocks - 1
    early = nodes - LANES
    toward_next, toward_kept = t + 2 - phase, t - 2 + phase
    turn = lax.div(phase, 2)
    gather_at = pl.multiple_of(LANES * (1 - turn), LANES)
    stream_at = pl.multiple_of(LANES * turn, LANES)
    kept_exists = toward_kept <= last
    helps = (odd == 1) & kept_exists
    own_rows = pl.ds(pl.multiple_of(c * LANES, LANES), LANES)

    def remote(src, dst, send, recv, tm, col):
        return pltpu.make_async_remote_copy(
            src_ref=src, dst_ref=dst, send_sem=send, recv_sem=recv,
            device_id={"tm": tm, "col": col}, device_id_type=MESH,
        )

    def arrived(dst, recv):
        remote(dst, dst, recv, recv, t, sibling).wait_recv()

    barrier = pltpu.get_barrier_semaphore()

    def greet(tm, col):
        pl.semaphore_signal(
            barrier, inc=1, device_id={"tm": tm, "col": col}, device_id_type=MESH
        )

    for other in range(1, cols):
        greet(t, lax.rem(c + other, cols))
    for other in range(1, blocks):
        greet(lax.rem(t + other, blocks), c)
    for other in (1, blocks - 1):
        greet(lax.rem(t + other, blocks), sibling)
    for k in range(count):
        accum[k] = jnp.zeros(accum.shape[1:], jnp.float32)
    lhs[...] = jnp.zeros(lhs.shape, jnp.bfloat16)
    rhs[...] = jnp.zeros(rhs.shape, jnp.bfloat16)
    pl.semaphore_wait(barrier, cols - 1 + blocks - 1 + 2)

    def coupling_copy(k):
        return remote(
            coup.at[0, :, pl.ds(k * LANES, LANES)], fbuf.at[0, k],
            csend.at[k], frecv.at[0, k], t + 1, c,
        )

    @pl.when(odd == 0)
    def _():
        for k in range(count):
            coupling_copy(k).start()

    def peer_of(other):
        return lax.rem(c + other, cols)

    def same_core(other):
        return 2 * lax.rem(y + other, chips) + q

    hops = [1, chips - 1] if chips > 2 else list(range(1, chips))
    rings = chips == 4

    def relay_ends(k):
        turn_at = 1 - 2 * lax.rem(y + k, 2)
        return lax.rem(y + turn_at + chips, chips), lax.rem(y - turn_at + chips, chips)

    def tile_copy(src_col, k, slot, target):
        place = dbuf.at[k, pl.ds(pl.multiple_of(src_col * LANES, LANES), LANES)]
        return remote(place, place, dsend.at[slot, k], drecv.at[src_col, k], t, target)

    def tile_arrived(src_col, k):
        place = dbuf.at[k, pl.ds(pl.multiple_of(src_col * LANES, LANES), LANES)]
        arrived(place, drecv.at[src_col, k])

    def by_ring(src, k):
        return (src > k) | ((src == k) & (k > 0))

    def own_tile_copies(k, action):
        @pl.when((c == k) & (k == 0))
        def _():
            for other in range(1, cols):
                action(tile_copy(c, k, other - 1, peer_of(other)))

        @pl.when(by_ring(c, k))
        def _():
            action(tile_copy(c, k, 0, sibling))
            for i, hop in enumerate(hops):
                action(tile_copy(c, k, 1 + i, same_core(hop)))

    def near_forwards(k, action):
        for i, hop in enumerate(hops):
            src = same_core(hop)

            @pl.when(by_ring(src, k))
            def _():
                action(src, tile_copy(src, k, 7 + i, sibling))

    def ring_forward(k, action):
        if rings:
            source, target = relay_ends(k)
            src = 2 * source + q

            @pl.when(by_ring(src, k))
            def _():
                action(tile_copy(src, k, 10, 2 * target + q))

    def opposite_forward(k, action):
        if rings:
            src = same_core(2)

            @pl.when(by_ring(src, k))
            def _():
                action(src, tile_copy(src, k, 9, sibling))

    def pass_on(src, k, copy):
        tile_arrived(src, k)
        copy.start()

    def relay_near(k):
        near_forwards(k, lambda src, copy: pass_on(src, k, copy))
        ring_forward(k, lambda copy: copy.start())

    def relay_opposite(k):
        opposite_forward(k, lambda src, copy: pass_on(src, k, copy))

    def arrow_copy(other):
        return remote(
            abuf.at[c], abuf.at[c], asend.at[other], arecv.at[c], t, peer_of(other)
        )

    def own_links(level, k):
        return done.at[k, pl.ds(link_top, 2 * LANES)] if level == 0 else stream.at[k]

    def own_side(level, k, at):
        if level == 0:
            return done.at[k, pl.ds(pl.multiple_of(link_top + at, LANES), LANES)]
        return stream.at[k, pl.ds(at, LANES)]

    def spread(src, place, level, side, k, action):
        for i, hop in enumerate(hops):
            action(remote(
                src, place.at[y, k], psend.at[level, side, 1 + i, k],
                precv.at[level, side, y, k], t, same_core(hop),
            ))
        if rings:
            @pl.when(k == count - 1)
            def _():
                action(remote(
                    src, place.at[y, k], psend.at[level, side, 3, k],
                    precv.at[level, side, y, k], t, same_core(2),
                ))

    def relay(place, level, side, k, action):
        if rings:
            @pl.when(k < count - 1)
            def _():
                source, target = relay_ends(k)
                tile = place.at[source, k]
                action(remote(
                    tile, tile, psend.at[level, side, 3, k],
                    precv.at[level, side, source, k], t, 2 * target + q,
                ))

    def relay_when_here(place, level, side, k):
        for hop in hops:
            slot = lax.rem(y + hop, chips)
            arrived(place.at[slot, k], precv.at[level, side, slot, k])
        relay(place, level, side, k, lambda copy: copy.start())

    def opposite_arrived(place, level, side, k):
        if rings:
            slot = lax.rem(y + 2, chips)
            arrived(place.at[slot, k], precv.at[level, side, slot, k])

    def pair_copy(level, k):
        return remote(
            own_links(level, k), pair.at[level, k],
            psend.at[level, 0, 0, k], precv.at[level, 0, chips, k], t, sibling,
        )

    def kept_copy(level, k):
        return remote(
            own_side(level, k, stream_at), kept_own.at[level, turn, k],
            psend.at[level, 1, 0, k], orecv.at[level, turn, k], toward_kept, c,
        )

    def helper_copy(k, side, part):
        at = LANES * (1 - side if part == 0 else side)
        return remote(
            done.at[k, pl.ds(link_top + at, LANES)], stream.at[k, pl.ds(at, LANES)],
            psend.at[0, part, side, k], orecv.at[1, part, k], t - 1 + 2 * side, c,
        )

    def each_second(k, action):
        for part, side in ((0, 0), (0, 1), (1, 0), (1, 1)):
            @pl.when(t + 2 * side <= last)
            def _():
                action(helper_copy(k, side, part))

    def kept_pair_copy(level, side, k):
        return remote(
            kept_own.at[level, side, k], kept_pair.at[level, side, k],
            psend.at[level, side, 0, k], precv.at[level, side, chips, k], t, sibling,
        )

    def near_wait(k):
        for side in range(2):
            arrived(nbuf.at[side, k], nrecv.at[side, k])

    def product_copy(kind, m, p):
        tile = 2 * m + q
        src, send, col = gsrc.at[kind, p, m], gsend.at[kind, p, m], 2 * y + p
        if kind == 0:
            dst, recv, tm = nbuf.at[1 - turn, tile], nrecv.at[1 - turn, tile], toward_next
        elif kind == 1:
            dst, recv, tm = fbuf.at[turn, tile], frecv.at[turn, tile], toward_next
        else:
            dst, recv, tm = fbuf.at[1 - turn, tile], frecv.at[1 - turn, tile], toward_kept
        return remote(src, dst, send, recv, tm, col)

    def tip_copy(side):
        tm = t + step_size if side else t - step_size
        return remote(
            tsrc.at[side], tbuf.at[second, side], tsend.at[side], trecv.at[second, side], tm, c
        )

    def square_copy():
        return remote(zsrc, zbuf.at[turn], zsend, zrecv.at[turn], toward_next, c)

    group = lax.div(t, 4)

    def total_copy(other):
        place = tipbuf.at[group]
        return remote(
            place, place, bsend.at[other], brecv.at[group], lax.rem(t + other, blocks), c
        )

    def lanes_of(k):
        return pl.ds(pl.multiple_of(k * LANES, LANES), LANES)

    def exchange(level, k):
        if level == 1:
            arrived(stream.at[k, pl.ds(gather_at, LANES)], orecv.at[1, 0, k])
        spread(
            own_side(level, k, gather_at), peer.at[level], level, 0, k, lambda copy: copy.start()
        )
        if level == 1:
            arrived(stream.at[k, pl.ds(stream_at, LANES)], orecv.at[1, 1, k])
        pair_copy(level, k).start()

        @pl.when(kept_exists)
        def _():
            kept_copy(level, k).start()

        peer[level, y, k] = own_side(level, k, gather_at)[...]

    def pass_links(level, k):
        relay_when_here(peer.at[level], level, 0, k)

    def exchange_done(level, k):
        spread(
            own_side(level, k, gather_at), peer.at[level], level, 0, k,
            lambda copy: copy.wait_send(),
        )
        relay(peer.at[level], level, 0, k, lambda copy: copy.wait_send())
        pair_copy(level, k).wait_send()

        @pl.when(kept_exists)
        def _():
            kept_copy(level, k).wait_send()

    def collect(level, k):
        opposite_arrived(peer.at[level], level, 0, k)
        arrived(pair.at[level, k], precv.at[level, 0, chips, k])
        lanes = lanes_of(k)
        for slot in range(chips):
            high, low = split_two(peer[level, slot, k])
            to = slice(slot * LANES, (slot + 1) * LANES)
            col_high[to, lanes] = high
            col_low[to, lanes] = low
        for place, at in ((0, stream_at), (1, gather_at)):
            for index, value in (
                (q, own_side(level, k, at)[...]),
                (1 - q, pair[level, k, pl.ds(at, LANES), :]),
            ):
                high, low = split_two(value)
                to = pl.ds(pl.multiple_of((2 * place + index) * LANES, LANES), LANES)
                row_high[to, lanes] = high
                row_low[to, lanes] = low

    def kinds_of(level):
        near, far = slice(2 * LANES, 4 * LANES), slice(0, 2 * LANES)
        return ((0, near), (1, far)) if level == 0 else ((2, far),)

    def products_begin(level):
        collect(level, count - 2)
        for kind, rows in kinds_of(level):
            acc[min(kind, 1)] = dot_three(
                row_high[rows, :early], row_low[rows, :early],
                col_high[:, :early], col_low[:, :early],
            )

    def products_end(level):
        pass_links(level, count - 1)
        collect(level, count - 1)

        def finish(kind, rows):
            value = acc[min(kind, 1)] + dot_three(
                row_high[rows, early:], row_low[rows, early:],
                col_high[:, early:], col_low[:, early:],
            )
            for m in range(chips):
                for p in range(2):
                    gsrc[kind, p, m] = -value[
                        p * LANES : (p + 1) * LANES, m * LANES : (m + 1) * LANES
                    ]

        kinds = kinds_of(level)
        order = sorted(
            ((m, kind) for m in range(chips) for kind, _ in kinds),
            key=lambda item: 2 * item[0] + (3 if item[1] else 0),
        )
        finish(*kinds[0])
        finished = 1
        for m, kind in order:
            if finished < len(kinds) and kind == kinds[finished][0]:
                finish(*kinds[finished])
                finished += 1
            for p in range(2):
                product_copy(kind, m, p).start()

    @pl.when(phase != 0)
    def _():
        @pl.when(odd == 1)
        def _():
            keep = jnp.where(t < last, 1.0, 0.0)
            for k in range(count):
                fbuf[1, k] = coup[0, :, k * LANES : (k + 1) * LANES] * keep

        def send_arrow():
            abuf[c] = arrow[0]

            @pl.when(is_second)
            def _():
                for side in range(2):
                    arrived(tbuf.at[0, side], trecv.at[0, side])
                abuf[c] = abuf[c] + (tbuf[0, 0] + tbuf[0, 1])

            for other in range(1, cols):
                arrow_copy(other).start()

        def send_tile(k):
            dbuf[k, own_rows, :] = diag[0, :, lanes_of(k)]

            @pl.when(is_second)
            def _():
                near_wait(k)
                dbuf[k, own_rows, :] = dbuf[k, own_rows, :] + (nbuf[0, k] + nbuf[1, k])

            own_tile_copies(k, lambda copy: copy.start())

        send_tile(0)

        @pl.when(c >= 1)
        def _():
            send_tile(1)

        @pl.when(c == 0)
        def _():
            send_arrow()

        relay_near(0)
        relay_near(1)
        for first in (2, 3):
            if first < count:
                @pl.when(c >= first)
                def _():
                    send_tile(first)

        def step(k, carry):
            here = lanes_of(k)

            @pl.when((k >= 2) & (k + 2 < count))
            def _():
                relay_near(k + 2)

            @pl.when((k >= 3) & (k + 1 < count))
            def _():
                relay_opposite(k + 1)

            @pl.when(((k == 0) & (c != 0)) | ((k > 0) & (lax.rem(k, 2) != q)))
            def _():
                tile_arrived(k, k)

            start = dbuf[k, here, :] + accum[k, here, :]
            prepare_step(k, start - dot_nt(lhs[here, :], rhs[here, :]), work)
            factor_and_update(accum, work, lhs, rhs)

            @pl.when(k == 0)
            def _():
                relay_opposite(0)
                relay_opposite(1)
                for first in (2, 3):
                    if first < count:
                        relay_near(first)

            @pl.when(k == 1)
            def _():
                for first in (2, 3):
                    if first < count:
                        relay_opposite(first)

            @pl.when(k + 4 <= c)
            def _():
                send_tile(k + 4)

            @pl.when((c == k + 2) | ((k == 0) & (c == 1)))
            def _():
                send_arrow()

            for chip in range(chips):
                src = 2 * chip + 1 - q

                @pl.when(src > k)
                def _():
                    tile_arrived(src, k)

            @pl.when(k != c)
            def _():
                arrived(abuf.at[k], arecv.at[k])

            arrived(fbuf.at[0, k], frecv.at[0, k])

            @pl.when(is_second)
            def _():
                arrived(fbuf.at[1, k], frecv.at[1, k])

            source = jnp.concatenate([dbuf[k], fbuf[0, k], fbuf[1, k], abuf[k]], 0)
            solve_panel(k, accum[k] + source, done, work, lhs, rhs, nodes)

            def send_links():
                @pl.when(odd == 1)
                def _():
                    exchange(0, k)

                @pl.when(is_second)
                def _():
                    each_second(k, lambda copy: copy.start())

            send_links()

            @pl.when((k >= 1) & (odd == 1))
            def _():
                pass_links(0, k - 1)

            @pl.when((k >= 2) & (odd == 1))
            def _():
                collect(0, k - 2)

            return carry

        lax.fori_loop(0, count, step, 0)

        @pl.when(odd == 1)
        def _():
            products_begin(0)

        terms = jnp.zeros((tip_rows, 2 * LANES + tip_rows), jnp.float32)
        for k in range(count):
            terms = terms - dot_nt(
                wide_left(done[k, tip_top:, :]), wide_right(done[k, link_top:, :])
            )
        tsrc[0] = terms[:, :LANES]
        tsrc[1] = terms[:, LANES : 2 * LANES]
        square = jnp.concatenate(
            [terms[: tip_rows // 2, 2 * LANES :], terms[tip_rows // 2 :, 2 * LANES :]], 1
        )
        tip_copy(0).start()

        @pl.when(t + step_size <= last)
        def _():
            tip_copy(1).start()

        @pl.when(odd == 1)
        def _():
            zsrc[...] = square
            square_copy().start()
            products_end(0)

        @pl.when(is_second)
        def _():
            for slot in range(2):
                arrived(zbuf.at[slot], zrecv.at[slot])
            tipbuf[group] = square + (zbuf[0] + zbuf[1])
            for other in range(1, blocks):
                total_copy(other).start()

        for k in range(count):
            lanes = slice(k * LANES, (k + 1) * LANES)
            factor_out[0, :, lanes] = done[k, own_rows, :]
            for side in range(2):
                part = slice(link_top + side * LANES, link_top + (side + 1) * LANES)
                link_out[0, side, :, lanes] = done[k, part, :]
        arrow_out[0] = done[c, tip_top:, :]

        @pl.when(helps)
        def _():
            def help_step(k, carry):
                exchange(1, k)

                @pl.when(k >= 1)
                def _():
                    pass_links(1, k - 1)

                @pl.when(k >= 2)
                def _():
                    collect(1, k - 2)

                return carry

            lax.fori_loop(0, count, help_step, 0)
            products_begin(1)
            products_end(1)

        def drain(k, carry):
            own_tile_copies(k, lambda copy: copy.wait_send())
            near_forwards(k, lambda src, copy: copy.wait_send())
            ring_forward(k, lambda copy: copy.wait_send())
            opposite_forward(k, lambda src, copy: copy.wait_send())

            @pl.when((k > c) & is_second)
            def _():
                near_wait(k)

            @pl.when(is_second)
            def _():
                each_second(k, lambda copy: copy.wait_send())

            @pl.when(odd == 1)
            def _():
                exchange_done(0, k)

            @pl.when(helps)
            def _():
                exchange_done(1, k)

            return carry

        lax.fori_loop(0, count, drain, 0)
        for other in range(1, cols):
            arrow_copy(other).wait_send()
        tip_copy(0).wait_send()

        @pl.when(t + step_size <= last)
        def _():
            tip_copy(1).wait_send()

        @pl.when(odd == 1)
        def _():
            square_copy().wait_send()
            for kind in range(2):
                for m in range(chips):
                    for p in range(2):
                        product_copy(kind, m, p).wait_send()

        @pl.when(helps)
        def _():
            for m in range(chips):
                for p in range(2):
                    product_copy(2, m, p).wait_send()

        @pl.when(is_second)
        def _():
            for other in range(1, blocks):
                total_copy(other).wait_send()

    @pl.when(phase == 0)
    def _():
        @pl.when(t == 0)
        def _():
            for level in range(2):
                tbuf[level, 1] = jnp.zeros(tbuf.shape[2:], jnp.float32)
            fbuf[0] = jnp.zeros(fbuf.shape[1:], jnp.float32)
            for ref in (kept_row_high, kept_row_low, kept_col_high, kept_col_low):
                ref[1] = jnp.zeros(ref.shape[1:], jnp.bfloat16)

        def each_side(action):
            action(0)

            @pl.when(t > 0)
            def _():
                action(1)

        def kept_pass(level, side, k):
            relay_when_here(kept_peer.at[level, side], level, side, k)

        def kept_collect(level, side, k):
            opposite_arrived(kept_peer.at[level, side], level, side, k)
            arrived(kept_pair.at[level, side, k], precv.at[level, side, chips, k])
            lanes = lanes_of(k)
            for slot in range(chips):
                high, low = split_two(kept_peer[level, side, slot, k])
                to = slice(slot * LANES, (slot + 1) * LANES)
                kept_col_high[side, to, lanes] = high
                kept_col_low[side, to, lanes] = low
            for index, value in (
                (q, kept_own[level, side, k]), (1 - q, kept_pair[level, side, k])
            ):
                high, low = split_two(value)
                to = pl.ds(pl.multiple_of(index * LANES, LANES), LANES)
                kept_row_high[side, to, lanes] = high
                kept_row_low[side, to, lanes] = low

        def kept_products(lanes):
            value = None
            for side in range(2):
                term = dot_three(
                    kept_row_high[side, :, lanes], kept_row_low[side, :, lanes],
                    kept_col_high[side, :, lanes], kept_col_low[side, :, lanes],
                )
                value = term if value is None else value + term
            return value

        for level in range(2):
            def kept_step(k, carry):
                def take(side):
                    arrived(kept_own.at[level, side, k], orecv.at[level, side, k])
                    spread(
                        kept_own.at[level, side, k], kept_peer.at[level, side], level, side, k,
                        lambda copy: copy.start(),
                    )
                    kept_pair_copy(level, side, k).start()
                    kept_peer[level, side, y, k] = kept_own[level, side, k]

                each_side(take)

                @pl.when(k >= 1)
                def _():
                    each_side(lambda side: kept_pass(level, side, k - 1))

                @pl.when(k >= 2)
                def _():
                    each_side(lambda side: kept_collect(level, side, k - 2))

                return carry

            lax.fori_loop(0, count, kept_step, 0)
            each_side(lambda side: kept_collect(level, side, count - 2))
            partial_sum = kept_products(slice(0, early))
            if level == 0:
                kept_acc[...] = partial_sum
            else:
                kept_acc[...] = kept_acc[...] + partial_sum
            each_side(lambda side: kept_pass(level, side, count - 1))
            each_side(lambda side: kept_collect(level, side, count - 1))
            kept_acc[...] = kept_acc[...] + kept_products(slice(early, nodes))

        def swap_copy():
            return remote(swap_src, swap_dst, ssend, srecv, t, sibling)

        other_rows = pl.ds(pl.multiple_of((1 - q) * LANES, LANES), LANES)
        for m in range(chips):
            swap_src[m] = kept_acc[other_rows, m * LANES : (m + 1) * LANES]
        swap_copy().start()
        my_rows = pl.ds(pl.multiple_of(q * LANES, LANES), LANES)
        for m in range(chips):
            lanes = lanes_of(2 * m + q)
            factor_out[0, :, lanes] = (
                diag[0, :, lanes] - kept_acc[my_rows, m * LANES : (m + 1) * LANES]
            )

        for level in range(2):
            each_side(lambda side: arrived(tbuf.at[level, side], trecv.at[level, side]))
        arrow_out[0] = arrow[0] + (
            (tbuf[0, 0] + tbuf[0, 1]) + (tbuf[1, 0] + tbuf[1, 1])
        )
        arrived(swap_dst, srecv)
        for m in range(chips):
            lanes = lanes_of(2 * m + 1 - q)
            factor_out[0, :, lanes] = diag[0, :, lanes] - swap_dst[m]
        for k in range(count):
            lanes = slice(k * LANES, (k + 1) * LANES)
            arrived(fbuf.at[1, k], frecv.at[1, k])
            link_out[0, 1, :, lanes] = fbuf[1, k]

            @pl.when(t > 0)
            def _():
                arrived(fbuf.at[0, k], frecv.at[0, k])

            link_out[0, 0, :, lanes] = fbuf[0, k]

        swap_copy().wait_send()

        def kept_drain(k, carry):
            def wait_all(side):
                for level in range(2):
                    spread(
                        kept_own.at[level, side, k], kept_peer.at[level, side], level, side, k,
                        lambda copy: copy.wait_send(),
                    )
                    relay(
                        kept_peer.at[level, side], level, side, k,
                        lambda copy: copy.wait_send(),
                    )
                    kept_pair_copy(level, side, k).wait_send()

            each_side(wait_all)
            return carry

        lax.fori_loop(0, count, kept_drain, 0)

    @pl.when(odd == 0)
    def _():
        for k in range(count):
            coupling_copy(k).wait_send()

    total = tip[...]
    for index in range(blocks // 4):
        @pl.when(t != 4 * index + 2)
        def _():
            arrived(tipbuf.at[index], brecv.at[index])

        part = tipbuf[index]
        total = total + jnp.concatenate([part[:, :tip_rows], part[:, tip_rows:]], 0)
    tip_out[...] = total


def publish_kernel(*refs):
    half = len(refs) // 2
    sources, targets, sems = refs[:half], refs[half : 2 * half], refs[-1]
    copies = [
        pltpu.make_async_copy(source, target, sems.at[index])
        for index, (source, target) in enumerate(zip(sources, targets))
    ]
    for copy in copies:
        copy.start()
    for copy in copies:
        copy.wait()


def publish(results):
    return pl.pallas_call(
        publish_kernel,
        out_shape=tuple(jax.ShapeDtypeStruct(r.shape, r.dtype) for r in results),
        in_specs=[pl.BlockSpec(memory_space=pltpu.VMEM)] * len(results),
        out_specs=(pl.BlockSpec(memory_space=pl.ANY),) * len(results),
        scratch_shapes=[pltpu.SemaphoreType.DMA((len(results),))],
        name="publish",
    )(*results)


def body(diagonal, coupling, arrowhead, tip_matrix):
    cols = lax.axis_size("col")
    blocks = lax.axis_size("tm")
    chips = cols // 2
    nodes = diagonal.shape[2]
    tip_rows = tip_matrix.shape[0]
    total = nodes + 2 * LANES + tip_rows
    count = nodes // LANES
    half = chips * LANES
    f32, bf16, dma = jnp.float32, jnp.bfloat16, pltpu.SemaphoreType.DMA
    tile = (LANES, LANES)
    scratch = [
        pltpu.VMEM((count, total, LANES), f32),
        pltpu.VMEM((count, total, LANES), f32),
        pltpu.VMEM((count, nodes, LANES), f32),
        pltpu.VMEM((2, count) + tile, f32),
        pltpu.VMEM((2, count) + tile, f32),
        pltpu.VMEM((2, chips, count) + tile, f32),
        pltpu.VMEM((2, count, 2 * LANES, LANES), f32),
        pltpu.VMEM((count, 2 * LANES, LANES), f32),
        pltpu.VMEM((3, 2, chips) + tile, f32),
        pltpu.VMEM((2, 2 * LANES, half), f32),
        pltpu.VMEM((2, 2, chips, count) + tile, f32),
        pltpu.VMEM((2, 2, count) + tile, f32),
        pltpu.VMEM((2, 2, count) + tile, f32),
        pltpu.VMEM((2 * LANES, half), f32),
        pltpu.VMEM((chips,) + tile, f32),
        pltpu.VMEM((chips,) + tile, f32),
        pltpu.VMEM((cols, tip_rows, LANES), f32),
        pltpu.VMEM((2, 2, tip_rows, LANES), f32),
        pltpu.VMEM((2, tip_rows, LANES), f32),
        pltpu.VMEM((2, tip_rows // 2, LANES), f32),
        pltpu.VMEM((tip_rows // 2, LANES), f32),
        pltpu.VMEM((blocks // 4, tip_rows // 2, LANES), f32),
        pltpu.VMEM((LANES, 2 * LANES), f32),
        pltpu.VMEM((total, 3 * LANES), bf16),
        pltpu.VMEM((nodes, 3 * LANES), bf16),
        pltpu.VMEM((4 * LANES, nodes), bf16),
        pltpu.VMEM((4 * LANES, nodes), bf16),
        pltpu.VMEM((half, nodes), bf16),
        pltpu.VMEM((half, nodes), bf16),
        pltpu.VMEM((2, 2 * LANES, nodes), bf16),
        pltpu.VMEM((2, 2 * LANES, nodes), bf16),
        pltpu.VMEM((2, half, nodes), bf16),
        pltpu.VMEM((2, half, nodes), bf16),
        dma((11, count)),
        dma((cols, count)),
        dma((cols,)),
        dma((cols,)),
        dma((2, 2, 4, count)),
        dma((2, 2, chips + 1, count)),
        dma((2, 2, count)),
        dma((count,)),
        dma((2, count)),
        dma((3, 2, chips)),
        dma((2, count)),
        dma((2,)),
        dma((2, 2)),
        dma,
        dma((2,)),
        dma((blocks,)),
        dma((blocks // 4,)),
        dma,
        dma,
    ]

    def call(*refs):
        kernel(chips, tip_rows, blocks, *refs)

    arrow_t = jnp.swapaxes(arrowhead, 1, 2)
    results = pl.pallas_call(
        call,
        out_shape=(
            jax.ShapeDtypeStruct(diagonal.shape, f32),
            jax.ShapeDtypeStruct((1, 2) + diagonal.shape[1:], f32),
            jax.ShapeDtypeStruct(arrow_t.shape, f32),
            jax.ShapeDtypeStruct(tip_matrix.shape, f32),
        ),
        in_specs=[pl.BlockSpec(memory_space=pltpu.VMEM)] * 4,
        out_specs=(pl.BlockSpec(memory_space=pltpu.VMEM),) * 4,
        scratch_shapes=scratch,
        compiler_params=pltpu.CompilerParams(
            collective_id=0, has_side_effects=True, vmem_limit_bytes=60 * 1024 * 1024
        ),
        name="cyclic_reduction",
    )(diagonal, coupling, arrow_t, tip_matrix)
    factors, links, arrows, reduced = publish(results)
    return factors, links, jnp.swapaxes(arrows, 1, 2), reduced


def solution(mesh):
    in_specs = (P("tm", "col", None), P("tm", "col", None), P("tm", "col", None), P())
    out_specs = (P("tm", "col", None), P("tm", None, "col", None), P("tm", "col", None), P())
    return jax.shard_map(body, mesh=mesh, in_specs=in_specs, out_specs=out_specs, check_vma=False)
```

```python
import jax
import jax.numpy as jnp
from jax import lax
from jax.experimental import pallas as pl
from jax.experimental.pallas import tpu as pltpu
from jax.sharding import PartitionSpec as P

LANES = 128
PANEL = 32
SPREAD = 16


def split_two(value):
    high = value.astype(jnp.bfloat16)
    low = (value - high.astype(jnp.float32)).astype(jnp.bfloat16)
    return high, low


def split_three(value):
    high = value.astype(jnp.bfloat16)
    rest = value - high.astype(jnp.float32)
    middle = rest.astype(jnp.bfloat16)
    low = (rest - middle.astype(jnp.float32)).astype(jnp.bfloat16)
    return high, middle, low


def spread_row(vec, row):
    return jnp.broadcast_to(vec[row : row + 1, :], (8, LANES))


def spread_lane(vec, lane):
    return jnp.take_along_axis(vec, jnp.full(vec.shape, lane, jnp.int32), axis=1)


def factor_tile(work, fill=lambda part: None):
    sub = lax.broadcasted_iota(jnp.int32, (8, LANES), 0)
    groups = PANEL // 8
    for panel in range(LANES // PANEL):
        first = panel * PANEL
        spans = [slice(first + 8 * g, first + 8 * g + 8) for g in range(groups)]
        left = [work[span, :LANES] for span in spans]
        right = [work[span, LANES:] for span in spans]
        pivots = [None] * groups
        pivot = None
        for r in range(PANEL):
            if r % SPREAD == 0:
                cols = {
                    c: [
                        spread_lane(left[g], first + c) if g >= c // 8 else None
                        for g in range(groups)
                    ]
                    for c in range(r, r + SPREAD)
                }
                fill((first + r) // SPREAD)
            h, q = r // 8, r % 8
            if r % SPREAD == 0:
                pivot = spread_row(cols[r][h], q)
            pivots[h] = pivot if q == 0 else jnp.where(sub == q, pivot, pivots[h])
            if r == PANEL - 1:
                break
            inverse = 1.0 / pivot
            if (r + 1) % SPREAD:
                h_next, q_next = (r + 1) // 8, (r + 1) % 8
                entry = spread_row(cols[r][h_next], q_next)
                pivot = spread_row(cols[r + 1][h_next], q_next) - (entry * inverse) * entry
            coef, masked = [None] * groups, [None] * groups
            for g in range(h, groups):
                coef[g] = cols[r][g] * inverse
                masked[g] = jnp.where(sub > q, coef[g], 0.0) if g == h else coef[g]
            for c in range(r + 1, r - r % SPREAD + SPREAD):
                entry = spread_row(cols[r][c // 8], c % 8)
                for g in range(c // 8, groups):
                    cols[c][g] = cols[c][g] - coef[g] * entry
            left_row, right_row = spread_row(left[h], q), spread_row(right[h], q)
            for g in range(h, groups):
                if g == h and q == 7:
                    continue
                left[g] = left[g] - masked[g] * left_row
                right[g] = right[g] - masked[g] * right_row
        rows = []
        for g in range(groups):
            scale = lax.rsqrt(pivots[g])
            rows.append(jnp.concatenate([left[g] * scale, right[g] * scale], 1))
        rows = jnp.concatenate(rows, 0)
        work[first : first + PANEL, :] = rows
        if first + PANEL < LANES:
            a, b, c = split_three(rows)
            lhs = jnp.concatenate([a, a, b, a, b, c], 0)[:, :LANES]
            rhs = jnp.concatenate([a, b, a, c, b, a], 0)
            update = lax.dot_general(
                lhs, rhs, (((0,), (0,)), ((), ())), preferred_element_type=jnp.float32
            )
            n = first + PANEL
            work[n:, :] = work[n:, :] - update[n:, :]


def dot_nt(left, right):
    return lax.dot_general(
        left, right, (((1,), (1,)), ((), ())), preferred_element_type=jnp.float32
    )


def wide_left(value):
    high, low = split_two(value)
    return jnp.concatenate([high, high, low], 1)


def wide_right(value):
    high, low = split_two(value)
    return jnp.concatenate([high, low, high], 1)


def prepare_step(k, start, work):
    row_id = lax.broadcasted_iota(jnp.int32, (LANES, LANES), 0)
    col_id = lax.broadcasted_iota(jnp.int32, (LANES, LANES), 1)
    work[:, :LANES] = start
    work[:, LANES:] = jnp.where(row_id == col_id, 1.0, 0.0)


def factor_and_update(acc, work, lhs, rhs):
    count, total, _ = acc.shape

    def fill(panel):
        pair, part = panel // 2, panel % 2
        if pair >= count // 2:
            return
        top = 2 * LANES * pair
        middle = top + (total - top) // 32 * 16
        rows = slice(top, middle) if part == 0 else slice(middle, total)
        update = dot_nt(lhs[rows, :], rhs[top : top + 2 * LANES, :])
        acc[2 * pair, rows, :] = acc[2 * pair, rows, :] - update[:, :LANES]
        acc[2 * pair + 1, rows, :] = acc[2 * pair + 1, rows, :] - update[:, LANES:]

    factor_tile(work, fill)


def solve_panel(k, column, done, work, lhs, rhs, nodes):
    total = column.shape[0]
    row_id = lax.broadcasted_iota(jnp.int32, (LANES, LANES), 0)
    col_id = lax.broadcasted_iota(jnp.int32, (LANES, LANES), 1)
    here = pl.ds(pl.multiple_of(k * LANES, LANES), LANES)
    solved = dot_nt(wide_left(column), wide_right(work[:, LANES:]))
    rows = lax.broadcasted_iota(jnp.int32, (total, LANES), 0)
    solved = jnp.where(rows >= (k + 1) * LANES, solved, 0.0)
    done[k] = solved
    done[k, here, :] = jnp.where(row_id <= col_id, work[:, :LANES], 0.0).T
    high, low = split_two(solved)
    lhs[...] = jnp.concatenate([high, high, low], 1)
    rhs[...] = jnp.concatenate([high[:nodes], low[:nodes], high[:nodes]], 1)


MESH = pl.DeviceIdType.MESH


def dot_three(left_high, left_low, right_high, right_low):
    value = dot_nt(left_high, right_high)
    value = value + dot_nt(left_high, right_low)
    return value + dot_nt(left_low, right_high)


def kernel(
    chips, tip_rows, blocks,
    diag, coup, arrow, tip,
    factor_out, link_out, arrow_out, tip_out,
    done, accum, dbuf, fbuf, nbuf, peer, pair, stream, gsrc, acc, kept_peer, kept_pair, kept_own,
    kept_acc, swap_src, swap_dst, abuf, tbuf, tsrc, zbuf, zsrc, tipbuf,
    work, lhs, rhs, row_high, row_low, col_high, col_low,
    kept_row_high, kept_row_low, kept_col_high, kept_col_low,
    dsend, drecv, asend, arecv, psend, precv, orecv, csend, frecv, gsend, nrecv,
    tsend, trecv, zsend, zrecv, bsend, brecv, ssend, srecv,
):
    t = lax.axis_index("tm")
    c = lax.axis_index("col")
    y, q = lax.div(c, 2), lax.rem(c, 2)
    sibling = c + 1 - 2 * q
    cols = 2 * chips
    count = cols
    nodes = count * LANES
    link_top, tip_top = nodes, nodes + 2 * LANES
    phase = lax.rem(t, 4)
    odd = lax.rem(t, 2)
    second = 1 - odd
    step_size = 2 - odd
    is_second = phase == 2
    last = blocks - 1
    early = nodes - LANES
    toward_next, toward_kept = t + 2 - phase, t - 2 + phase
    turn = lax.div(phase, 2)
    gather_at = pl.multiple_of(LANES * (1 - turn), LANES)
    stream_at = pl.multiple_of(LANES * turn, LANES)
    kept_exists = toward_kept <= last
    helps = (odd == 1) & kept_exists
    own_rows = pl.ds(pl.multiple_of(c * LANES, LANES), LANES)

    def remote(src, dst, send, recv, tm, col):
        return pltpu.make_async_remote_copy(
            src_ref=src, dst_ref=dst, send_sem=send, recv_sem=recv,
            device_id={"tm": tm, "col": col}, device_id_type=MESH,
        )

    def arrived(dst, recv):
        remote(dst, dst, recv, recv, t, sibling).wait_recv()

    barrier = pltpu.get_barrier_semaphore()

    def greet(tm, col):
        pl.semaphore_signal(
            barrier, inc=1, device_id={"tm": tm, "col": col}, device_id_type=MESH
        )

    for other in range(1, cols):
        greet(t, lax.rem(c + other, cols))
    for other in range(1, blocks):
        greet(lax.rem(t + other, blocks), c)
    for other in (1, blocks - 1):
        greet(lax.rem(t + other, blocks), sibling)
    for k in range(count):
        accum[k] = jnp.zeros(accum.shape[1:], jnp.float32)
    lhs[...] = jnp.zeros(lhs.shape, jnp.bfloat16)
    rhs[...] = jnp.zeros(rhs.shape, jnp.bfloat16)
    pl.semaphore_wait(barrier, cols - 1 + blocks - 1 + 2)

    def coupling_copy(k):
        return remote(
            coup.at[0, :, pl.ds(k * LANES, LANES)], fbuf.at[0, k],
            csend.at[k], frecv.at[0, k], t + 1, c,
        )

    @pl.when(odd == 0)
    def _():
        for k in range(count):
            coupling_copy(k).start()

    def peer_of(other):
        return lax.rem(c + other, cols)

    def same_core(other):
        return 2 * lax.rem(y + other, chips) + q

    hops = [1, chips - 1] if chips > 2 else list(range(1, chips))
    rings = chips == 4

    def relay_ends(k):
        turn_at = 1 - 2 * lax.rem(y + k, 2)
        return lax.rem(y + turn_at + chips, chips), lax.rem(y - turn_at + chips, chips)

    def tile_copy(src_col, k, slot, target):
        place = dbuf.at[k, pl.ds(pl.multiple_of(src_col * LANES, LANES), LANES)]
        return remote(place, place, dsend.at[slot, k], drecv.at[src_col, k], t, target)

    def tile_arrived(src_col, k):
        place = dbuf.at[k, pl.ds(pl.multiple_of(src_col * LANES, LANES), LANES)]
        arrived(place, drecv.at[src_col, k])

    def by_ring(src, k):
        return (src > k) | ((src == k) & (k > 0))

    def own_tile_copies(k, action):
        @pl.when((c == k) & (k == 0))
        def _():
            for other in range(1, cols):
                action(tile_copy(c, k, other - 1, peer_of(other)))

        @pl.when(by_ring(c, k))
        def _():
            action(tile_copy(c, k, 0, sibling))
            for i, hop in enumerate(hops):
                action(tile_copy(c, k, 1 + i, same_core(hop)))

    def near_forwards(k, action):
        for i, hop in enumerate(hops):
            src = same_core(hop)

            @pl.when(by_ring(src, k))
            def _():
                action(src, tile_copy(src, k, 7 + i, sibling))

    def ring_forward(k, action):
        if rings:
            source, target = relay_ends(k)
            src = 2 * source + q

            @pl.when(by_ring(src, k))
            def _():
                action(tile_copy(src, k, 10, 2 * target + q))

    def opposite_forward(k, action):
        if rings:
            src = same_core(2)

            @pl.when(by_ring(src, k))
            def _():
                action(src, tile_copy(src, k, 9, sibling))

    def pass_on(src, k, copy):
        tile_arrived(src, k)
        copy.start()

    def relay_near(k):
        near_forwards(k, lambda src, copy: pass_on(src, k, copy))
        ring_forward(k, lambda copy: copy.start())

    def relay_opposite(k):
        opposite_forward(k, lambda src, copy: pass_on(src, k, copy))

    def arrow_copy(other):
        return remote(
            abuf.at[c], abuf.at[c], asend.at[other], arecv.at[c], t, peer_of(other)
        )

    def own_links(level, k):
        return done.at[k, pl.ds(link_top, 2 * LANES)] if level == 0 else stream.at[k]

    def own_side(level, k, at):
        if level == 0:
            return done.at[k, pl.ds(pl.multiple_of(link_top + at, LANES), LANES)]
        return stream.at[k, pl.ds(at, LANES)]

    def spread(src, place, level, side, k, action):
        for i, hop in enumerate(hops):
            action(remote(
                src, place.at[y, k], psend.at[level, side, 1 + i, k],
                precv.at[level, side, y, k], t, same_core(hop),
            ))
        if rings:
            @pl.when(k == count - 1)
            def _():
                action(remote(
                    src, place.at[y, k], psend.at[level, side, 3, k],
                    precv.at[level, side, y, k], t, same_core(2),
                ))

    def relay(place, level, side, k, action):
        if rings:
            @pl.when(k < count - 1)
            def _():
                source, target = relay_ends(k)
                tile = place.at[source, k]
                action(remote(
                    tile, tile, psend.at[level, side, 3, k],
                    precv.at[level, side, source, k], t, 2 * target + q,
                ))

    def relay_when_here(place, level, side, k):
        for hop in hops:
            slot = lax.rem(y + hop, chips)
            arrived(place.at[slot, k], precv.at[level, side, slot, k])
        relay(place, level, side, k, lambda copy: copy.start())

    def opposite_arrived(place, level, side, k):
        if rings:
            slot = lax.rem(y + 2, chips)
            arrived(place.at[slot, k], precv.at[level, side, slot, k])

    def pair_copy(level, k):
        return remote(
            own_links(level, k), pair.at[level, k],
            psend.at[level, 0, 0, k], precv.at[level, 0, chips, k], t, sibling,
        )

    def kept_copy(level, k):
        return remote(
            own_side(level, k, stream_at), kept_own.at[level, turn, k],
            psend.at[level, 1, 0, k], orecv.at[level, turn, k], toward_kept, c,
        )

    def helper_copy(k, side, part):
        at = LANES * (1 - side if part == 0 else side)
        return remote(
            done.at[k, pl.ds(link_top + at, LANES)], stream.at[k, pl.ds(at, LANES)],
            psend.at[0, part, side, k], orecv.at[1, part, k], t - 1 + 2 * side, c,
        )

    def each_second(k, action):
        for part, side in ((0, 0), (0, 1), (1, 0), (1, 1)):
            @pl.when(t + 2 * side <= last)
            def _():
                action(helper_copy(k, side, part))

    def kept_pair_copy(level, side, k):
        return remote(
            kept_own.at[level, side, k], kept_pair.at[level, side, k],
            psend.at[level, side, 0, k], precv.at[level, side, chips, k], t, sibling,
        )

    def near_wait(k):
        for side in range(2):
            arrived(nbuf.at[side, k], nrecv.at[side, k])

    def product_copy(kind, m, p):
        tile = 2 * m + q
        src, send, col = gsrc.at[kind, p, m], gsend.at[kind, p, m], 2 * y + p
        if kind == 0:
            dst, recv, tm = nbuf.at[1 - turn, tile], nrecv.at[1 - turn, tile], toward_next
        elif kind == 1:
            dst, recv, tm = fbuf.at[turn, tile], frecv.at[turn, tile], toward_next
        else:
            dst, recv, tm = fbuf.at[1 - turn, tile], frecv.at[1 - turn, tile], toward_kept
        return remote(src, dst, send, recv, tm, col)

    def tip_copy(side):
        tm = t + step_size if side else t - step_size
        return remote(
            tsrc.at[side], tbuf.at[second, side], tsend.at[side], trecv.at[second, side], tm, c
        )

    def square_copy():
        return remote(zsrc, zbuf.at[turn], zsend, zrecv.at[turn], toward_next, c)

    group = lax.div(t, 4)

    def total_copy(other):
        place = tipbuf.at[group]
        return remote(
            place, place, bsend.at[other], brecv.at[group], lax.rem(t + other, blocks), c
        )

    def lanes_of(k):
        return pl.ds(pl.multiple_of(k * LANES, LANES), LANES)

    def exchange(level, k):
        if level == 1:
            arrived(stream.at[k, pl.ds(gather_at, LANES)], orecv.at[1, 0, k])
        spread(
            own_side(level, k, gather_at), peer.at[level], level, 0, k, lambda copy: copy.start()
        )
        if level == 1:
            arrived(stream.at[k, pl.ds(stream_at, LANES)], orecv.at[1, 1, k])
        pair_copy(level, k).start()

        @pl.when(kept_exists)
        def _():
            kept_copy(level, k).start()

        peer[level, y, k] = own_side(level, k, gather_at)[...]

    def pass_links(level, k):
        relay_when_here(peer.at[level], level, 0, k)

    def exchange_done(level, k):
        spread(
            own_side(level, k, gather_at), peer.at[level], level, 0, k,
            lambda copy: copy.wait_send(),
        )
        relay(peer.at[level], level, 0, k, lambda copy: copy.wait_send())
        pair_copy(level, k).wait_send()

        @pl.when(kept_exists)
        def _():
            kept_copy(level, k).wait_send()

    def collect(level, k):
        opposite_arrived(peer.at[level], level, 0, k)
        arrived(pair.at[level, k], precv.at[level, 0, chips, k])
        lanes = lanes_of(k)
        for slot in range(chips):
            high, low = split_two(peer[level, slot, k])
            to = slice(slot * LANES, (slot + 1) * LANES)
            col_high[to, lanes] = high
            col_low[to, lanes] = low
        for place, at in ((0, stream_at), (1, gather_at)):
            for index, value in (
                (q, own_side(level, k, at)[...]),
                (1 - q, pair[level, k, pl.ds(at, LANES), :]),
            ):
                high, low = split_two(value)
                to = pl.ds(pl.multiple_of((2 * place + index) * LANES, LANES), LANES)
                row_high[to, lanes] = high
                row_low[to, lanes] = low

    def kinds_of(level):
        near, far = slice(2 * LANES, 4 * LANES), slice(0, 2 * LANES)
        return ((0, near), (1, far)) if level == 0 else ((2, far),)

    def products_begin(level):
        collect(level, count - 2)
        for kind, rows in kinds_of(level):
            acc[min(kind, 1)] = dot_three(
                row_high[rows, :early], row_low[rows, :early],
                col_high[:, :early], col_low[:, :early],
            )

    def products_end(level):
        pass_links(level, count - 1)
        collect(level, count - 1)

        def finish(kind, rows):
            value = acc[min(kind, 1)] + dot_three(
                row_high[rows, early:], row_low[rows, early:],
                col_high[:, early:], col_low[:, early:],
            )
            for m in range(chips):
                for p in range(2):
                    gsrc[kind, p, m] = -value[
                        p * LANES : (p + 1) * LANES, m * LANES : (m + 1) * LANES
                    ]

        kinds = kinds_of(level)
        order = sorted(
            ((m, kind) for m in range(chips) for kind, _ in kinds),
            key=lambda item: 2 * item[0] + (3 if item[1] else 0),
        )
        finish(*kinds[0])
        finished = 1
        for m, kind in order:
            if finished < len(kinds) and kind == kinds[finished][0]:
                finish(*kinds[finished])
                finished += 1
            for p in range(2):
                product_copy(kind, m, p).start()

    @pl.when(phase != 0)
    def _():
        @pl.when(odd == 1)
        def _():
            keep = jnp.where(t < last, 1.0, 0.0)
            for k in range(count):
                fbuf[1, k] = coup[0, :, k * LANES : (k + 1) * LANES] * keep

        def send_arrow():
            abuf[c] = arrow[0]

            @pl.when(is_second)
            def _():
                for side in range(2):
                    arrived(tbuf.at[0, side], trecv.at[0, side])
                abuf[c] = abuf[c] + (tbuf[0, 0] + tbuf[0, 1])

            for other in range(1, cols):
                arrow_copy(other).start()

        def send_tile(k):
            dbuf[k, own_rows, :] = diag[0, :, lanes_of(k)]

            @pl.when(is_second)
            def _():
                near_wait(k)
                dbuf[k, own_rows, :] = dbuf[k, own_rows, :] + (nbuf[0, k] + nbuf[1, k])

            own_tile_copies(k, lambda copy: copy.start())

        send_tile(0)

        @pl.when(c >= 1)
        def _():
            send_tile(1)

        @pl.when(c == 0)
        def _():
            send_arrow()

        relay_near(0)
        relay_near(1)
        for first in (2, 3):
            if first < count:
                @pl.when(c >= first)
                def _():
                    send_tile(first)

        def step(k, carry):
            here = lanes_of(k)

            @pl.when((k >= 2) & (k + 2 < count))
            def _():
                relay_near(k + 2)

            @pl.when((k >= 3) & (k + 1 < count))
            def _():
                relay_opposite(k + 1)

            @pl.when(((k == 0) & (c != 0)) | ((k > 0) & (lax.rem(k, 2) != q)))
            def _():
                tile_arrived(k, k)

            start = dbuf[k, here, :] + accum[k, here, :]
            prepare_step(k, start - dot_nt(lhs[here, :], rhs[here, :]), work)
            factor_and_update(accum, work, lhs, rhs)

            @pl.when(k == 0)
            def _():
                relay_opposite(0)
                relay_opposite(1)
                for first in (2, 3):
                    if first < count:
                        relay_near(first)

            @pl.when(k == 1)
            def _():
                for first in (2, 3):
                    if first < count:
                        relay_opposite(first)

            @pl.when(k + 4 <= c)
            def _():
                send_tile(k + 4)

            @pl.when((c == k + 2) | ((k == 0) & (c == 1)))
            def _():
                send_arrow()

            for chip in range(chips):
                src = 2 * chip + 1 - q

                @pl.when(src > k)
                def _():
                    tile_arrived(src, k)

            @pl.when(k != c)
            def _():
                arrived(abuf.at[k], arecv.at[k])

            arrived(fbuf.at[0, k], frecv.at[0, k])

            @pl.when(is_second)
            def _():
                arrived(fbuf.at[1, k], frecv.at[1, k])

            source = jnp.concatenate([dbuf[k], fbuf[0, k], fbuf[1, k], abuf[k]], 0)
            solve_panel(k, accum[k] + source, done, work, lhs, rhs, nodes)

            def send_links():
                @pl.when(odd == 1)
                def _():
                    exchange(0, k)

                @pl.when(is_second)
                def _():
                    each_second(k, lambda copy: copy.start())

            send_links()

            @pl.when((k >= 1) & (odd == 1))
            def _():
                pass_links(0, k - 1)

            @pl.when((k >= 2) & (odd == 1))
            def _():
                collect(0, k - 2)

            return carry

        lax.fori_loop(0, count, step, 0)

        @pl.when(odd == 1)
        def _():
            products_begin(0)

        terms = jnp.zeros((tip_rows, 2 * LANES + tip_rows), jnp.float32)
        for k in range(count):
            terms = terms - dot_nt(
                wide_left(done[k, tip_top:, :]), wide_right(done[k, link_top:, :])
            )
        tsrc[0] = terms[:, :LANES]
        tsrc[1] = terms[:, LANES : 2 * LANES]
        square = jnp.concatenate(
            [terms[: tip_rows // 2, 2 * LANES :], terms[tip_rows // 2 :, 2 * LANES :]], 1
        )
        tip_copy(0).start()

        @pl.when(t + step_size <= last)
        def _():
            tip_copy(1).start()

        @pl.when(odd == 1)
        def _():
            zsrc[...] = square
            square_copy().start()
            products_end(0)

        @pl.when(is_second)
        def _():
            for slot in range(2):
                arrived(zbuf.at[slot], zrecv.at[slot])
            tipbuf[group] = square + (zbuf[0] + zbuf[1])
            for other in range(1, blocks):
                total_copy(other).start()

        for k in range(count):
            lanes = slice(k * LANES, (k + 1) * LANES)
            factor_out[0, :, lanes] = done[k, own_rows, :]
            for side in range(2):
                part = slice(link_top + side * LANES, link_top + (side + 1) * LANES)
                link_out[0, side, :, lanes] = done[k, part, :]
        arrow_out[0] = done[c, tip_top:, :]

        @pl.when(helps)
        def _():
            def help_step(k, carry):
                exchange(1, k)

                @pl.when(k >= 1)
                def _():
                    pass_links(1, k - 1)

                @pl.when(k >= 2)
                def _():
                    collect(1, k - 2)

                return carry

            lax.fori_loop(0, count, help_step, 0)
            products_begin(1)
            products_end(1)

        def drain(k, carry):
            own_tile_copies(k, lambda copy: copy.wait_send())
            near_forwards(k, lambda src, copy: copy.wait_send())
            ring_forward(k, lambda copy: copy.wait_send())
            opposite_forward(k, lambda src, copy: copy.wait_send())

            @pl.when((k > c) & is_second)
            def _():
                near_wait(k)

            @pl.when(is_second)
            def _():
                each_second(k, lambda copy: copy.wait_send())

            @pl.when(odd == 1)
            def _():
                exchange_done(0, k)

            @pl.when(helps)
            def _():
                exchange_done(1, k)

            return carry

        lax.fori_loop(0, count, drain, 0)
        for other in range(1, cols):
            arrow_copy(other).wait_send()
        tip_copy(0).wait_send()

        @pl.when(t + step_size <= last)
        def _():
            tip_copy(1).wait_send()

        @pl.when(odd == 1)
        def _():
            square_copy().wait_send()
            for kind in range(2):
                for m in range(chips):
                    for p in range(2):
                        product_copy(kind, m, p).wait_send()

        @pl.when(helps)
        def _():
            for m in range(chips):
                for p in range(2):
                    product_copy(2, m, p).wait_send()

        @pl.when(is_second)
        def _():
            for other in range(1, blocks):
                total_copy(other).wait_send()

    @pl.when(phase == 0)
    def _():
        @pl.when(t == 0)
        def _():
            for level in range(2):
                tbuf[level, 1] = jnp.zeros(tbuf.shape[2:], jnp.float32)
            fbuf[0] = jnp.zeros(fbuf.shape[1:], jnp.float32)
            for ref in (kept_row_high, kept_row_low, kept_col_high, kept_col_low):
                ref[1] = jnp.zeros(ref.shape[1:], jnp.bfloat16)

        def each_side(action):
            action(0)

            @pl.when(t > 0)
            def _():
                action(1)

        def kept_pass(level, side, k):
            relay_when_here(kept_peer.at[level, side], level, side, k)

        def kept_collect(level, side, k):
            opposite_arrived(kept_peer.at[level, side], level, side, k)
            arrived(kept_pair.at[level, side, k], precv.at[level, side, chips, k])
            lanes = lanes_of(k)
            for slot in range(chips):
                high, low = split_two(kept_peer[level, side, slot, k])
                to = slice(slot * LANES, (slot + 1) * LANES)
                kept_col_high[side, to, lanes] = high
                kept_col_low[side, to, lanes] = low
            for index, value in (
                (q, kept_own[level, side, k]), (1 - q, kept_pair[level, side, k])
            ):
                high, low = split_two(value)
                to = pl.ds(pl.multiple_of(index * LANES, LANES), LANES)
                kept_row_high[side, to, lanes] = high
                kept_row_low[side, to, lanes] = low

        def kept_products(lanes):
            value = None
            for side in range(2):
                term = dot_three(
                    kept_row_high[side, :, lanes], kept_row_low[side, :, lanes],
                    kept_col_high[side, :, lanes], kept_col_low[side, :, lanes],
                )
                value = term if value is None else value + term
            return value

        for level in range(2):
            def kept_step(k, carry):
                def take(side):
                    arrived(kept_own.at[level, side, k], orecv.at[level, side, k])
                    spread(
                        kept_own.at[level, side, k], kept_peer.at[level, side], level, side, k,
                        lambda copy: copy.start(),
                    )
                    kept_pair_copy(level, side, k).start()
                    kept_peer[level, side, y, k] = kept_own[level, side, k]

                each_side(take)

                @pl.when(k >= 1)
                def _():
                    each_side(lambda side: kept_pass(level, side, k - 1))

                @pl.when(k >= 2)
                def _():
                    each_side(lambda side: kept_collect(level, side, k - 2))

                return carry

            lax.fori_loop(0, count, kept_step, 0)
            each_side(lambda side: kept_collect(level, side, count - 2))
            partial_sum = kept_products(slice(0, early))
            if level == 0:
                kept_acc[...] = partial_sum
            else:
                kept_acc[...] = kept_acc[...] + partial_sum
            each_side(lambda side: kept_pass(level, side, count - 1))
            each_side(lambda side: kept_collect(level, side, count - 1))
            kept_acc[...] = kept_acc[...] + kept_products(slice(early, nodes))

        def swap_copy():
            return remote(swap_src, swap_dst, ssend, srecv, t, sibling)

        other_rows = pl.ds(pl.multiple_of((1 - q) * LANES, LANES), LANES)
        for m in range(chips):
            swap_src[m] = kept_acc[other_rows, m * LANES : (m + 1) * LANES]
        swap_copy().start()
        my_rows = pl.ds(pl.multiple_of(q * LANES, LANES), LANES)
        for m in range(chips):
            lanes = lanes_of(2 * m + q)
            factor_out[0, :, lanes] = (
                diag[0, :, lanes] - kept_acc[my_rows, m * LANES : (m + 1) * LANES]
            )

        for level in range(2):
            each_side(lambda side: arrived(tbuf.at[level, side], trecv.at[level, side]))
        arrow_out[0] = arrow[0] + (
            (tbuf[0, 0] + tbuf[0, 1]) + (tbuf[1, 0] + tbuf[1, 1])
        )
        arrived(swap_dst, srecv)
        for m in range(chips):
            lanes = lanes_of(2 * m + 1 - q)
            factor_out[0, :, lanes] = diag[0, :, lanes] - swap_dst[m]
        for k in range(count):
            lanes = slice(k * LANES, (k + 1) * LANES)
            arrived(fbuf.at[1, k], frecv.at[1, k])
            link_out[0, 1, :, lanes] = fbuf[1, k]

            @pl.when(t > 0)
            def _():
                arrived(fbuf.at[0, k], frecv.at[0, k])

            link_out[0, 0, :, lanes] = fbuf[0, k]

        swap_copy().wait_send()

        def kept_drain(k, carry):
            def wait_all(side):
                for level in range(2):
                    spread(
                        kept_own.at[level, side, k], kept_peer.at[level, side], level, side, k,
                        lambda copy: copy.wait_send(),
                    )
                    relay(
                        kept_peer.at[level, side], level, side, k,
                        lambda copy: copy.wait_send(),
                    )
                    kept_pair_copy(level, side, k).wait_send()

            each_side(wait_all)
            return carry

        lax.fori_loop(0, count, kept_drain, 0)

    @pl.when(odd == 0)
    def _():
        for k in range(count):
            coupling_copy(k).wait_send()

    total = tip[...]
    for index in range(blocks // 4):
        @pl.when(t != 4 * index + 2)
        def _():
            arrived(tipbuf.at[index], brecv.at[index])

        part = tipbuf[index]
        total = total + jnp.concatenate([part[:, :tip_rows], part[:, tip_rows:]], 0)
    tip_out[...] = total


def publish_kernel(*refs):
    half = (len(refs) - 2) // 3
    sources, targets, held = refs[:half], refs[half : 2 * half], refs[2 * half : 3 * half]
    reads, writes = refs[-2:]
    pieces = []
    for index, source in enumerate(sources):
        rows = source.shape[-2]
        leading = [(0,)] if len(source.shape) == 3 else [(0, 0), (0, 1)]
        for lead in leading if len(source.shape) > 2 else [()]:
            for first in range(0, rows, 64):
                pieces.append((index, lead + (pl.ds(first, 64),)))
    into = [
        pltpu.make_async_copy(sources[i].at[at], held[i].at[at], reads.at[n])
        for n, (i, at) in enumerate(pieces)
    ]
    out = [
        pltpu.make_async_copy(held[i].at[at], targets[i].at[at], writes.at[n])
        for n, (i, at) in enumerate(pieces)
    ]
    for copy in into:
        copy.start()
    for read, write in zip(into, out):
        read.wait()
        write.start()
    for copy in out:
        copy.wait()


def publish(results):
    return pl.pallas_call(
        publish_kernel,
        out_shape=tuple(jax.ShapeDtypeStruct(r.shape, r.dtype) for r in results),
        in_specs=[pl.BlockSpec(memory_space=pl.ANY)] * len(results),
        out_specs=(pl.BlockSpec(memory_space=pl.ANY),) * len(results),
        scratch_shapes=[pltpu.VMEM(r.shape, r.dtype) for r in results]
        + [pltpu.SemaphoreType.DMA((8,)), pltpu.SemaphoreType.DMA((8,))],
        name="publish",
    )(*results)


def body(diagonal, coupling, arrowhead, tip_matrix):
    cols = lax.axis_size("col")
    blocks = lax.axis_size("tm")
    chips = cols // 2
    nodes = diagonal.shape[2]
    tip_rows = tip_matrix.shape[0]
    total = nodes + 2 * LANES + tip_rows
    count = nodes // LANES
    half = chips * LANES
    f32, bf16, dma = jnp.float32, jnp.bfloat16, pltpu.SemaphoreType.DMA
    tile = (LANES, LANES)
    scratch = [
        pltpu.VMEM((count, total, LANES), f32),
        pltpu.VMEM((count, total, LANES), f32),
        pltpu.VMEM((count, nodes, LANES), f32),
        pltpu.VMEM((2, count) + tile, f32),
        pltpu.VMEM((2, count) + tile, f32),
        pltpu.VMEM((2, chips, count) + tile, f32),
        pltpu.VMEM((2, count, 2 * LANES, LANES), f32),
        pltpu.VMEM((count, 2 * LANES, LANES), f32),
        pltpu.VMEM((3, 2, chips) + tile, f32),
        pltpu.VMEM((2, 2 * LANES, half), f32),
        pltpu.VMEM((2, 2, chips, count) + tile, f32),
        pltpu.VMEM((2, 2, count) + tile, f32),
        pltpu.VMEM((2, 2, count) + tile, f32),
        pltpu.VMEM((2 * LANES, half), f32),
        pltpu.VMEM((chips,) + tile, f32),
        pltpu.VMEM((chips,) + tile, f32),
        pltpu.VMEM((cols, tip_rows, LANES), f32),
        pltpu.VMEM((2, 2, tip_rows, LANES), f32),
        pltpu.VMEM((2, tip_rows, LANES), f32),
        pltpu.VMEM((2, tip_rows // 2, LANES), f32),
        pltpu.VMEM((tip_rows // 2, LANES), f32),
        pltpu.VMEM((blocks // 4, tip_rows // 2, LANES), f32),
        pltpu.VMEM((LANES, 2 * LANES), f32),
        pltpu.VMEM((total, 3 * LANES), bf16),
        pltpu.VMEM((nodes, 3 * LANES), bf16),
        pltpu.VMEM((4 * LANES, nodes), bf16),
        pltpu.VMEM((4 * LANES, nodes), bf16),
        pltpu.VMEM((half, nodes), bf16),
        pltpu.VMEM((half, nodes), bf16),
        pltpu.VMEM((2, 2 * LANES, nodes), bf16),
        pltpu.VMEM((2, 2 * LANES, nodes), bf16),
        pltpu.VMEM((2, half, nodes), bf16),
        pltpu.VMEM((2, half, nodes), bf16),
        dma((11, count)),
        dma((cols, count)),
        dma((cols,)),
        dma((cols,)),
        dma((2, 2, 4, count)),
        dma((2, 2, chips + 1, count)),
        dma((2, 2, count)),
        dma((count,)),
        dma((2, count)),
        dma((3, 2, chips)),
        dma((2, count)),
        dma((2,)),
        dma((2, 2)),
        dma,
        dma((2,)),
        dma((blocks,)),
        dma((blocks // 4,)),
        dma,
        dma,
    ]

    def call(*refs):
        kernel(chips, tip_rows, blocks, *refs)

    arrow_t = jnp.swapaxes(arrowhead, 1, 2)
    results = pl.pallas_call(
        call,
        out_shape=(
            jax.ShapeDtypeStruct(diagonal.shape, f32),
            jax.ShapeDtypeStruct((1, 2) + diagonal.shape[1:], f32),
            jax.ShapeDtypeStruct(arrow_t.shape, f32),
            jax.ShapeDtypeStruct(tip_matrix.shape, f32),
        ),
        in_specs=[pl.BlockSpec(memory_space=pltpu.VMEM)] * 4,
        out_specs=(pl.BlockSpec(memory_space=pltpu.VMEM),) * 4,
        scratch_shapes=scratch,
        compiler_params=pltpu.CompilerParams(
            collective_id=0, has_side_effects=True, vmem_limit_bytes=60 * 1024 * 1024
        ),
        name="cyclic_reduction",
    )(diagonal, coupling, arrow_t, tip_matrix)
    factors, links, arrows, reduced = publish(results)
    return factors, links, jnp.swapaxes(arrows, 1, 2), reduced


def solution(mesh):
    in_specs = (P("tm", "col", None), P("tm", "col", None), P("tm", "col", None), P())
    out_specs = (P("tm", "col", None), P("tm", None, "col", None), P("tm", "col", None), P())
    return jax.shard_map(body, mesh=mesh, in_specs=in_specs, out_specs=out_specs, check_vma=False)
```

```python
import jax
import jax.numpy as jnp
from jax import lax
from jax.experimental import pallas as pl
from jax.experimental.pallas import tpu as pltpu
from jax.sharding import PartitionSpec as P

LANES = 128
PANEL = 32
SPREAD = 16


def split_two(value):
    high = value.astype(jnp.bfloat16)
    low = (value - high.astype(jnp.float32)).astype(jnp.bfloat16)
    return high, low


def split_three(value):
    high = value.astype(jnp.bfloat16)
    rest = value - high.astype(jnp.float32)
    middle = rest.astype(jnp.bfloat16)
    low = (rest - middle.astype(jnp.float32)).astype(jnp.bfloat16)
    return high, middle, low


def spread_row(vec, row):
    return jnp.broadcast_to(vec[row : row + 1, :], (8, LANES))


def spread_lane(vec, lane):
    return jnp.take_along_axis(vec, jnp.full(vec.shape, lane, jnp.int32), axis=1)


def factor_tile(work, fill=lambda part: None):
    sub = lax.broadcasted_iota(jnp.int32, (8, LANES), 0)
    groups = PANEL // 8
    for panel in range(LANES // PANEL):
        first = panel * PANEL
        spans = [slice(first + 8 * g, first + 8 * g + 8) for g in range(groups)]
        left = [work[span, :LANES] for span in spans]
        right = [work[span, LANES:] for span in spans]
        pivots = [None] * groups
        pivot = None
        for r in range(PANEL):
            if r % SPREAD == 0:
                cols = {
                    c: [
                        spread_lane(left[g], first + c) if g >= c // 8 else None
                        for g in range(groups)
                    ]
                    for c in range(r, r + SPREAD)
                }
                fill((first + r) // SPREAD)
            h, q = r // 8, r % 8
            if r % SPREAD == 0:
                pivot = spread_row(cols[r][h], q)
            pivots[h] = pivot if q == 0 else jnp.where(sub == q, pivot, pivots[h])
            if r == PANEL - 1:
                break
            inverse = 1.0 / pivot
            if (r + 1) % SPREAD:
                h_next, q_next = (r + 1) // 8, (r + 1) % 8
                entry = spread_row(cols[r][h_next], q_next)
                pivot = spread_row(cols[r + 1][h_next], q_next) - (entry * inverse) * entry
            coef, masked = [None] * groups, [None] * groups
            for g in range(h, groups):
                coef[g] = cols[r][g] * inverse
                masked[g] = jnp.where(sub > q, coef[g], 0.0) if g == h else coef[g]
            for c in range(r + 1, r - r % SPREAD + SPREAD):
                entry = spread_row(cols[r][c // 8], c % 8)
                for g in range(c // 8, groups):
                    cols[c][g] = cols[c][g] - coef[g] * entry
            left_row, right_row = spread_row(left[h], q), spread_row(right[h], q)
            for g in range(h, groups):
                if g == h and q == 7:
                    continue
                left[g] = left[g] - masked[g] * left_row
                right[g] = right[g] - masked[g] * right_row
        rows = []
        for g in range(groups):
            scale = lax.rsqrt(pivots[g])
            rows.append(jnp.concatenate([left[g] * scale, right[g] * scale], 1))
        rows = jnp.concatenate(rows, 0)
        work[first : first + PANEL, :] = rows
        if first + PANEL < LANES:
            a, b, c = split_three(rows)
            lhs = jnp.concatenate([a, a, b, a, b, c], 0)[:, :LANES]
            rhs = jnp.concatenate([a, b, a, c, b, a], 0)
            update = lax.dot_general(
                lhs, rhs, (((0,), (0,)), ((), ())), preferred_element_type=jnp.float32
            )
            n = first + PANEL
            work[n:, :] = work[n:, :] - update[n:, :]


def dot_nt(left, right):
    return lax.dot_general(
        left, right, (((1,), (1,)), ((), ())), preferred_element_type=jnp.float32
    )


def wide_left(value):
    high, low = split_two(value)
    return jnp.concatenate([high, high, low], 1)


def wide_right(value):
    high, low = split_two(value)
    return jnp.concatenate([high, low, high], 1)


def prepare_step(k, start, work):
    row_id = lax.broadcasted_iota(jnp.int32, (LANES, LANES), 0)
    col_id = lax.broadcasted_iota(jnp.int32, (LANES, LANES), 1)
    work[:, :LANES] = start
    work[:, LANES:] = jnp.where(row_id == col_id, 1.0, 0.0)


def factor_and_update(acc, work, lhs, rhs):
    count, total, _ = acc.shape

    def fill(panel):
        pair, part = panel // 2, panel % 2
        if pair >= count // 2:
            return
        top = 2 * LANES * pair
        middle = top + (total - top) // 32 * 16
        rows = slice(top, middle) if part == 0 else slice(middle, total)
        update = dot_nt(lhs[rows, :], rhs[top : top + 2 * LANES, :])
        acc[2 * pair, rows, :] = acc[2 * pair, rows, :] - update[:, :LANES]
        acc[2 * pair + 1, rows, :] = acc[2 * pair + 1, rows, :] - update[:, LANES:]

    factor_tile(work, fill)


def solve_panel(k, column, done, work, lhs, rhs, nodes):
    total = column.shape[0]
    row_id = lax.broadcasted_iota(jnp.int32, (LANES, LANES), 0)
    col_id = lax.broadcasted_iota(jnp.int32, (LANES, LANES), 1)
    here = pl.ds(pl.multiple_of(k * LANES, LANES), LANES)
    solved = dot_nt(wide_left(column), wide_right(work[:, LANES:]))
    rows = lax.broadcasted_iota(jnp.int32, (total, LANES), 0)
    solved = jnp.where(rows >= (k + 1) * LANES, solved, 0.0)
    done[k] = solved
    done[k, here, :] = jnp.where(row_id <= col_id, work[:, :LANES], 0.0).T
    high, low = split_two(solved)
    lhs[...] = jnp.concatenate([high, high, low], 1)
    rhs[...] = jnp.concatenate([high[:nodes], low[:nodes], high[:nodes]], 1)


MESH = pl.DeviceIdType.MESH


def dot_three(left_high, left_low, right_high, right_low):
    value = dot_nt(left_high, right_high)
    value = value + dot_nt(left_high, right_low)
    return value + dot_nt(left_low, right_high)


def kernel(
    chips, tip_rows, blocks,
    diag, coup, arrow, tip,
    factor_out, link_out, arrow_out, tip_out,
    done, accum, dbuf, fbuf, nbuf, peer, pair, stream, gsrc, acc, kept_peer, kept_pair, kept_own,
    kept_acc, swap_src, swap_dst, abuf, tbuf, tsrc, zbuf, zsrc, tipbuf,
    work, lhs, rhs, row_high, row_low, col_high, col_low,
    kept_row_high, kept_row_low, kept_col_high, kept_col_low,
    dsend, drecv, asend, arecv, psend, precv, orecv, csend, frecv, gsend, nrecv,
    tsend, trecv, zsend, zrecv, bsend, brecv, ssend, srecv,
):
    t = lax.axis_index("tm")
    c = lax.axis_index("col")
    y, q = lax.div(c, 2), lax.rem(c, 2)
    sibling = c + 1 - 2 * q
    cols = 2 * chips
    count = cols
    nodes = count * LANES
    link_top, tip_top = nodes, nodes + 2 * LANES
    phase = lax.rem(t, 4)
    odd = lax.rem(t, 2)
    second = 1 - odd
    step_size = 2 - odd
    is_second = phase == 2
    last = blocks - 1
    early = nodes - LANES
    toward_next, toward_kept = t + 2 - phase, t - 2 + phase
    turn = lax.div(phase, 2)
    gather_at = pl.multiple_of(LANES * (1 - turn), LANES)
    stream_at = pl.multiple_of(LANES * turn, LANES)
    kept_exists = toward_kept <= last
    helps = (odd == 1) & kept_exists
    own_rows = pl.ds(pl.multiple_of(c * LANES, LANES), LANES)

    def remote(src, dst, send, recv, tm, col):
        return pltpu.make_async_remote_copy(
            src_ref=src, dst_ref=dst, send_sem=send, recv_sem=recv,
            device_id={"tm": tm, "col": col}, device_id_type=MESH,
        )

    def arrived(dst, recv):
        remote(dst, dst, recv, recv, t, sibling).wait_recv()

    barrier = pltpu.get_barrier_semaphore()

    def greet(tm, col):
        pl.semaphore_signal(
            barrier, inc=1, device_id={"tm": tm, "col": col}, device_id_type=MESH
        )

    for other in range(1, cols):
        greet(t, lax.rem(c + other, cols))
    for other in range(1, blocks):
        greet(lax.rem(t + other, blocks), c)
    for other in (1, blocks - 1):
        greet(lax.rem(t + other, blocks), sibling)
    for k in range(count):
        accum[k] = jnp.zeros(accum.shape[1:], jnp.float32)
    lhs[...] = jnp.zeros(lhs.shape, jnp.bfloat16)
    rhs[...] = jnp.zeros(rhs.shape, jnp.bfloat16)

    @pl.when(odd == 1)
    def _():
        keep = jnp.where(t < last, 1.0, 0.0)
        for k in range(count):
            fbuf[1, k] = coup[0, :, k * LANES : (k + 1) * LANES] * keep

    pl.semaphore_wait(barrier, cols - 1 + blocks - 1 + 2)

    def coupling_copy(k):
        return remote(
            coup.at[0, :, pl.ds(k * LANES, LANES)], fbuf.at[0, k],
            csend.at[k], frecv.at[0, k], t + 1, c,
        )

    @pl.when(odd == 0)
    def _():
        for k in range(count):
            coupling_copy(k).start()

    def peer_of(other):
        return lax.rem(c + other, cols)

    def same_core(other):
        return 2 * lax.rem(y + other, chips) + q

    hops = [1, chips - 1] if chips > 2 else list(range(1, chips))
    rings = chips == 4

    def relay_ends(k):
        turn_at = 1 - 2 * lax.rem(y + k, 2)
        return lax.rem(y + turn_at + chips, chips), lax.rem(y - turn_at + chips, chips)

    def tile_copy(src_col, k, slot, target):
        place = dbuf.at[k, pl.ds(pl.multiple_of(src_col * LANES, LANES), LANES)]
        return remote(place, place, dsend.at[slot, k], drecv.at[src_col, k], t, target)

    def tile_arrived(src_col, k):
        place = dbuf.at[k, pl.ds(pl.multiple_of(src_col * LANES, LANES), LANES)]
        arrived(place, drecv.at[src_col, k])

    def by_ring(src, k):
        return (src > k) | ((src == k) & (k > 0))

    def own_tile_copies(k, action):
        @pl.when((c == k) & (k == 0))
        def _():
            for other in range(1, cols):
                action(tile_copy(c, k, other - 1, peer_of(other)))

        @pl.when(by_ring(c, k))
        def _():
            action(tile_copy(c, k, 0, sibling))
            for i, hop in enumerate(hops):
                action(tile_copy(c, k, 1 + i, same_core(hop)))

    def near_forwards(k, action):
        for i, hop in enumerate(hops):
            src = same_core(hop)

            @pl.when(by_ring(src, k))
            def _():
                action(src, tile_copy(src, k, 7 + i, sibling))

    def ring_forward(k, action):
        if rings:
            source, target = relay_ends(k)
            src = 2 * source + q

            @pl.when(by_ring(src, k))
            def _():
                action(tile_copy(src, k, 10, 2 * target + q))

    def opposite_forward(k, action):
        if rings:
            src = same_core(2)

            @pl.when(by_ring(src, k))
            def _():
                action(src, tile_copy(src, k, 9, sibling))

    def pass_on(src, k, copy):
        tile_arrived(src, k)
        copy.start()

    def relay_near(k):
        near_forwards(k, lambda src, copy: pass_on(src, k, copy))
        ring_forward(k, lambda copy: copy.start())

    def relay_opposite(k):
        opposite_forward(k, lambda src, copy: pass_on(src, k, copy))

    def arrow_copy(other):
        return remote(
            abuf.at[c], abuf.at[c], asend.at[other], arecv.at[c], t, peer_of(other)
        )

    def own_links(level, k):
        return done.at[k, pl.ds(link_top, 2 * LANES)] if level == 0 else stream.at[k]

    def own_side(level, k, at):
        if level == 0:
            return done.at[k, pl.ds(pl.multiple_of(link_top + at, LANES), LANES)]
        return stream.at[k, pl.ds(at, LANES)]

    def spread(src, place, level, side, k, action):
        for i, hop in enumerate(hops):
            action(remote(
                src, place.at[y, k], psend.at[level, side, 1 + i, k],
                precv.at[level, side, y, k], t, same_core(hop),
            ))
        if rings:
            @pl.when(k == count - 1)
            def _():
                action(remote(
                    src, place.at[y, k], psend.at[level, side, 3, k],
                    precv.at[level, side, y, k], t, same_core(2),
                ))

    def relay(place, level, side, k, action):
        if rings:
            @pl.when(k < count - 1)
            def _():
                source, target = relay_ends(k)
                tile = place.at[source, k]
                action(remote(
                    tile, tile, psend.at[level, side, 3, k],
                    precv.at[level, side, source, k], t, 2 * target + q,
                ))

    def relay_when_here(place, level, side, k):
        for hop in hops:
            slot = lax.rem(y + hop, chips)
            arrived(place.at[slot, k], precv.at[level, side, slot, k])
        relay(place, level, side, k, lambda copy: copy.start())

    def opposite_arrived(place, level, side, k):
        if rings:
            slot = lax.rem(y + 2, chips)
            arrived(place.at[slot, k], precv.at[level, side, slot, k])

    def pair_copy(level, k):
        return remote(
            own_links(level, k), pair.at[level, k],
            psend.at[level, 0, 0, k], precv.at[level, 0, chips, k], t, sibling,
        )

    def kept_copy(level, k):
        return remote(
            own_side(level, k, stream_at), kept_own.at[level, turn, k],
            psend.at[level, 1, 0, k], orecv.at[level, turn, k], toward_kept, c,
        )

    def helper_copy(k, side, part):
        at = LANES * (1 - side if part == 0 else side)
        return remote(
            done.at[k, pl.ds(link_top + at, LANES)], stream.at[k, pl.ds(at, LANES)],
            psend.at[0, part, side, k], orecv.at[1, part, k], t - 1 + 2 * side, c,
        )

    def each_second(k, action):
        for part, side in ((0, 0), (0, 1), (1, 0), (1, 1)):
            @pl.when(t + 2 * side <= last)
            def _():
                action(helper_copy(k, side, part))

    def kept_pair_copy(level, side, k):
        return remote(
            kept_own.at[level, side, k], kept_pair.at[level, side, k],
            psend.at[level, side, 0, k], precv.at[level, side, chips, k], t, sibling,
        )

    def near_wait(k):
        for side in range(2):
            arrived(nbuf.at[side, k], nrecv.at[side, k])

    def product_copy(kind, m, p):
        tile = 2 * m + q
        src, send, col = gsrc.at[kind, p, m], gsend.at[kind, p, m], 2 * y + p
        if kind == 0:
            dst, recv, tm = nbuf.at[1 - turn, tile], nrecv.at[1 - turn, tile], toward_next
        elif kind == 1:
            dst, recv, tm = fbuf.at[turn, tile], frecv.at[turn, tile], toward_next
        else:
            dst, recv, tm = fbuf.at[1 - turn, tile], frecv.at[1 - turn, tile], toward_kept
        return remote(src, dst, send, recv, tm, col)

    def tip_copy(side):
        tm = t + step_size if side else t - step_size
        return remote(
            tsrc.at[side], tbuf.at[second, side], tsend.at[side], trecv.at[second, side], tm, c
        )

    def square_copy():
        return remote(zsrc, zbuf.at[turn], zsend, zrecv.at[turn], toward_next, c)

    group = lax.div(t, 4)

    def total_copy(other):
        place = tipbuf.at[group]
        return remote(
            place, place, bsend.at[other], brecv.at[group], lax.rem(t + other, blocks), c
        )

    def lanes_of(k):
        return pl.ds(pl.multiple_of(k * LANES, LANES), LANES)

    def exchange(level, k):
        if level == 1:
            arrived(stream.at[k, pl.ds(gather_at, LANES)], orecv.at[1, 0, k])
        spread(
            own_side(level, k, gather_at), peer.at[level], level, 0, k, lambda copy: copy.start()
        )
        if level == 1:
            arrived(stream.at[k, pl.ds(stream_at, LANES)], orecv.at[1, 1, k])
        pair_copy(level, k).start()

        @pl.when(kept_exists)
        def _():
            kept_copy(level, k).start()

        peer[level, y, k] = own_side(level, k, gather_at)[...]

    def pass_links(level, k):
        relay_when_here(peer.at[level], level, 0, k)

    def exchange_done(level, k):
        spread(
            own_side(level, k, gather_at), peer.at[level], level, 0, k,
            lambda copy: copy.wait_send(),
        )
        relay(peer.at[level], level, 0, k, lambda copy: copy.wait_send())
        pair_copy(level, k).wait_send()

        @pl.when(kept_exists)
        def _():
            kept_copy(level, k).wait_send()

    def collect(level, k):
        opposite_arrived(peer.at[level], level, 0, k)
        arrived(pair.at[level, k], precv.at[level, 0, chips, k])
        lanes = lanes_of(k)
        for slot in range(chips):
            high, low = split_two(peer[level, slot, k])
            to = slice(slot * LANES, (slot + 1) * LANES)
            col_high[to, lanes] = high
            col_low[to, lanes] = low
        for place, at in ((0, stream_at), (1, gather_at)):
            for index, value in (
                (q, own_side(level, k, at)[...]),
                (1 - q, pair[level, k, pl.ds(at, LANES), :]),
            ):
                high, low = split_two(value)
                to = pl.ds(pl.multiple_of((2 * place + index) * LANES, LANES), LANES)
                row_high[to, lanes] = high
                row_low[to, lanes] = low

    def kinds_of(level):
        near, far = slice(2 * LANES, 4 * LANES), slice(0, 2 * LANES)
        return ((0, near), (1, far)) if level == 0 else ((2, far),)

    def products_begin(level):
        collect(level, count - 2)
        for kind, rows in kinds_of(level):
            acc[min(kind, 1)] = dot_three(
                row_high[rows, :early], row_low[rows, :early],
                col_high[:, :early], col_low[:, :early],
            )

    def products_end(level):
        pass_links(level, count - 1)
        collect(level, count - 1)

        def finish(kind, rows):
            value = acc[min(kind, 1)] + dot_three(
                row_high[rows, early:], row_low[rows, early:],
                col_high[:, early:], col_low[:, early:],
            )
            for m in range(chips):
                for p in range(2):
                    gsrc[kind, p, m] = -value[
                        p * LANES : (p + 1) * LANES, m * LANES : (m + 1) * LANES
                    ]

        kinds = kinds_of(level)
        order = sorted(
            ((m, kind) for m in range(chips) for kind, _ in kinds),
            key=lambda item: 2 * item[0] + (3 if item[1] else 0),
        )
        finish(*kinds[0])
        finished = 1
        for m, kind in order:
            if finished < len(kinds) and kind == kinds[finished][0]:
                finish(*kinds[finished])
                finished += 1
            for p in range(2):
                product_copy(kind, m, p).start()

    @pl.when(phase != 0)
    def _():
        def send_arrow():
            abuf[c] = arrow[0]

            @pl.when(is_second)
            def _():
                for side in range(2):
                    arrived(tbuf.at[0, side], trecv.at[0, side])
                abuf[c] = abuf[c] + (tbuf[0, 0] + tbuf[0, 1])

            for other in range(1, cols):
                arrow_copy(other).start()

        def send_tile(k):
            dbuf[k, own_rows, :] = diag[0, :, lanes_of(k)]

            @pl.when(is_second)
            def _():
                near_wait(k)
                dbuf[k, own_rows, :] = dbuf[k, own_rows, :] + (nbuf[0, k] + nbuf[1, k])

            own_tile_copies(k, lambda copy: copy.start())

        send_tile(0)

        @pl.when(c >= 1)
        def _():
            send_tile(1)

        @pl.when(c == 0)
        def _():
            send_arrow()

        relay_near(0)
        relay_near(1)
        for first in (2, 3):
            if first < count:
                @pl.when(c >= first)
                def _():
                    send_tile(first)

        def step(k, carry):
            here = lanes_of(k)

            @pl.when((k >= 2) & (k + 2 < count))
            def _():
                relay_near(k + 2)

            @pl.when((k >= 3) & (k + 1 < count))
            def _():
                relay_opposite(k + 1)

            @pl.when(((k == 0) & (c != 0)) | ((k > 0) & (lax.rem(k, 2) != q)))
            def _():
                tile_arrived(k, k)

            start = dbuf[k, here, :] + accum[k, here, :]
            prepare_step(k, start - dot_nt(lhs[here, :], rhs[here, :]), work)
            factor_and_update(accum, work, lhs, rhs)

            @pl.when(k == 0)
            def _():
                relay_opposite(0)
                relay_opposite(1)
                for first in (2, 3):
                    if first < count:
                        relay_near(first)

            @pl.when(k == 1)
            def _():
                for first in (2, 3):
                    if first < count:
                        relay_opposite(first)

            @pl.when(k + 4 <= c)
            def _():
                send_tile(k + 4)

            @pl.when((c == k + 2) | ((k == 0) & (c == 1)))
            def _():
                send_arrow()

            for chip in range(chips):
                src = 2 * chip + 1 - q

                @pl.when(src > k)
                def _():
                    tile_arrived(src, k)

            @pl.when(k != c)
            def _():
                arrived(abuf.at[k], arecv.at[k])

            arrived(fbuf.at[0, k], frecv.at[0, k])

            @pl.when(is_second)
            def _():
                arrived(fbuf.at[1, k], frecv.at[1, k])

            source = jnp.concatenate([dbuf[k], fbuf[0, k], fbuf[1, k], abuf[k]], 0)
            solve_panel(k, accum[k] + source, done, work, lhs, rhs, nodes)

            def send_links():
                @pl.when(odd == 1)
                def _():
                    exchange(0, k)

                @pl.when(is_second)
                def _():
                    each_second(k, lambda copy: copy.start())

            send_links()

            @pl.when((k >= 1) & (odd == 1))
            def _():
                pass_links(0, k - 1)

            @pl.when((k >= 2) & (odd == 1))
            def _():
                collect(0, k - 2)

            return carry

        lax.fori_loop(0, count, step, 0)

        @pl.when(odd == 1)
        def _():
            products_begin(0)

        terms = jnp.zeros((tip_rows, 2 * LANES + tip_rows), jnp.float32)
        for k in range(count):
            terms = terms - dot_nt(
                wide_left(done[k, tip_top:, :]), wide_right(done[k, link_top:, :])
            )
        tsrc[0] = terms[:, :LANES]
        tsrc[1] = terms[:, LANES : 2 * LANES]
        square = jnp.concatenate(
            [terms[: tip_rows // 2, 2 * LANES :], terms[tip_rows // 2 :, 2 * LANES :]], 1
        )
        tip_copy(0).start()

        @pl.when(t + step_size <= last)
        def _():
            tip_copy(1).start()

        @pl.when(odd == 1)
        def _():
            zsrc[...] = square
            square_copy().start()
            products_end(0)

        @pl.when(is_second)
        def _():
            for slot in range(2):
                arrived(zbuf.at[slot], zrecv.at[slot])
            tipbuf[group] = square + (zbuf[0] + zbuf[1])
            for other in range(1, blocks):
                total_copy(other).start()

        for k in range(count):
            lanes = slice(k * LANES, (k + 1) * LANES)
            factor_out[0, :, lanes] = done[k, own_rows, :]
            for side in range(2):
                part = slice(link_top + side * LANES, link_top + (side + 1) * LANES)
                link_out[0, side, :, lanes] = done[k, part, :]
        arrow_out[0] = done[c, tip_top:, :]

        @pl.when(helps)
        def _():
            def help_step(k, carry):
                exchange(1, k)

                @pl.when(k >= 1)
                def _():
                    pass_links(1, k - 1)

                @pl.when(k >= 2)
                def _():
                    collect(1, k - 2)

                return carry

            lax.fori_loop(0, count, help_step, 0)
            products_begin(1)
            products_end(1)

        def drain(k, carry):
            own_tile_copies(k, lambda copy: copy.wait_send())
            near_forwards(k, lambda src, copy: copy.wait_send())
            ring_forward(k, lambda copy: copy.wait_send())
            opposite_forward(k, lambda src, copy: copy.wait_send())

            @pl.when((k > c) & is_second)
            def _():
                near_wait(k)

            @pl.when(is_second)
            def _():
                each_second(k, lambda copy: copy.wait_send())

            @pl.when(odd == 1)
            def _():
                exchange_done(0, k)

            @pl.when(helps)
            def _():
                exchange_done(1, k)

            return carry

        lax.fori_loop(0, count, drain, 0)
        for other in range(1, cols):
            arrow_copy(other).wait_send()
        tip_copy(0).wait_send()

        @pl.when(t + step_size <= last)
        def _():
            tip_copy(1).wait_send()

        @pl.when(odd == 1)
        def _():
            square_copy().wait_send()
            for kind in range(2):
                for m in range(chips):
                    for p in range(2):
                        product_copy(kind, m, p).wait_send()

        @pl.when(helps)
        def _():
            for m in range(chips):
                for p in range(2):
                    product_copy(2, m, p).wait_send()

        @pl.when(is_second)
        def _():
            for other in range(1, blocks):
                total_copy(other).wait_send()

    @pl.when(phase == 0)
    def _():
        @pl.when(t == 0)
        def _():
            for level in range(2):
                tbuf[level, 1] = jnp.zeros(tbuf.shape[2:], jnp.float32)
            fbuf[0] = jnp.zeros(fbuf.shape[1:], jnp.float32)
            for ref in (kept_row_high, kept_row_low, kept_col_high, kept_col_low):
                ref[1] = jnp.zeros(ref.shape[1:], jnp.bfloat16)

        def each_side(action):
            action(0)

            @pl.when(t > 0)
            def _():
                action(1)

        def kept_pass(level, side, k):
            relay_when_here(kept_peer.at[level, side], level, side, k)

        def kept_collect(level, side, k):
            opposite_arrived(kept_peer.at[level, side], level, side, k)
            arrived(kept_pair.at[level, side, k], precv.at[level, side, chips, k])
            lanes = lanes_of(k)
            for slot in range(chips):
                high, low = split_two(kept_peer[level, side, slot, k])
                to = slice(slot * LANES, (slot + 1) * LANES)
                kept_col_high[side, to, lanes] = high
                kept_col_low[side, to, lanes] = low
            for index, value in (
                (q, kept_own[level, side, k]), (1 - q, kept_pair[level, side, k])
            ):
                high, low = split_two(value)
                to = pl.ds(pl.multiple_of(index * LANES, LANES), LANES)
                kept_row_high[side, to, lanes] = high
                kept_row_low[side, to, lanes] = low

        def kept_products(lanes):
            value = None
            for side in range(2):
                term = dot_three(
                    kept_row_high[side, :, lanes], kept_row_low[side, :, lanes],
                    kept_col_high[side, :, lanes], kept_col_low[side, :, lanes],
                )
                value = term if value is None else value + term
            return value

        for level in range(2):
            def kept_step(k, carry):
                def take(side):
                    arrived(kept_own.at[level, side, k], orecv.at[level, side, k])
                    spread(
                        kept_own.at[level, side, k], kept_peer.at[level, side], level, side, k,
                        lambda copy: copy.start(),
                    )
                    kept_pair_copy(level, side, k).start()
                    kept_peer[level, side, y, k] = kept_own[level, side, k]

                each_side(take)

                @pl.when(k >= 1)
                def _():
                    each_side(lambda side: kept_pass(level, side, k - 1))

                @pl.when(k >= 2)
                def _():
                    each_side(lambda side: kept_collect(level, side, k - 2))

                return carry

            lax.fori_loop(0, count, kept_step, 0)
            each_side(lambda side: kept_collect(level, side, count - 2))
            partial_sum = kept_products(slice(0, early))
            if level == 0:
                kept_acc[...] = partial_sum
            else:
                kept_acc[...] = kept_acc[...] + partial_sum
            each_side(lambda side: kept_pass(level, side, count - 1))
            each_side(lambda side: kept_collect(level, side, count - 1))
            kept_acc[...] = kept_acc[...] + kept_products(slice(early, nodes))

        def swap_copy():
            return remote(swap_src, swap_dst, ssend, srecv, t, sibling)

        other_rows = pl.ds(pl.multiple_of((1 - q) * LANES, LANES), LANES)
        for m in range(chips):
            swap_src[m] = kept_acc[other_rows, m * LANES : (m + 1) * LANES]
        swap_copy().start()
        my_rows = pl.ds(pl.multiple_of(q * LANES, LANES), LANES)
        for m in range(chips):
            lanes = lanes_of(2 * m + q)
            factor_out[0, :, lanes] = (
                diag[0, :, lanes] - kept_acc[my_rows, m * LANES : (m + 1) * LANES]
            )

        for level in range(2):
            each_side(lambda side: arrived(tbuf.at[level, side], trecv.at[level, side]))
        arrow_out[0] = arrow[0] + (
            (tbuf[0, 0] + tbuf[0, 1]) + (tbuf[1, 0] + tbuf[1, 1])
        )
        arrived(swap_dst, srecv)
        for m in range(chips):
            lanes = lanes_of(2 * m + 1 - q)
            factor_out[0, :, lanes] = diag[0, :, lanes] - swap_dst[m]
        for k in range(count):
            lanes = slice(k * LANES, (k + 1) * LANES)
            arrived(fbuf.at[1, k], frecv.at[1, k])
            link_out[0, 1, :, lanes] = fbuf[1, k]

            @pl.when(t > 0)
            def _():
                arrived(fbuf.at[0, k], frecv.at[0, k])

            link_out[0, 0, :, lanes] = fbuf[0, k]

        swap_copy().wait_send()

        def kept_drain(k, carry):
            def wait_all(side):
                for level in range(2):
                    spread(
                        kept_own.at[level, side, k], kept_peer.at[level, side], level, side, k,
                        lambda copy: copy.wait_send(),
                    )
                    relay(
                        kept_peer.at[level, side], level, side, k,
                        lambda copy: copy.wait_send(),
                    )
                    kept_pair_copy(level, side, k).wait_send()

            each_side(wait_all)
            return carry

        lax.fori_loop(0, count, kept_drain, 0)

    @pl.when(odd == 0)
    def _():
        for k in range(count):
            coupling_copy(k).wait_send()

    total = tip[...]
    for index in range(blocks // 4):
        @pl.when(t != 4 * index + 2)
        def _():
            arrived(tipbuf.at[index], brecv.at[index])

        part = tipbuf[index]
        total = total + jnp.concatenate([part[:, :tip_rows], part[:, tip_rows:]], 0)
    tip_out[...] = total


def publish_kernel(*refs):
    half = (len(refs) - 2) // 3
    sources, targets, held = refs[:half], refs[half : 2 * half], refs[2 * half : 3 * half]
    reads, writes = refs[-2:]
    pieces = []
    for index, source in enumerate(sources):
        rows = source.shape[-2]
        leading = [(0,)] if len(source.shape) == 3 else [(0, 0), (0, 1)]
        for lead in leading if len(source.shape) > 2 else [()]:
            for first in range(0, rows, 64):
                pieces.append((index, lead + (pl.ds(first, 64),)))
    into = [
        pltpu.make_async_copy(sources[i].at[at], held[i].at[at], reads.at[n])
        for n, (i, at) in enumerate(pieces)
    ]
    out = [
        pltpu.make_async_copy(held[i].at[at], targets[i].at[at], writes.at[n])
        for n, (i, at) in enumerate(pieces)
    ]
    for copy in into:
        copy.start()
    for read, write in zip(into, out):
        read.wait()
        write.start()
    for copy in out:
        copy.wait()


def publish(results):
    return pl.pallas_call(
        publish_kernel,
        out_shape=tuple(jax.ShapeDtypeStruct(r.shape, r.dtype) for r in results),
        in_specs=[pl.BlockSpec(memory_space=pl.ANY)] * len(results),
        out_specs=(pl.BlockSpec(memory_space=pl.ANY),) * len(results),
        scratch_shapes=[pltpu.VMEM(r.shape, r.dtype) for r in results]
        + [pltpu.SemaphoreType.DMA((8,)), pltpu.SemaphoreType.DMA((8,))],
        name="publish",
    )(*results)


def body(diagonal, coupling, arrowhead, tip_matrix):
    cols = lax.axis_size("col")
    blocks = lax.axis_size("tm")
    chips = cols // 2
    nodes = diagonal.shape[2]
    tip_rows = tip_matrix.shape[0]
    total = nodes + 2 * LANES + tip_rows
    count = nodes // LANES
    half = chips * LANES
    f32, bf16, dma = jnp.float32, jnp.bfloat16, pltpu.SemaphoreType.DMA
    tile = (LANES, LANES)
    scratch = [
        pltpu.VMEM((count, total, LANES), f32),
        pltpu.VMEM((count, total, LANES), f32),
        pltpu.VMEM((count, nodes, LANES), f32),
        pltpu.VMEM((2, count) + tile, f32),
        pltpu.VMEM((2, count) + tile, f32),
        pltpu.VMEM((2, chips, count) + tile, f32),
        pltpu.VMEM((2, count, 2 * LANES, LANES), f32),
        pltpu.VMEM((count, 2 * LANES, LANES), f32),
        pltpu.VMEM((3, 2, chips) + tile, f32),
        pltpu.VMEM((2, 2 * LANES, half), f32),
        pltpu.VMEM((2, 2, chips, count) + tile, f32),
        pltpu.VMEM((2, 2, count) + tile, f32),
        pltpu.VMEM((2, 2, count) + tile, f32),
        pltpu.VMEM((2 * LANES, half), f32),
        pltpu.VMEM((chips,) + tile, f32),
        pltpu.VMEM((chips,) + tile, f32),
        pltpu.VMEM((cols, tip_rows, LANES), f32),
        pltpu.VMEM((2, 2, tip_rows, LANES), f32),
        pltpu.VMEM((2, tip_rows, LANES), f32),
        pltpu.VMEM((2, tip_rows // 2, LANES), f32),
        pltpu.VMEM((tip_rows // 2, LANES), f32),
        pltpu.VMEM((blocks // 4, tip_rows // 2, LANES), f32),
        pltpu.VMEM((LANES, 2 * LANES), f32),
        pltpu.VMEM((total, 3 * LANES), bf16),
        pltpu.VMEM((nodes, 3 * LANES), bf16),
        pltpu.VMEM((4 * LANES, nodes), bf16),
        pltpu.VMEM((4 * LANES, nodes), bf16),
        pltpu.VMEM((half, nodes), bf16),
        pltpu.VMEM((half, nodes), bf16),
        pltpu.VMEM((2, 2 * LANES, nodes), bf16),
        pltpu.VMEM((2, 2 * LANES, nodes), bf16),
        pltpu.VMEM((2, half, nodes), bf16),
        pltpu.VMEM((2, half, nodes), bf16),
        dma((11, count)),
        dma((cols, count)),
        dma((cols,)),
        dma((cols,)),
        dma((2, 2, 4, count)),
        dma((2, 2, chips + 1, count)),
        dma((2, 2, count)),
        dma((count,)),
        dma((2, count)),
        dma((3, 2, chips)),
        dma((2, count)),
        dma((2,)),
        dma((2, 2)),
        dma,
        dma((2,)),
        dma((blocks,)),
        dma((blocks // 4,)),
        dma,
        dma,
    ]

    def call(*refs):
        kernel(chips, tip_rows, blocks, *refs)

    arrow_t = jnp.swapaxes(arrowhead, 1, 2)
    results = pl.pallas_call(
        call,
        out_shape=(
            jax.ShapeDtypeStruct(diagonal.shape, f32),
            jax.ShapeDtypeStruct((1, 2) + diagonal.shape[1:], f32),
            jax.ShapeDtypeStruct(arrow_t.shape, f32),
            jax.ShapeDtypeStruct(tip_matrix.shape, f32),
        ),
        in_specs=[pl.BlockSpec(memory_space=pltpu.VMEM)] * 4,
        out_specs=(pl.BlockSpec(memory_space=pltpu.VMEM),) * 4,
        scratch_shapes=scratch,
        compiler_params=pltpu.CompilerParams(
            collective_id=0, has_side_effects=True, vmem_limit_bytes=60 * 1024 * 1024
        ),
        name="cyclic_reduction",
    )(diagonal, coupling, arrow_t, tip_matrix)
    factors, links, arrows, reduced = publish(results)
    return factors, links, jnp.swapaxes(arrows, 1, 2), reduced


def solution(mesh):
    in_specs = (P("tm", "col", None), P("tm", "col", None), P("tm", "col", None), P())
    out_specs = (P("tm", "col", None), P("tm", None, "col", None), P("tm", "col", None), P())
    return jax.shard_map(body, mesh=mesh, in_specs=in_specs, out_specs=out_specs, check_vma=False)
```
